32 devices in a mesh: wide: 8 (over z, y), narrow: 4 (over x, core).
Axes of the slice: x: 2, y: 2, z: 4, core: 2. Of those that a mesh axis runs over, the one named last changes fastest.
Arguments:
- hidden_in: bfloat16 [8192, 768], P('wide'), may hold values from -6 to 6
- lengths: int32 [256], P('wide'), may hold values from 0 to 1024, as said below
- positive: int32 [256], P('wide'), may hold values from 0 to 255, as said below
- norm1_gain: float32 [768], replicated, may hold values from 0.5 to 1.5
- w_query: bfloat16 [768, 768], P(None, 'narrow'), may hold values from -0.0546875 to 0.0546875
- w_key: bfloat16 [768, 768], P(None, 'narrow'), may hold values from -0.21875 to 0.21875
- w_value: bfloat16 [768, 768], P(None, 'narrow'), may hold values from -0.21875 to 0.21875
- rel_bias: float32 [32, 12], P(None, 'narrow'), may hold values from -4 to 4
- w_out: bfloat16 [768, 768], P('narrow'), may hold values from -0.75 to 0.75
- norm2_gain: float32 [768], replicated, may hold values from 0.5 to 1.5
- w_in: bfloat16 [768, 3072], P(None, 'narrow'), may hold values from -0.21875 to 0.21875
- w_ffout: bfloat16 [3072, 768], P('narrow'), may hold values from -0.109375 to 0.109375
- final_gain: float32 [768], replicated, may hold values from 0.5 to 1.5
- w_proj: bfloat16 [768, 768], replicated, may hold values from -0.21875 to 0.21875
- proj_bias: float32 [768], replicated, may hold values from -0.3 to 0.3
Outputs:
- hidden_out: float32 [8192, 768], P('wide')
- seq_loss: float32 [256], P('wide')
- grad_input: float32 [8192, 768], P('wide')
- grad_norm1: float32 [768], replicated
- grad_query: float32 [768, 768], P('wide', 'narrow')
- grad_key: float32 [768, 768], P('wide', 'narrow')
- grad_value: float32 [768, 768], P('wide', 'narrow')
- grad_rel_bias: float32 [32, 12], P(None, 'narrow')
- grad_out: float32 [768, 768], P('narrow', 'wide')
- grad_norm2: float32 [768], replicated
- grad_in: float32 [768, 3072], P('wide', 'narrow')
- grad_ffout: float32 [3072, 768], P('narrow', 'wide')
- grad_final: float32 [768], replicated
- grad_proj: float32 [768, 768], P('wide')
- grad_proj_bias: float32 [768], replicated
The draws below stay inside these ranges and needn't reach their ends.
Inputs may be any that keep to these rules, and one draw needn't show every extreme that they name: Each pack of 32 slots is either one document of 1024 tokens in its first slot with zero lengths after it, or 32 queries of 16 to 32 tokens; document packs are every eighth pack from an offset. `positive`: for a slot of nonzero length the index of another slot of nonzero length: a query's is a document, a document's a query. Slots of zero length hold the index of a query.
All inputs are finite; a program needn't handle non-finite values.
Results may differ from the reference program's by a relative error of at most 0.018.
Values may be sent and summed in bfloat16 or wider, within the bound.
No kernel may reach another device: no remote copies, remote signals or barrier semaphores. Data moves between devices by JAX's collectives and lax.ppermute only.
A program may use at most 128 MiB of HBM per device.

```python
import jax
import jax.numpy as jnp
from jax import lax

D = 768
HEADS = 12
HEAD = 64
FF = 3072
BUCKETS = 32
TOK_DEV = 1024
QLEN = 32
SEQ_DEV = 32
NSEQ = 256
TOKENS = 8192


def document_layout(key):
    pack_count = NSEQ // SEQ_DEV
    offset = jax.random.randint(jax.random.fold_in(key, 17), (), 0, 8)
    pack_index = jnp.arange(pack_count, dtype=jnp.int32)
    return (offset, pack_index % 8 == offset)


def draw_lengths(key, part):
    offset, doc_pack = document_layout(key)
    key = jax.random.fold_in(key, 3)
    pack_count = NSEQ // SEQ_DEV
    queries = jax.random.randint(key, (pack_count, SEQ_DEV), QLEN // 2, QLEN + 1)
    slot_index = jnp.arange(SEQ_DEV, dtype=jnp.int32)
    document = jnp.where(slot_index == 0, TOK_DEV, 0)
    lengths = jnp.where(doc_pack[:, None], document[None, :], queries)
    return lengths.reshape(NSEQ).astype(jnp.int32)


def draw_positive(key, part):
    offset, doc_pack = document_layout(key)
    key = jax.random.fold_in(key, 5)
    pack_count = NSEQ // SEQ_DEV
    first_key, second_key, third_key = jax.random.split(key, 3)
    sequence = jnp.arange(NSEQ, dtype=jnp.int32)
    own_pack = sequence // SEQ_DEV
    document = offset + 8 * jax.random.randint(first_key, (NSEQ,), 0, pack_count // 8)
    query_pack = (own_pack + jax.random.randint(second_key, (NSEQ,), 1, 8)) % pack_count
    query_slot = jax.random.randint(third_key, (NSEQ,), 0, SEQ_DEV)
    in_document = own_pack % 8 == offset
    target = jnp.where(in_document, query_pack * SEQ_DEV + query_slot, document * SEQ_DEV)
    return target.astype(jnp.int32)


def with_spikes(values, key, source, target, shards_of, factor):
    def block_of(dim):
        return (jnp.arange(values.shape[dim]) // (values.shape[dim] // shards_of)).reshape((-1,) + (1,) * (values.ndim - 1 - dim))

    one_side = jax.random.permutation(key, shards_of)[block_of(target)]
    second = (block_of(target) + shards_of // 2) % shards_of
    return jnp.where((block_of(source) == one_side) | (block_of(source) == second), factor * values, values)


def block_scale(stream_key, extent, cuts, smallest, largest):
    def one(dim, parts):
        draws = jax.random.uniform(jax.random.fold_in(jax.random.fold_in(stream_key, 6), dim), (parts,), jnp.float32, smallest / len(cuts), largest / len(cuts))
        return jnp.repeat(jnp.exp(draws), extent[dim] // parts).reshape((-1,) + (1,) * (len(extent) - dim - 1))

    level = one(*cuts[0])
    for cut in cuts[1:]:
        level = level * one(*cut)
    return level


def scatter_about(key, dims, scale, most, cuts=(), held_as=jnp.bfloat16):
    values = jax.random.normal(key, dims, jnp.float32) * scale
    if len(cuts) > 0:
        values = block_scale(key, dims, cuts, -0.22, 0.18) * values
    return jnp.clip(values, min=-most, max=most).astype(held_as)


def heavy_noise(stream_key, extent, width, bound, cuts, heavy, kind=jnp.bfloat16):
    values = width * jax.random.normal(stream_key, extent, jnp.float32)
    if cuts:
        values = values * block_scale(stream_key, extent, cuts, -0.22, 0.18)
    return jnp.clip(with_spikes(values, jax.random.fold_in(stream_key, 3), *heavy), -bound, bound).astype(kind)


def setup_inputs(seed: int = 0) -> dict:
    key_of = jax.random.split(jax.random.key(seed), 16)
    return {
        "hidden_in": heavy_noise(key_of[0], (TOKENS, D), 1.0, 6.0, ((0, 8),), (0, 1, 8, 2.0)),
        "lengths": draw_lengths(jax.random.fold_in(key_of[15], 71), 0),
        "positive": draw_positive(jax.random.fold_in(key_of[15], 71), 0),
        "norm1_gain": jnp.clip(1.0 + 0.1 * jax.random.normal(key_of[3], (D,), jnp.float32), 0.5, 1.5),
        "w_query": scatter_about(key_of[4], (D, HEADS * HEAD), (16 * D) ** -0.5, 0.0546875, ((1, 4),)),
        "w_key": scatter_about(key_of[5], (D, HEADS * HEAD), D ** -0.5, 0.21875, ((1, 4),)),
        "w_value": scatter_about(key_of[6], (D, HEADS * HEAD), D ** -0.5, 0.21875, ((1, 4),)),
        "rel_bias": scatter_about(key_of[7], (BUCKETS, HEADS), 1.0, 4.0, ((1, 4),), jnp.float32),
        "w_out": scatter_about(key_of[8], (HEADS * HEAD, D), HEAD ** -0.5, 0.75, ((0, 4),)),
        "norm2_gain": jnp.clip(1.0 + 0.1 * jax.random.normal(key_of[9], (D,), jnp.float32), 0.5, 1.5),
        "w_in": scatter_about(key_of[10], (D, FF), D ** -0.5, 0.21875, ((1, 4),)),
        "w_ffout": scatter_about(key_of[11], (FF, D), FF ** -0.5, 0.109375, ((0, 4),)),
        "final_gain": jnp.clip(1.0 + 0.1 * jax.random.normal(key_of[12], (D,), jnp.float32), 0.5, 1.5),
        "w_proj": scatter_about(key_of[13], (D, D), D ** -0.5, 0.21875),
        "proj_bias": scatter_about(key_of[14], (D,), 0.05, 0.3, (), jnp.float32),
    }


EPSILON = 1e-06
CONTRAST = 30.0
THRESHOLDS = (12, 16, 23, 32, 46, 64, 91)
HIGHEST = lax.Precision.HIGHEST

@jax.custom_vjp
def low(v):
    return lax.optimization_barrier(v.astype(jnp.bfloat16)).astype(jnp.float32)

@jax.custom_vjp
def low_back(v):
    return v

def low_keep(v):
    return (low(v), None)

def low_pass(kept, grad):
    return (grad,)

def back_keep(v):
    return (v, None)

def back_low(kept, grad):
    return (low(grad),)
low.defvjp(low_keep, low_pass)
low_back.defvjp(back_keep, back_low)

def rms_norm(values, gain):
    return values * lax.rsqrt(lax.optimization_barrier(jnp.mean(values * values, axis=-1, keepdims=True)) + EPSILON) * gain

def bucket_ids(row_index, col_index):
    offset = col_index[None, :] - row_index[:, None]
    distance = jnp.abs(offset)
    far_bucket = 8 + sum(((distance >= limit).astype(jnp.int32) for limit in THRESHOLDS))
    return jnp.where(distance < 8, distance, far_bucket) + 16 * (offset > 0).astype(jnp.int32)

def segment_ids(lengths, token_count):
    ends = jnp.cumsum(lengths, dtype=jnp.int32)
    position = jnp.arange(token_count, dtype=jnp.int32)
    passed = lax.optimization_barrier(jnp.sum((position[:, None] >= ends[None, :]).astype(jnp.int32), axis=1)).astype(jnp.int32)
    return jnp.where(passed >= lengths.shape[0], lengths.shape[0] + position, passed).astype(jnp.int32)

def pack_layer(inputs, lengths, gain_one, query_w, key_w, value_w, table, out_w, gain_two, in_w, ffout_w, gain_final):
    token_count = inputs.shape[0]
    head_count = table.shape[1]
    head_width = query_w.shape[1] // head_count
    segment = segment_ids(lengths, token_count)
    position = jnp.arange(token_count, dtype=jnp.int32)
    allowed = segment[:, None] == segment[None, :]
    bias_full = jnp.transpose(table[bucket_ids(position, position)], (2, 0, 1))
    norm_one = low(rms_norm(inputs, gain_one))

    def project(weight_w):
        result = low(low_back(jnp.dot(norm_one, weight_w, precision=HIGHEST)))
        return jnp.transpose(result.reshape(token_count, head_count, head_width), (1, 0, 2))
    query_h, key_h, value_h = (project(query_w), project(key_w), project(value_w))
    scores = low_back(jnp.einsum('hqe,hke->hqk', query_h, key_h, precision=HIGHEST) + bias_full)
    probs = jax.nn.softmax(jnp.where(allowed[None], scores, -1e+30), axis=-1)
    mixed = jnp.einsum('hqk,hke->hqe', low(probs), value_h, precision=HIGHEST)
    mixed = low(low_back(jnp.transpose(mixed, (1, 0, 2)).reshape(token_count, head_count * head_width)))
    after_attn = inputs + low_back(jnp.dot(mixed, out_w, precision=HIGHEST))
    norm_two = low(rms_norm(after_attn, gain_two))
    pre_act = low_back(jnp.dot(norm_two, in_w, precision=HIGHEST))
    act_low = low(jax.nn.gelu(pre_act))
    layer_out = after_attn + low_back(jnp.dot(act_low, ffout_w, precision=HIGHEST))
    final = rms_norm(layer_out, gain_final)
    member = (segment[None, :] == jnp.arange(lengths.shape[0], dtype=jnp.int32)[:, None]).astype(jnp.float32)
    pooled = jnp.dot(member, final, precision=HIGHEST) / jnp.maximum(lengths, 1).astype(jnp.float32)[:, None]
    return (layer_out, pooled)

def reference(hidden_in, lengths, positive, norm1_gain, w_query, w_key, w_value, rel_bias, w_out, norm2_gain, w_in, w_ffout, final_gain, w_proj, proj_bias):
    pack_count = lengths.shape[0] // SEQ_DEV
    is_valid = lengths > 0
    seq_index = jnp.arange(NSEQ, dtype=jnp.int32)

    def forward(inputs, gain_one, query_w, key_w, value_w, table, out_w, gain_two, in_w, ffout_w, gain_final, proj_w, bias_p):

        def one_pack(pieces):
            return pack_layer(pieces[0], pieces[1], gain_one, query_w, key_w, value_w, table, out_w, gain_two, in_w, ffout_w, gain_final)
        layer_out, pooled = lax.map(jax.checkpoint(one_pack), (inputs.reshape(pack_count, TOK_DEV, D), lengths.reshape(pack_count, SEQ_DEV)))
        pooled = pooled.reshape(NSEQ, D)
        embed = low_back(jnp.dot(low(pooled), proj_w, precision=HIGHEST) + bias_p)
        unit = low(embed * lax.rsqrt(lax.optimization_barrier(jnp.sum(embed * embed, axis=-1, keepdims=True)) + EPSILON))
        sims = CONTRAST * jnp.dot(unit, unit.T, precision=HIGHEST)
        usable = is_valid[None, :] & (seq_index[None, :] != seq_index[:, None])
        spread = jax.nn.logsumexp(jnp.where(usable, sims, -1e+30), axis=1)
        pos_score = lax.optimization_barrier(jnp.sum(jnp.where(seq_index[None, :] == positive[:, None], sims, 0.0), axis=1))
        seq_loss = jnp.where(is_valid, spread - pos_score, 0.0)
        return (jnp.sum(seq_loss), (layer_out.reshape(TOKENS, D), seq_loss))
    floats = tuple((item.astype(jnp.float32) for item in (hidden_in, norm1_gain, w_query, w_key, w_value, rel_bias, w_out, norm2_gain, w_in, w_ffout, final_gain, w_proj, proj_bias)))
    total_loss, pull_back, extras = jax.vjp(forward, *floats, has_aux=True)
    grads = pull_back(jnp.ones((), jnp.float32))
    return (extras[0], extras[1], grads[0], grads[1], grads[2], grads[3], grads[4], grads[5], grads[6], grads[7], grads[8], grads[9], grads[10], grads[11], grads[12])
```

```python
import functools

import jax
import jax.numpy as jnp
from jax import lax
from jax.experimental import pallas as pl
from jax.experimental.pallas import tpu as pltpu
from jax.sharding import PartitionSpec as P

EPSILON = 1e-06
CONTRAST = 30.0
THRESHOLDS = (12, 16, 23, 32, 46, 64, 91)
GELU = 0.7978845608028654
CUBE = 0.044715
BLOCK = 128
MIB = 1024 * 1024
QUICK = pl.CostEstimate(flops=2**20, bytes_accessed=2**16, transcendentals=0)
SCALARS = pl.BlockSpec(memory_space=pltpu.SMEM)
VECTORS = pl.BlockSpec(memory_space=pltpu.VMEM)
ANYWHERE = pl.BlockSpec(memory_space=pl.ANY)


def in_main(value):
    return pltpu.with_memory_space_constraint(value, pltpu.HBM)


def exchange(value, axis, step):
    count = lax.axis_size(axis)
    return lax.ppermute(value, axis, [(k, k ^ step) for k in range(count)])


def add_low(left, right):
    return (left.astype(jnp.float32) + right.astype(jnp.float32)).astype(jnp.bfloat16)


def summed_over_narrow(keep, send):
    part = add_low(keep, exchange(send, "narrow", 1))
    own = add_low(part, exchange(part, "narrow", 2))
    return own, exchange(own, "narrow", 1)


def over_parity(blocks):
    count = lax.axis_size("wide")
    return (blocks[0], *(exchange(blocks[k], "wide", 2 * k) for k in range(1, count // 2)))


def two_terms(value):
    high = value.astype(jnp.bfloat16)
    return high, (value - high.astype(jnp.float32)).astype(jnp.bfloat16)


def offset_buckets(offset):
    distance = jnp.abs(offset)
    far_bucket = 8 + sum(((distance >= limit).astype(jnp.int32) for limit in THRESHOLDS))
    return jnp.where(distance < 8, distance, far_bucket) + 16 * (offset > 0).astype(jnp.int32)


def dot_over(left, right, left_dim, right_dim):
    return lax.dot_general(
        left, right, (((left_dim,), (right_dim,)), ((), ())), preferred_element_type=jnp.float32
    )


def row_dot(left, right):
    return lax.dot_general(
        left, right, (((1,), (1,)), ((), ())), preferred_element_type=jnp.float32
    )


def plain_dot(left, right):
    return lax.dot_general(
        left, right, (((1,), (0,)), ((), ())), preferred_element_type=jnp.float32
    )


def col_dot(left, right):
    return lax.dot_general(
        left, right, (((0,), (0,)), ((), ())), preferred_element_type=jnp.float32
    )


def slot_edges(lengths_ref, position):
    low = jnp.zeros_like(position)
    high = jnp.zeros_like(position)
    start = jnp.int32(0)
    for slot in range(lengths_ref.shape[0]):
        reached = position >= start
        low = jnp.where(reached, start, low)
        start_next = start + lengths_ref[slot]
        high = jnp.where(reached, start_next, high)
        start = start_next
    padded = position >= start
    return jnp.where(padded, position, low), jnp.where(padded, position + 1, high)


def bias_tiles(table_ref, tiles, turned):
    head_count, bucket_count = table_ref.shape
    lane = lax.broadcasted_iota(jnp.int32, (8, 4 * BLOCK), 1)
    offset = 2 * BLOCK - lane if turned else lane - 2 * BLOCK
    bucket = offset_buckets(offset)
    for head in range(head_count):
        line = jnp.zeros((8, 4 * BLOCK), jnp.float32)
        for index in range(bucket_count):
            line = jnp.where(bucket == index, table_ref[head, index], line)
        spread = jnp.broadcast_to(line[:1], (BLOCK, 4 * BLOCK))
        tiles[head] = pltpu.roll(spread, 0, 1, stride=1, stride_axis=0)


def unrolled_sum(tile):
    width = tile.shape[1]
    group = tile[:8]
    for first in range(8, tile.shape[0], 8):
        group = group + pltpu.roll(tile[first : first + 8], width - first, 1)
    line = group[:1]
    for row in range(1, 8):
        line = line + pltpu.roll(group, width - row, 1)[row : row + 1]
    return line


def attend_kernel(
    lengths_ref,
    table_ref,
    hidden_hbm,
    gain_ref,
    wq_hbm,
    wk_hbm,
    wv_hbm,
    norm_hbm,
    q_hbm,
    k_hbm,
    v_hbm,
    mixed_hbm,
    packed_hbm,
    spread_hbm,
    tiles,
    heads_q,
    heads_k,
    heads_v,
    heads_o,
    edges,
    spreads,
    hidden_ref,
    wq_ref,
    wk_ref,
    wv_ref,
    norm_ref,
    q_ref,
    k_ref,
    v_ref,
    mixed_ref,
    packed_ref,
    spread_ref,
    came,
    left,
):
    token_count = hidden_ref.shape[0]
    head_count, bucket_count = table_ref.shape
    width = q_ref.shape[1] // head_count
    chunk = 2 * BLOCK
    blocks = token_count // BLOCK
    starts = range(0, token_count, chunk)
    loads = []
    for index, (source, target) in enumerate(
        ((wq_hbm, wq_ref), (wk_hbm, wk_ref), (wv_hbm, wv_ref))
    ):
        loads.append(pltpu.make_async_copy(source, target, came.at[index]))
    for index, start in enumerate(starts):
        rows = pl.ds(start, chunk)
        loads.append(
            pltpu.make_async_copy(
                hidden_hbm.at[rows, :], hidden_ref.at[rows, :], came.at[3 + index]
            )
        )
    for load in (loads[3], *loads[:3], *loads[4:]):
        load.start()
    bias_tiles(table_ref, tiles, False)
    stores = []

    def store(source, target):
        copy = pltpu.make_async_copy(source, target, left.at[len(stores)])
        copy.start()
        stores.append(copy)

    for index, start in enumerate(starts):
        rows = pl.ds(start, chunk)
        loads[3 + index].wait()
        values = hidden_ref[rows, :].astype(jnp.float32)
        norm = (values * norm_scale(values) * gain_ref[...].reshape(1, -1)).astype(jnp.bfloat16)
        norm_ref[rows, :] = norm
        if index == 0:
            for load in loads[:3]:
                load.wait()
        for weight, out, parts in (
            (wq_ref, q_ref, heads_q),
            (wk_ref, k_ref, heads_k),
            (wv_ref, v_ref, heads_v),
        ):
            value = row_dot(norm, weight[...]).astype(jnp.bfloat16)
            out[rows, :] = value
            for head in range(head_count):
                parts[head, rows, :] = value[:, head * width : (head + 1) * width]
    for source, target in (
        (norm_ref, norm_hbm),
        (q_ref, q_hbm),
        (k_ref, k_hbm),
        (v_ref, v_hbm),
    ):
        store(source, target)
    lane = lax.broadcasted_iota(jnp.int32, (1, BLOCK), 1)

    def finish(head, rows, scores):
        top = jnp.max(scores, axis=1, keepdims=True)
        weights = jnp.exp(scores - top)
        total = jnp.sum(weights, axis=1, keepdims=True)
        keep = jnp.where(lane == head, top + jnp.log(total), spreads[rows, :])
        spreads[rows, :] = keep
        return weights.astype(jnp.bfloat16), 1.0 / total

    @pl.when(lengths_ref[0] > lengths_ref.shape[0])
    def document():
        def one_head(head, carry):
            keys, values = heads_k[head], heads_v[head]
            past = table_ref[head, bucket_count // 2 - 1]
            future = table_ref[head, bucket_count - 1]
            for start in range(0, token_count, chunk):
                rows = pl.ds(start, chunk)
                raw = row_dot(heads_q[head, rows, :], keys)
                lines = []
                for part in range(chunk // BLOCK):
                    line = []
                    for block in range(blocks):
                        away = block - start // BLOCK - part
                        piece = raw[
                            part * BLOCK : (part + 1) * BLOCK, block * BLOCK : (block + 1) * BLOCK
                        ]
                        if abs(away) <= 1:
                            first = (2 + away) * BLOCK
                            piece = piece + tiles[head, :, first : first + BLOCK]
                        else:
                            piece = piece + (past if away < 0 else future)
                        line.append(piece)
                    lines.append(jnp.concatenate(line, axis=1))
                weights, scale = finish(head, rows, jnp.concatenate(lines, axis=0))
                heads_o[head, rows, :] = (plain_dot(weights, values) * scale).astype(jnp.bfloat16)
            return carry

        lax.fori_loop(0, head_count, one_head, 0)

    @pl.when(lengths_ref[0] <= lengths_ref.shape[0])
    def queries():
        position = lax.broadcasted_iota(jnp.int32, (8, token_count), 1)
        low, high = slot_edges(lengths_ref, position)
        edges[0] = low
        edges[1] = high

        def one_head(head, carry):
            for block in range(blocks):
                first = max(block - 1, 0)
                last = min(block + 1, blocks - 1) + 1
                rows = pl.ds(block * BLOCK, BLOCK)
                window = pl.ds(first * BLOCK, (last - first) * BLOCK)
                scores = row_dot(heads_q[head, rows, :], heads_k[head, window, :])
                shift = (2 + first - block) * BLOCK
                scores = scores + tiles[head, :, shift : shift + (last - first) * BLOCK]
                token = block * BLOCK + lax.broadcasted_iota(jnp.int32, scores.shape, 0)
                inside = (token >= edges[0, :1, window]) & (token < edges[1, :1, window])
                weights, scale = finish(head, rows, jnp.where(inside, scores, -1e30))
                heads_o[head, rows, :] = (
                    plain_dot(weights, heads_v[head, window, :]) * scale
                ).astype(jnp.bfloat16)
            return carry

        lax.fori_loop(0, head_count, one_head, 0)

    half = token_count // 2
    pair = jnp.concatenate([heads_o[0], heads_o[1]], axis=1)
    mixed_ref[:, : 2 * width] = pair
    mixed_ref[:, 2 * width :] = heads_o[2]
    packed_ref[:token_count, :] = pair
    packed_ref[token_count:, :] = jnp.concatenate([heads_o[2, :half], heads_o[2, half:]], axis=1)
    store(packed_ref, packed_hbm)
    store(mixed_ref, mixed_hbm)
    for start in range(0, token_count, BLOCK):
        turned = jnp.transpose(spreads[pl.ds(start, BLOCK), :])
        spread_ref[:, start : start + BLOCK] = turned[:8]
    store(spread_ref, spread_hbm)
    for copy in stores:
        copy.wait()


def attend(lengths, table, hidden_in, gain, w_query, w_key, w_value):
    token_count, model = hidden_in.shape
    head_count = table.shape[0]
    inner = w_query.shape[0]
    width = inner // head_count
    low = jnp.bfloat16
    heads = pltpu.VMEM((head_count, token_count, width), low)
    weight = pltpu.VMEM((inner, model), low)
    results = (
        ((token_count, model), low),
        ((token_count, inner), low),
        ((token_count, inner), low),
        ((token_count, inner), low),
        ((token_count, inner), low),
        ((token_count * 3 // 2, 2 * width), low),
        ((8, token_count), jnp.float32),
    )
    return pl.pallas_call(
        attend_kernel,
        out_shape=tuple(
            (jax.ShapeDtypeStruct if index == 5 else pltpu.HBM)(*result)
            for index, result in enumerate(results)
        ),
        in_specs=[SCALARS, SCALARS, ANYWHERE, VECTORS] + [ANYWHERE] * 3,
        out_specs=(ANYWHERE,) * 7,
        scratch_shapes=[
            pltpu.VMEM((head_count, BLOCK, 4 * BLOCK), jnp.float32),
            heads,
            heads,
            heads,
            heads,
            pltpu.VMEM((2, 8, token_count), jnp.int32),
            pltpu.VMEM((token_count, BLOCK), jnp.float32),
            pltpu.VMEM((token_count, model), low),
            weight,
            weight,
            weight,
            *(pltpu.VMEM(*result) for result in results),
            pltpu.SemaphoreType.DMA((3 + token_count // (2 * BLOCK),)),
            pltpu.SemaphoreType.DMA((7,)),
        ],
        compiler_params=pltpu.CompilerParams(vmem_limit_bytes=28 * MIB),
        cost_estimate=QUICK,
        name="attend",
    )(
        *(in_main(value) for value in (lengths, table, hidden_in, gain)),
        *(in_main(value) for value in (w_query, w_key, w_value)),
    )


def attend_back_kernel(
    later_count,
    place_ref,
    lengths_ref,
    table_ref,
    q_hbm,
    k_hbm,
    v_hbm,
    grad_own_hbm,
    grad_far_hbm,
    spread_hbm,
    hidden_hbm,
    wq_hbm,
    wk_hbm,
    wv_hbm,
    norm_hbm,
    mixed_hbm,
    *refs,
):
    refs = refs[later_count:]
    dq_hbm, dk_hbm, dv_hbm, table_grad_hbm, hidden_near, weights_near = refs[:6]
    norm_near, mixed_near = refs[6:8]
    refs = refs[8:]
    tiles, heads_q, heads_k, heads_v, heads_g, probs, grads, sums_q, sums_k, sums_v = refs[:10]
    near, far, edges, lines_s, q_ref, k_ref, v_ref, grad_own_ref, grad_far_ref = refs[10:19]
    spread_ref, dq_ref, dk_ref, dv_ref, table_grad_ref, came, left = refs[19:]
    token_count = q_ref.shape[0]
    head_count, bucket_count = table_ref.shape
    width = q_ref.shape[1] // head_count
    chunk = 2 * BLOCK
    blocks = token_count // BLOCK
    loads = [
        pltpu.make_async_copy(source, target, came.at[index])
        for index, (source, target) in enumerate(
            (
                (q_hbm, q_ref),
                (k_hbm, k_ref),
                (v_hbm, v_ref),
                (grad_own_hbm, grad_own_ref),
                (grad_far_hbm, grad_far_ref),
                (spread_hbm, spread_ref),
                (hidden_hbm, hidden_near),
                (wq_hbm, weights_near.at[0]),
                (wk_hbm, weights_near.at[1]),
                (wv_hbm, weights_near.at[2]),
                (norm_hbm, norm_near),
                (mixed_hbm, mixed_near),
            )
        )
    ]
    for load in loads:
        load.start()
    stores = []

    def store(source, target):
        copy = pltpu.make_async_copy(source, target, left.at[len(stores)])
        copy.start()
        stores.append(copy)

    half = token_count // 2
    side = place_ref[0] % 2
    own_rows = pl.ds(pl.multiple_of(side * half, half), half)
    far_rows = pl.ds(pl.multiple_of((1 - side) * half, half), half)
    bias_tiles(table_ref, tiles, True)
    token = lax.broadcasted_iota(jnp.int32, (token_count, BLOCK - width), 0)
    lane = lax.broadcasted_iota(jnp.int32, (token_count, BLOCK - width), 1)
    marks = (token // BLOCK == lane).astype(jnp.float32).astype(jnp.bfloat16)
    for load in loads[:6]:
        load.wait()
    for head in range(head_count):
        cut = slice(head * width, (head + 1) * width)
        heads_q[head] = jnp.concatenate([q_ref[:, cut], marks], axis=1)
        heads_k[head] = k_ref[:, cut]
        heads_v[head] = v_ref[:, cut]
        heads_g[head, own_rows, :] = grad_own_ref[:, cut]
        heads_g[head, far_rows, :] = grad_far_ref[:, cut]
        lines_s[head] = jnp.broadcast_to(spread_ref[head : head + 1, :], (8, token_count))
    near[...] = jnp.zeros_like(near)
    far[...] = jnp.zeros_like(far)

    def score_back(scores, spread, grad_probs):
        weights = jnp.exp(scores - spread)
        delta = jnp.sum(weights * grad_probs, axis=0, keepdims=True)
        return weights, weights * (grad_probs - delta)

    @pl.when(lengths_ref[0] > lengths_ref.shape[0])
    def document():
        def one_head(head, carry):
            keys, values = heads_k[head], heads_v[head]
            past = table_ref[head, bucket_count // 2 - 1]
            future = table_ref[head, bucket_count - 1]
            for start in range(0, token_count, chunk):
                rows = pl.ds(start, chunk)
                raw = row_dot(keys, heads_q[head, rows, :width])
                lines = []
                for block in range(blocks):
                    line = []
                    for part in range(chunk // BLOCK):
                        away = block - start // BLOCK - part
                        piece = raw[
                            block * BLOCK : (block + 1) * BLOCK, part * BLOCK : (part + 1) * BLOCK
                        ]
                        if abs(away) <= 1:
                            first = (2 - away) * BLOCK
                            piece = piece + tiles[head, :, first : first + BLOCK]
                        else:
                            piece = piece + (past if away < 0 else future)
                        line.append(piece)
                    lines.append(jnp.concatenate(line, axis=1))
                scores = jnp.concatenate(lines, axis=0)
                grad_probs = row_dot(values, heads_g[head, rows, :])
                weights, score_grad = score_back(
                    scores, lines_s[head, :1, rows], grad_probs
                )
                probs[:, rows] = weights.astype(jnp.bfloat16)
                grads[:, rows] = score_grad.astype(jnp.bfloat16)
                for block in range(blocks):
                    for part in range(chunk // BLOCK):
                        away = block - start // BLOCK - part
                        if abs(away) <= 1:
                            first = (2 - away) * BLOCK
                            near[head, :, first : first + BLOCK] += score_grad[
                                block * BLOCK : (block + 1) * BLOCK,
                                part * BLOCK : (part + 1) * BLOCK,
                            ]
            sums_v[head] = plain_dot(probs[...], heads_g[head])
            key_sums = plain_dot(grads[...], heads_q[head])
            sums_k[head] = key_sums[:, :width]
            sums_q[head] = col_dot(grads[...], keys)
            for block in range(blocks):
                line = jnp.sum(key_sums[block * BLOCK : (block + 1) * BLOCK], axis=0, keepdims=True)
                far[head, block : block + 1, :] = line
            return carry

        lax.fori_loop(0, head_count, one_head, 0)

    @pl.when(lengths_ref[0] <= lengths_ref.shape[0])
    def queries():
        position = lax.broadcasted_iota(jnp.int32, (8, token_count), 1)
        low, high = slot_edges(lengths_ref, position)
        edges[0] = low
        edges[1] = high
        sums_k[...] = jnp.zeros_like(sums_k)
        sums_v[...] = jnp.zeros_like(sums_v)

        def one_head(head, carry):
            for block in range(blocks):
                first = max(block - 1, 0)
                last = min(block + 1, blocks - 1) + 1
                rows = pl.ds(block * BLOCK, BLOCK)
                window = pl.ds(first * BLOCK, (last - first) * BLOCK)
                scores = row_dot(heads_k[head, window, :], heads_q[head, rows, :width])
                lines = []
                for other in range(first, last):
                    begin = (2 - (other - block)) * BLOCK
                    lines.append(tiles[head, :, begin : begin + BLOCK])
                scores = scores + jnp.concatenate(lines, axis=0)
                token = first * BLOCK + lax.broadcasted_iota(jnp.int32, scores.shape, 0)
                inside = (token >= edges[0, :1, rows]) & (token < edges[1, :1, rows])
                grad_probs = row_dot(heads_v[head, window, :], heads_g[head, rows, :])
                weights, score_grad = score_back(
                    jnp.where(inside, scores, -1e30), lines_s[head, :1, rows], grad_probs
                )
                for other in range(first, last):
                    begin = (2 - (other - block)) * BLOCK
                    near[head, :, begin : begin + BLOCK] += score_grad[
                        (other - first) * BLOCK : (other - first + 1) * BLOCK
                    ]
                grad_low = score_grad.astype(jnp.bfloat16)
                sums_v[head, window, :] += plain_dot(
                    weights.astype(jnp.bfloat16), heads_g[head, rows, :]
                )
                sums_k[head, window, :] += plain_dot(grad_low, heads_q[head, rows, :width])
                sums_q[head, rows, :] = col_dot(grad_low, heads_k[head, window, :])
            return carry

        lax.fori_loop(0, head_count, one_head, 0)

    for sums, out in ((sums_q, dq_ref), (sums_k, dk_ref), (sums_v, dv_ref)):
        out[...] = jnp.concatenate(
            [sums[head].astype(jnp.bfloat16) for head in range(head_count)], axis=1
        )
    for source, target in ((dq_ref, dq_hbm), (dk_ref, dk_hbm), (dv_ref, dv_hbm)):
        store(source, target)
    lines = []
    for head in range(head_count):
        lines.append(unrolled_sum(near[head]))
    lines.append(jnp.zeros((8 - head_count, 4 * BLOCK), jnp.float32))
    by_offset = jnp.concatenate(lines, axis=0)
    offset = 2 * BLOCK - lax.broadcasted_iota(jnp.int32, (4 * BLOCK, BLOCK), 0)
    place = lax.broadcasted_iota(jnp.int32, (4 * BLOCK, BLOCK), 1)
    onehot = (offset_buckets(offset) == place).astype(jnp.float32).astype(jnp.bfloat16)
    high, rest = two_terms(by_offset)
    table_grad = plain_dot(high, onehot) + plain_dot(rest, onehot)
    row = lax.broadcasted_iota(jnp.int32, (blocks, BLOCK), 0)
    column = lax.broadcasted_iota(jnp.int32, (blocks, BLOCK), 1) - width
    real = (column >= 0) & (column < blocks)
    is_past = real & (row - column <= -2)
    is_future = real & (row - column >= 2)
    lane = lax.broadcasted_iota(jnp.int32, (1, BLOCK), 1)
    lines = []
    for head in range(head_count):
        past = jnp.sum(jnp.where(is_past, far[head], 0.0), keepdims=True)
        future = jnp.sum(jnp.where(is_future, far[head], 0.0), keepdims=True)
        lines.append(
            table_grad[head : head + 1]
            + jnp.where(lane == bucket_count // 2 - 1, past, 0.0)
            + jnp.where(lane == bucket_count - 1, future, 0.0)
        )
    lines.append(jnp.zeros((8 - head_count, BLOCK), jnp.float32))
    table_grad_ref[...] = jnp.concatenate(lines, axis=0)
    store(table_grad_ref, table_grad_hbm)
    for copy in (*stores, *loads[6:]):
        copy.wait()


def attend_back(
    place, lengths, table, query, key, value, grads, spread, hidden_in, weights, norm, mixed, later
):
    token_count, inner = query.shape
    model = hidden_in.shape[1]
    head_count = table.shape[0]
    width = inner // head_count
    low, full = jnp.bfloat16, jnp.float32
    heads = pltpu.VMEM((head_count, token_count, width), low)
    sums = pltpu.VMEM((head_count, token_count, width), full)
    square = pltpu.VMEM((token_count, token_count), low)
    tile = pltpu.VMEM((head_count, BLOCK, 4 * BLOCK), full)
    flat = pltpu.VMEM((token_count, inner), low)
    half = pltpu.VMEM((token_count // 2, inner), low)
    return pl.pallas_call(
        functools.partial(attend_back_kernel, len(later)),
        out_shape=(
            shape_of(token_count, inner, low),
            shape_of(token_count, inner, low),
            shape_of(token_count, inner, low),
            shape_of(8, BLOCK, full),
            near_shape(token_count, model, low),
            pltpu.VMEM((3, inner, model), low),
            near_shape(token_count, model, low),
            near_shape(token_count, inner, low),
        ),
        in_specs=[SCALARS] * 3 + [ANYWHERE] * (12 + len(later)),
        out_specs=(ANYWHERE,) * 8,
        scratch_shapes=[
            tile,
            pltpu.VMEM((head_count, token_count, BLOCK), low),
            heads,
            heads,
            heads,
            square,
            square,
            sums,
            sums,
            sums,
            tile,
            pltpu.VMEM((head_count, token_count // BLOCK, BLOCK), full),
            pltpu.VMEM((2, 8, token_count), jnp.int32),
            pltpu.VMEM((head_count, 8, token_count), full),
            flat,
            flat,
            flat,
            half,
            half,
            pltpu.VMEM((8, token_count), full),
            flat,
            flat,
            flat,
            pltpu.VMEM((8, BLOCK), full),
            pltpu.SemaphoreType.DMA((12,)),
            pltpu.SemaphoreType.DMA((4,)),
        ],
        compiler_params=pltpu.CompilerParams(vmem_limit_bytes=34 * MIB),
        cost_estimate=pl.CostEstimate(
            flops=12 * 2**30, bytes_accessed=2**16, transcendentals=0
        ),
        name="attend_back",
    )(
        *(in_main(value) for value in (place, lengths, table, query, key, value)),
        *grads,
        *(in_main(value) for value in (spread, hidden_in, *weights, norm, mixed)),
        *later,
    )


def parts_kernel(flip, later_count, place_ref, dq_ref, dk_ref, dv_ref, hidden_ref, w_ref, *refs):
    part_ref, one_ref = refs[later_count:]
    half = (place_ref[0] % 2) ^ flip
    one = jnp.zeros(one_ref.shape, jnp.float32)
    for _, own, whole in chunk_rows(part_ref.shape[0], half):
        part = plain_dot(dq_ref[whole, :], w_ref[0])
        part = part + plain_dot(dk_ref[whole, :], w_ref[1])
        part = part + plain_dot(dv_ref[whole, :], w_ref[2])
        part_ref[own, :] = part.astype(jnp.bfloat16)
        values = hidden_ref[whole, :].astype(jnp.float32)
        one = one + jnp.sum(part * values * norm_scale(values), axis=0, keepdims=True)
    one_ref[...] = one


def norm1_parts(flip, place, grads, hidden, weights, later):
    token_count, model = hidden.shape
    return pl.pallas_call(
        functools.partial(parts_kernel, flip, len(later)),
        out_shape=(
            shape_of(token_count // 2, model, jnp.bfloat16),
            shape_of(1, model, jnp.float32),
        ),
        in_specs=[SCALARS] + [VECTORS] * 5 + [ANYWHERE] * len(later),
        out_specs=(VECTORS, VECTORS),
        compiler_params=pltpu.CompilerParams(vmem_limit_bytes=20 * MIB),
        cost_estimate=pl.CostEstimate(
            flops=3 * weights.size * token_count // 3,
            bytes_accessed=4 * hidden.size,
            transcendentals=0,
        ),
        name="norm1_parts",
    )(in_main(place), *grads, hidden, weights, *later)


def split_gelu(value):
    square = value * value
    inner = GELU * value * (1.0 + CUBE * square)
    turn = jnp.tanh(inner)
    half = 0.5 * (1.0 + turn)
    slope = half + 0.5 * value * (1.0 - turn * turn) * GELU * (1.0 + 3.0 * CUBE * square)
    return half * value, slope


def norm_scale(values):
    return lax.rsqrt(jnp.mean(values * values, axis=1, keepdims=True) + EPSILON)


def norm_back(values, gain, grad):
    scale = norm_scale(values)
    scaled = grad * gain
    share = jnp.mean(scaled * values, axis=1, keepdims=True)
    back = scale * scaled - (scale * scale * scale) * values * share
    return back, jnp.sum(grad * values * scale, axis=0, keepdims=True)


def slot_lines(lengths_ref, shape, axis):
    slot = lax.broadcasted_iota(jnp.int32, shape, axis)
    starts = jnp.zeros(shape, jnp.int32)
    ends = jnp.zeros(shape, jnp.int32)
    start = jnp.int32(0)
    for index in range(lengths_ref.shape[0]):
        end = start + lengths_ref[index]
        starts = jnp.where(slot == index, start, starts)
        ends = jnp.where(slot == index, end, ends)
        start = end
    return starts, ends


def as_low(mask):
    return mask.astype(jnp.float32).astype(jnp.bfloat16)


def row_call(kernel, flip, inputs, outputs, scratch, place, aliases, flops):
    specs = {"scalar": SCALARS, "line": VECTORS, "near": VECTORS, "any": ANYWHERE}
    return pl.pallas_call(
        functools.partial(kernel, flip),
        out_shape=tuple(shape for _, shape in outputs),
        in_specs=[SCALARS] + [specs[kind] for kind, _ in inputs],
        out_specs=tuple(specs[kind] for kind, _ in outputs),
        scratch_shapes=scratch,
        input_output_aliases=aliases,
        compiler_params=pltpu.CompilerParams(vmem_limit_bytes=24 * MIB),
        cost_estimate=pl.CostEstimate(flops=flops, bytes_accessed=6 * 2**20, transcendentals=0),
        name=kernel.__name__,
    )(
        in_main(place),
        *(in_main(value) if kind in ("line", "scalar") else value for kind, value in inputs),
    )


def near_shape(rows, columns, kind):
    return pltpu.VMEM((rows, columns), kind)


def main_shape(rows, columns, kind):
    return pltpu.HBM((rows, columns), kind)


def shape_of(rows, columns, kind):
    return jax.ShapeDtypeStruct((rows, columns), kind)


def chunk_rows(rows, half):
    chunk = rows // 2
    for step in range(2):
        whole = pl.ds(pl.multiple_of(half * rows + step * chunk, chunk), chunk)
        yield step, pl.ds(step * chunk, chunk), whole


def middle_kernel(
    flip,
    place_ref,
    hidden_hbm,
    piece0_any,
    piece1_any,
    piece2_any,
    piece3_any,
    w_mine_any,
    w_other_any,
    gain_ref,
    w_in_ref,
    w_ffout_ref,
    after_ref,
    norm_ref,
    act_ref,
    slope_ref,
    part_ref,
    hidden_s,
    mains,
    rests,
    w_out_s,
    sems,
):
    narrow = place_ref[0]
    side = narrow % 2
    half = side ^ flip
    rows = after_ref.shape[0]
    inner = w_out_s.shape[1]
    whole = pl.ds(pl.multiple_of(half * rows, rows), rows)
    loads = []
    for index, piece in enumerate((piece0_any, piece1_any, piece2_any, piece3_any)):
        loads.append((piece.at[whole, :], mains.at[narrow ^ index]))
        loads.append((piece.at[pl.ds(2 * rows, rows), :], rests.at[narrow ^ index]))
    for index in range(2):
        taken = pl.ds(index * inner, inner)
        loads.append((w_mine_any.at[taken, :], w_out_s.at[2 * index + side]))
        loads.append((w_other_any.at[taken, :], w_out_s.at[2 * index + 1 - side]))
    loads.append((hidden_hbm.at[whole, :], hidden_s))
    loads = [
        pltpu.make_async_copy(source, target, sems.at[index])
        for index, (source, target) in enumerate(loads)
    ]
    for load in loads:
        load.start()
    for load in loads:
        load.wait()
    for _, own, _ in chunk_rows(rows, 0):
        total = jnp.zeros((rows // 2, after_ref.shape[1]), jnp.float32)
        for index in range(4):
            rest = rests[index, own, :]
            width = rest.shape[1] // 2
            tail = jnp.where(half == 0, rest[:, :width], rest[:, width:])
            piece = jnp.concatenate([mains[index, own, :], tail], axis=1)
            total = total + plain_dot(piece, w_out_s[index])
        after = hidden_s[own, :].astype(jnp.float32) + total
        after_ref[own, :] = after
        norm = (after * norm_scale(after) * gain_ref[...].reshape(1, -1)).astype(jnp.bfloat16)
        norm_ref[own, :] = norm
        act, slope = split_gelu(plain_dot(norm, w_in_ref[...]))
        act_low = act.astype(jnp.bfloat16)
        act_ref[own, :] = act_low
        slope_ref[own, :] = slope.astype(jnp.bfloat16)
        part_ref[own, :] = plain_dot(act_low, w_ffout_ref[...]).astype(jnp.bfloat16)


def middle(flip, place, hidden_in, packed, w_outs, gain, w_in, w_ffout):
    token_count, model = hidden_in.shape
    hidden_count = w_in.shape[1]
    rows = token_count // 2
    low = jnp.bfloat16
    inputs = [("any", in_main(hidden_in))] + [("any", piece) for piece in packed]
    inputs += [("any", weight) for weight in w_outs]
    inputs += [("line", gain), ("near", w_in), ("near", w_ffout)]
    outputs = [
        ("near", shape_of(rows, model, jnp.float32)),
        ("near", shape_of(rows, model, low)),
        ("near", shape_of(rows, hidden_count, low)),
        ("near", shape_of(rows, hidden_count, low)),
        ("near", shape_of(rows, model, low)),
    ]
    scratch = [
        pltpu.VMEM((rows, model), low),
        pltpu.VMEM((4, rows, 128), low),
        pltpu.VMEM((4, rows, 128), low),
        pltpu.VMEM((4, w_outs[0].shape[0] // 2, model), low),
        pltpu.SemaphoreType.DMA((13,)),
    ]
    flops = 2 * rows * model * (model + 2 * hidden_count)
    return row_call(middle_kernel, flip, inputs, outputs, scratch, place, {}, flops)


def pool_kernel(flip, place_ref, lengths_ref, after_ref, total_ref, gain_ref, *refs):
    half = (place_ref[0] % 2) ^ flip
    rows, model = after_ref.shape
    chunk = rows // 2
    slots = lengths_ref.shape[0]
    if flip == 0:
        out_ref, pooled_ref = refs
        pooled = jnp.zeros(pooled_ref.shape, jnp.float32)
    else:
        positive_ref, partial_ref, out_ref, block_ref, rows_s = refs
        pooled = partial_ref[...]
    starts, ends = slot_lines(lengths_ref, (slots, 1), 0)
    for step, own, _ in chunk_rows(rows, half):
        value = after_ref[own, :] + total_ref[own, :].astype(jnp.float32)
        out_ref[own, :] = value
        high, rest = two_terms(value * norm_scale(value) * gain_ref[...].reshape(1, -1))
        token = half * rows + step * chunk
        token = token + lax.broadcasted_iota(jnp.int32, (slots, chunk), 1)
        member = as_low((token >= starts) & (token < ends))
        pooled = pooled + (plain_dot(member, high) + plain_dot(member, rest))
    if flip == 0:
        pooled_ref[...] = pooled
        return
    count = jnp.maximum(ends - starts, 1).astype(jnp.float32)
    slot = lax.broadcasted_iota(jnp.int32, (slots, 128), 0)
    lane = lax.broadcasted_iota(jnp.int32, (slots, 128), 1)
    partner = jnp.zeros((slots, 128), jnp.int32)
    for index in range(slots):
        partner = jnp.where(slot == index, positive_ref[index], partner)
    used = jnp.where(ends > starts, 1, 0)
    facts = jnp.where(lane == 0, used, jnp.where(lane == 1, partner >> 7, partner & 127))
    rows_s[:, :model] = pooled / count
    rows_s[:, model:] = facts.astype(jnp.float32)
    part = slots // 2
    own = rows_s[pl.ds(pl.multiple_of((place_ref[0] % 2) * part, part), part), :]
    block_ref[...] = own.astype(jnp.bfloat16)


def pool(flip, place, lengths, after, total, gain, more):
    rows, model = after.shape
    slots = lengths.shape[0]
    inputs = [("scalar", lengths), ("near", after), ("near", total), ("line", gain)]
    outputs = [("near", shape_of(rows, model, jnp.float32))]
    scratch = []
    if flip == 0:
        outputs.append(("near", shape_of(slots, model, jnp.float32)))
    else:
        positive, partial = more
        inputs += [("scalar", positive), ("near", partial)]
        outputs.append(("near", shape_of(slots // 2, model + 128, jnp.bfloat16)))
        scratch = [pltpu.VMEM((slots, model + 128), jnp.float32)]
    return row_call(pool_kernel, flip, inputs, outputs, scratch, place, {}, 2**24)


def assemble_kernel(place_ref, own_ref, far_ref, later_ref, out_hbm, token_ref, sems):
    rows = own_ref.shape[0]
    token_ref[...] = jnp.zeros(token_ref.shape, jnp.float32)
    copies = []
    for flip, ref in enumerate((own_ref, far_ref)):
        half = (place_ref[0] % 2) ^ flip
        target = out_hbm.at[pl.ds(pl.multiple_of(half * rows, rows), rows), :]
        copies.append(pltpu.make_async_copy(ref, target, sems.at[flip]))
    for copy in copies:
        copy.start()
    for copy in copies:
        copy.wait()


def assemble(place, own, far, later):
    rows, model = own.shape
    return pl.pallas_call(
        assemble_kernel,
        out_shape=(main_shape(2 * rows, model, own.dtype), shape_of(8, 128, jnp.float32)),
        in_specs=[SCALARS] + [ANYWHERE] * 3,
        out_specs=(ANYWHERE, VECTORS),
        scratch_shapes=[pltpu.SemaphoreType.DMA((2,))],
        compiler_params=pltpu.CompilerParams(vmem_limit_bytes=4 * MIB),
        cost_estimate=QUICK,
        name="assemble",
    )(in_main(place), own, far, later)


def contrast_kernel(groups, place_ref, *refs):
    mine, other = refs[:groups], refs[groups : 2 * groups]
    w_proj_ref, bias_ref, loss_ref, pooled_hbm, low_hbm, bias_grad_ref = refs[
        2 * groups : 2 * groups + 6
    ]
    slot_grad_ref, pooled_ref, low_ref, sems, embeds, units, facts, spreads, losses = refs[
        2 * groups + 6 :
    ]
    narrow, wide = place_ref[0], place_ref[1]
    part = mine[0].shape[0] // 2
    model = w_proj_ref.shape[0]
    slots = 2 * part
    count = 2 * groups * slots
    block = min(count, 256)
    side = narrow % 2
    for refs_at, at in ((mine, side), (other, 1 - side)):
        for index, ref in enumerate(refs_at):
            for odd in range(2):
                pack = wide ^ (2 * index + odd)
                rows = pl.ds(pl.multiple_of(pack * slots + at * part, part), part)
                pooled_ref[rows, :] = ref[odd * part : (odd + 1) * part, :model]
                facts[rows, :] = ref[odd * part : (odd + 1) * part, model:]
    for start in range(0, count, block):
        rows = pl.ds(start, block)
        embed = plain_dot(pooled_ref[rows, :], w_proj_ref[...]) + bias_ref[...].reshape(1, -1)
        embeds[rows, :] = embed
        scale = lax.rsqrt(jnp.sum(embed * embed, axis=1, keepdims=True) + EPSILON)
        units[rows, :] = (embed * scale).astype(jnp.bfloat16)
    pick_row = lax.broadcasted_iota(jnp.int32, (8, 128), 0)
    pick_lane = lax.broadcasted_iota(jnp.int32, (8, 128), 1)
    pick = as_low(pick_row == pick_lane)
    lines = row_dot(pick, facts[...])
    used_line = lines[:1] > 0.5
    partner_line = (lines[1:2] * 128.0 + lines[2:3]).astype(jnp.int32)
    column = lax.broadcasted_iota(jnp.int32, (block, count), 1)
    row = lax.broadcasted_iota(jnp.int32, (block, count), 0)

    def columns_of(rows):
        values = facts[rows, :].astype(jnp.float32)
        used = values[:, :1] > 0.5
        partner = (values[:, 1:2] * 128.0 + values[:, 2:3]).astype(jnp.int32)
        return used, partner

    for start in range(0, count, block):
        rows = pl.ds(start, block)
        sims = CONTRAST * row_dot(units[rows, :], units[...])
        used, partner = columns_of(rows)
        usable = used_line & (column != row + start)
        masked = jnp.where(usable, sims, -1e30)
        top = jnp.max(masked, axis=1, keepdims=True)
        total = jnp.sum(jnp.exp(masked - top), axis=1, keepdims=True)
        spread = top + jnp.log(total)
        score = jnp.sum(jnp.where(column == partner, sims, 0.0), axis=1, keepdims=True)
        losses[rows, :] = jnp.where(used, spread - score, 0.0)
        turned = jnp.transpose(jnp.broadcast_to(spread, (block, 128)))
        spreads[:, start : start + block] = turned[:8]
    loss = losses[pl.ds(pl.multiple_of(wide * slots, slots), slots), :]
    loss = jnp.transpose(jnp.broadcast_to(loss, (slots, 128)))
    loss_ref[...] = loss[:1, :].reshape(slots)
    bias_grad = jnp.zeros((1, model), jnp.float32)
    for start in range(0, count, block):
        rows = pl.ds(start, block)
        sims = CONTRAST * row_dot(units[rows, :], units[...])
        used, partner = columns_of(rows)
        differ = column != row + start
        spread = jnp.transpose(jnp.broadcast_to(spreads[:1, start : start + block], (128, block)))
        masked = jnp.where(used_line & differ, sims, -1e30)
        ahead = jnp.exp(masked - spread[:, :1]) - jnp.where(column == partner, 1.0, 0.0)
        masked = jnp.where(used & differ, sims, -1e30)
        behind = jnp.exp(masked - spreads[:1, :]) - jnp.where(
            row + start == partner_line, 1.0, 0.0
        )
        both = jnp.where(used, ahead, 0.0) + jnp.where(used_line, behind, 0.0)
        high, rest = two_terms(both)
        grad = CONTRAST * (plain_dot(high, units[...]) + plain_dot(rest, units[...]))
        embed = embeds[rows, :]
        scale = lax.rsqrt(jnp.sum(embed * embed, axis=1, keepdims=True) + EPSILON)
        share = jnp.sum(embed * grad, axis=1, keepdims=True)
        back = scale * grad - (scale * scale * scale) * embed * share
        back_low = back.astype(jnp.bfloat16)
        low_ref[rows, :] = back_low
        bias_grad = bias_grad + jnp.sum(back_low.astype(jnp.float32), axis=0, keepdims=True)
    bias_grad_ref[...] = bias_grad.reshape(model)
    own = low_ref[pl.ds(pl.multiple_of(wide * slots, slots), slots), :]
    stores = [
        pltpu.make_async_copy(pooled_ref, pooled_hbm, sems.at[0]),
        pltpu.make_async_copy(low_ref, low_hbm, sems.at[1]),
    ]
    for store in stores:
        store.start()
    slot_grad_ref[...] = row_dot(own, w_proj_ref[...])
    for store in stores:
        store.wait()


def gathered_blocks(block):
    pair = jnp.concatenate([block, exchange(block, "wide", 1)], axis=0)
    mine = [pair]
    for mask in range(2, lax.axis_size("wide"), 2):
        mine.append(exchange(pair, "wide", mask))
    return (*mine, *(exchange(blocks, "narrow", 1) for blocks in mine))


def contrast(place, block, w_proj, proj_bias):
    parts = gathered_blocks(block)
    part = block.shape[0]
    model = w_proj.shape[0]
    count = len(parts) * 2 * part
    low = jnp.bfloat16
    return pl.pallas_call(
        functools.partial(contrast_kernel, len(parts) // 2),
        out_shape=(
            jax.ShapeDtypeStruct((2 * part,), jnp.float32),
            main_shape(count, model, low),
            main_shape(count, model, low),
            jax.ShapeDtypeStruct((model,), jnp.float32),
            shape_of(2 * part, model, jnp.float32),
        ),
        in_specs=[SCALARS] + [VECTORS] * (len(parts) + 2),
        out_specs=(VECTORS, ANYWHERE, ANYWHERE, VECTORS, VECTORS),
        scratch_shapes=[
            pltpu.VMEM((count, model), low),
            pltpu.VMEM((count, model), low),
            pltpu.SemaphoreType.DMA((2,)),
            pltpu.VMEM((count, model), jnp.float32),
            pltpu.VMEM((count, model), low),
            pltpu.VMEM((count, 128), low),
            pltpu.VMEM((8, count), jnp.float32),
            pltpu.VMEM((count, 1), jnp.float32),
        ],
        compiler_params=pltpu.CompilerParams(vmem_limit_bytes=(12 if count <= 256 else 56) * MIB),
        cost_estimate=pl.CostEstimate(
            flops=2 * count * model * (model + 4 * count),
            bytes_accessed=4 * model * model,
            transcendentals=3 * count * count,
        ),
        name="contrast",
    )(in_main(place), *parts, w_proj, in_main(proj_bias))


def turn_kernel(
    flip,
    place_ref,
    lengths_ref,
    out_ref,
    slot_grad_ref,
    slope_ref,
    gain_ref,
    w_ffout_ref,
    w_in_ref,
    grad_ref,
    low_ref,
    pre_ref,
    part_ref,
    gain_grad_ref,
):
    half = (place_ref[0] % 2) ^ flip
    rows = out_ref.shape[0]
    chunk = rows // 2
    slots = lengths_ref.shape[0]
    starts, ends = slot_lines(lengths_ref, (slots, 1), 0)
    count = jnp.maximum(ends - starts, 1).astype(jnp.float32)
    high, rest = two_terms(slot_grad_ref[...] / count)
    starts, ends = slot_lines(lengths_ref, (1, slots), 1)
    total = jnp.zeros(gain_grad_ref.shape, jnp.float32)
    for step, own, _ in chunk_rows(rows, half):
        token = half * rows + step * chunk
        token = token + lax.broadcasted_iota(jnp.int32, (chunk, slots), 0)
        member = as_low((token >= starts) & (token < ends))
        final_grad = plain_dot(member, high) + plain_dot(member, rest)
        gain = gain_ref[...].reshape(1, -1)
        grad, gain_grad = norm_back(out_ref[own, :], gain, final_grad)
        total = total + gain_grad
        grad_ref[own, :] = grad
        low = grad.astype(jnp.bfloat16)
        low_ref[own, :] = low
        pre = row_dot(low, w_ffout_ref[...]) * slope_ref[own, :].astype(jnp.float32)
        pre = pre.astype(jnp.bfloat16)
        pre_ref[own, :] = pre
        part_ref[own, :] = row_dot(pre, w_in_ref[...]).astype(jnp.bfloat16)
    gain_grad_ref[...] = total


def turn(flip, place, lengths, layer_out, slot_grad, slope, gain, w_ffout, w_in):
    rows, hidden_count = slope.shape
    model = layer_out.shape[1]
    low = jnp.bfloat16
    inputs = [("scalar", lengths), ("near", layer_out), ("near", slot_grad), ("near", slope)]
    inputs += [("line", gain), ("near", w_ffout), ("near", w_in)]
    outputs = [
        ("near", shape_of(rows, model, jnp.float32)),
        ("near", shape_of(rows, model, low)),
        ("near", shape_of(rows, hidden_count, low)),
        ("near", shape_of(rows, model, low)),
        ("near", shape_of(1, model, jnp.float32)),
    ]
    flops = 4 * rows * model * hidden_count
    return row_call(turn_kernel, flip, inputs, outputs, [], place, {}, flops)


def join_kernel(
    flip,
    place_ref,
    out_grad_ref,
    after_ref,
    total_ref,
    gain_ref,
    w_out_ref,
    mid_ref,
    low_ref,
    mixed_grad_ref,
    gain_grad_ref,
):
    total = jnp.zeros(gain_grad_ref.shape, jnp.float32)
    gain = gain_ref[...].reshape(1, -1)
    for _, own, _ in chunk_rows(after_ref.shape[0], 0):
        back, gain_grad = norm_back(
            after_ref[own, :], gain, total_ref[own, :].astype(jnp.float32)
        )
        total = total + gain_grad
        mid = out_grad_ref[own, :] + back
        mid_ref[own, :] = mid
        low = mid.astype(jnp.bfloat16)
        low_ref[own, :] = low
        mixed_grad_ref[own, :] = row_dot(low, w_out_ref[...]).astype(jnp.bfloat16)
    gain_grad_ref[...] = total


def join(flip, place, out_grad, after, total, gain, w_out):
    rows, model = out_grad.shape
    inner = w_out.shape[0]
    low = jnp.bfloat16
    inputs = [("near", out_grad), ("near", after), ("near", total)]
    inputs += [("line", gain), ("near", w_out)]
    outputs = [
        ("near", shape_of(rows, model, jnp.float32)),
        ("near", shape_of(rows, model, low)),
        ("near", shape_of(rows, inner, low)),
        ("near", shape_of(1, model, jnp.float32)),
    ]
    flops = 2 * rows * model * inner
    return row_call(join_kernel, flip, inputs, outputs, [], place, {}, flops)


def last_kernel(flip, place_ref, mid_ref, hidden_ref, total_ref, gain_ref, *refs):
    out_hbm, token_ref, rows_s, sems = refs[-4:]
    half = (place_ref[0] % 2) ^ flip
    gain = gain_ref[...].reshape(1, -1)
    copies = []
    for step, own, whole in chunk_rows(mid_ref.shape[0], half):
        back, _ = norm_back(
            hidden_ref[whole, :].astype(jnp.float32), gain, total_ref[own, :].astype(jnp.float32)
        )
        rows_s[own, :] = mid_ref[own, :] + back
        copy = pltpu.make_async_copy(rows_s.at[own, :], out_hbm.at[whole, :], sems.at[step])
        copy.start()
        copies.append(copy)
    token_ref[...] = jnp.zeros(token_ref.shape, jnp.float32)
    for copy in copies:
        copy.wait()


def last(flip, place, mid, hidden_in, total, gain, given):
    rows, model = mid.shape
    inputs = [("near", mid), ("near", hidden_in), ("near", total), ("line", gain)]
    inputs.append(("any", given))
    aliases = {5: 0} if flip == 1 else {}
    outputs = [
        ("any", main_shape(2 * rows, model, jnp.float32)),
        ("near", shape_of(8, 128, jnp.float32)),
    ]
    scratch = [pltpu.VMEM((rows, model), jnp.float32), pltpu.SemaphoreType.DMA((2,))]
    return row_call(last_kernel, flip, inputs, outputs, scratch, place, aliases, 2**22)


def sum_kernel(count, *refs):
    refs[-1][...] = arrived_sum(refs[:count])


def summed(blocks, later):
    return pl.pallas_call(
        functools.partial(sum_kernel, len(blocks)),
        out_shape=jax.ShapeDtypeStruct(blocks[0].shape, jnp.float32),
        in_specs=[VECTORS] * len(blocks) + [ANYWHERE],
        out_specs=VECTORS,
        compiler_params=pltpu.CompilerParams(vmem_limit_bytes=12 * MIB),
        cost_estimate=QUICK,
        name="summed",
    )(*blocks, later)


def pair_grads_kernel(place_ref, *refs):
    lefts, rights = refs[0:2], refs[2:4]
    value = col_dot(lefts[0][...], rights[0][...]) + col_dot(lefts[1][...], rights[1][...])
    split_pairs(value, place_ref[1] % 2, refs[5], refs[6])


def split_pairs(value, parity, keep_ref, send_ref):
    pairs = keep_ref.shape[0]
    rows = value.shape[0] // (2 * pairs)
    for pair in range(pairs):
        first = value[2 * pair * rows : (2 * pair + 1) * rows].astype(jnp.bfloat16)
        second = value[(2 * pair + 1) * rows : (2 * pair + 2) * rows].astype(jnp.bfloat16)
        keep_ref[pair, :rows, :] = jnp.where(parity == 0, first, second)
        send_ref[pair, :rows, :] = jnp.where(parity == 0, second, first)


def pair_grads(place, lefts, rights, later, pairs):
    rows, model = lefts[0].shape
    width = rights[0].shape[1]
    piece = jax.ShapeDtypeStruct((pairs, model // (2 * pairs), width), jnp.bfloat16)
    return pl.pallas_call(
        pair_grads_kernel,
        out_shape=(piece, piece),
        in_specs=[SCALARS] + [VECTORS] * 4 + [ANYWHERE],
        out_specs=(VECTORS, VECTORS),
        compiler_params=pltpu.CompilerParams(vmem_limit_bytes=16 * MIB),
        cost_estimate=pl.CostEstimate(
            flops=4 * rows * model * width, bytes_accessed=5 * rows * model, transcendentals=0
        ),
        name="pair_grads",
    )(in_main(place), *lefts, *rights, later)


def add_kernel(left_ref, right_ref, *refs):
    refs[-1][...] = add_low(left_ref[...], right_ref[...])


def add_after(left, right, *later):
    return pl.pallas_call(
        add_kernel,
        out_shape=jax.ShapeDtypeStruct(left.shape, jnp.bfloat16),
        in_specs=[VECTORS, VECTORS] + [ANYWHERE] * len(later),
        out_specs=VECTORS,
        compiler_params=pltpu.CompilerParams(vmem_limit_bytes=12 * MIB),
        cost_estimate=pl.CostEstimate(
            flops=left.size, bytes_accessed=6 * left.size, transcendentals=0
        ),
        name="add_after",
    )(left, right, *later)


def halve_kernel(count, later_count, place_ref, *refs):
    own = place_ref[1] // 2
    outs = refs[2 * count + later_count :]
    width = refs[0].shape[2]
    for index, out in enumerate(outs):
        for part in range(count):
            out[:, part * width : (part + 1) * width] = add_low(
                refs[2 * part][own ^ index], refs[2 * part + 1][own ^ index]
            )


def halved(place, sides, *later):
    pairs, rows, width = sides[0].shape
    count = len(sides) // 2
    return pl.pallas_call(
        functools.partial(halve_kernel, count, len(later)),
        out_shape=(shape_of(rows, count * width, jnp.bfloat16),) * pairs,
        in_specs=[SCALARS] + [VECTORS] * len(sides) + [ANYWHERE] * len(later),
        out_specs=(VECTORS,) * pairs,
        compiler_params=pltpu.CompilerParams(vmem_limit_bytes=16 * MIB),
        cost_estimate=QUICK,
        name="halved",
    )(in_main(place), *sides, *later)


def arrived_sum(refs):
    total = refs[0][...].astype(jnp.float32)
    for ref in refs[1:]:
        total = total + ref[...].astype(jnp.float32)
    return total


def head_grads_kernel(
    place_ref,
    norm_ref,
    dq_ref,
    dk_ref,
    dv_ref,
    mid_own_ref,
    mid_far_ref,
    mixed_ref,
    one_ref,
    two_own_ref,
    two_far_ref,
    last_own_ref,
    last_far_ref,
    table_ref,
    later_ref,
    keep_ref,
    send_ref,
):
    half, model = mid_own_ref.shape
    side = place_ref[0] % 2
    own_rows = pl.ds(pl.multiple_of(side * half, half), half)
    far_rows = pl.ds(pl.multiple_of((1 - side) * half, half), half)
    norm = norm_ref[...]
    values = [col_dot(norm, ref[...]) for ref in (dq_ref, dk_ref, dv_ref)]
    last = col_dot(mid_own_ref[...], mixed_ref[own_rows, :])
    values.append(last + col_dot(mid_far_ref[...], mixed_ref[far_rows, :]))
    split_pairs(jnp.concatenate(values, axis=1), place_ref[1] % 2, keep_ref, send_ref)
    table = [table_ref[head : head + 1, :] for head in range(model // 128)]
    small = jnp.concatenate(
        [
            one_ref[...],
            two_own_ref[...] + two_far_ref[...],
            last_own_ref[...] + last_far_ref[...],
            jnp.concatenate(table, axis=1),
        ],
        axis=0,
    )
    high, rest = two_terms(small)
    small = jnp.concatenate([high, rest, jnp.zeros((8, model), jnp.bfloat16)], axis=0)
    rows = keep_ref.shape[1] - 16
    for pair in range(keep_ref.shape[0]):
        keep_ref[pair, rows:, :] = small
        send_ref[pair, rows:, :] = small


def head_grads(place, norm, grads, mid_own, mid_far, mixed, lines, table, later, pairs):
    model = norm.shape[1]
    piece = jax.ShapeDtypeStruct((pairs, model // (2 * pairs) + 16, model), jnp.bfloat16)
    return pl.pallas_call(
        head_grads_kernel,
        out_shape=(piece, piece),
        in_specs=[SCALARS] + [VECTORS] * 13 + [ANYWHERE],
        out_specs=(VECTORS, VECTORS),
        compiler_params=pltpu.CompilerParams(vmem_limit_bytes=24 * MIB),
        cost_estimate=QUICK,
        name="head_grads",
    )(in_main(place), norm, *grads, mid_own, mid_far, mixed, *lines, table, later)


def finish_kernel(count, *refs):
    dq_ref, dk_ref, dv_ref, out_ref, one_ref, two_ref, last_ref, rest_ref = refs[count + 1 :]
    total = arrived_sum(refs[:count])
    rows, inner = dq_ref.shape
    model = total.shape[1]
    dq_ref[...] = total[:rows, :inner]
    dk_ref[...] = total[:rows, inner : 2 * inner]
    dv_ref[...] = total[:rows, 2 * inner : 3 * inner]
    last = total[:rows, 3 * inner :]
    out_ref[...] = jnp.transpose(last) if out_ref.shape[0] == inner else last
    small = total[rows : rows + 4] + total[rows + 4 : rows + 8]
    one_ref[...] = small[0:1].reshape(model)
    two_ref[...] = small[1:2].reshape(model)
    last_ref[...] = small[2:3].reshape(model)
    lines = [small[3:4, index * 128 : (index + 1) * 128] for index in range(model // 128)]
    lines.append(jnp.zeros((8 - len(lines), 128), jnp.float32))
    rest_ref[...] = jnp.concatenate(lines, axis=0)


def finish(arrived, inner, later):
    rows, model = arrived[0].shape
    rows = rows - 16
    full = jnp.float32
    line = jax.ShapeDtypeStruct((model,), full)
    piece = shape_of(rows, inner, full)
    turned = rows % 8 == 0
    results = pl.pallas_call(
        functools.partial(finish_kernel, len(arrived)),
        out_shape=(
            piece,
            piece,
            piece,
            shape_of(inner, rows, full) if turned else piece,
            line,
            line,
            line,
            shape_of(8, 128, full),
        ),
        in_specs=[VECTORS] * len(arrived) + [ANYWHERE],
        out_specs=(VECTORS,) * 8,
        compiler_params=pltpu.CompilerParams(vmem_limit_bytes=12 * MIB),
        cost_estimate=pl.CostEstimate(
            flops=8 * rows * model, bytes_accessed=16 * rows * model, transcendentals=0
        ),
        name="finish",
    )(*arrived, later)
    grad_out = results[3] if turned else results[3].T
    return (*results[:3], grad_out, *results[4:])


def body(
    hidden_in,
    lengths,
    positive,
    norm1_gain,
    w_query,
    w_key,
    w_value,
    rel_bias,
    w_out,
    norm2_gain,
    w_in,
    w_ffout,
    final_gain,
    w_proj,
    proj_bias,
):
    bucket_count, head_count = rel_bias.shape
    pairs = lax.axis_size("wide") // 2
    wide = lax.axis_index("wide")
    place = jnp.stack([lax.axis_index("narrow"), wide]).astype(jnp.int32)
    table = rel_bias.T
    weights = (w_query.T, w_key.T, w_value.T)
    w_mine = lax.all_gather(
        w_out, "narrow", axis=0, axis_index_groups=[[0, 2], [1, 3]], tiled=True
    )

    norm1, query, key, value, mixed, packed, spread = attend(
        lengths, table, hidden_in, norm1_gain, *weights
    )
    across = exchange(packed, "narrow", 2)
    pieces = (packed, exchange(packed, "narrow", 1), across, exchange(across, "narrow", 1))
    w_outs = (w_mine, exchange(w_mine, "narrow", 1))
    far = middle(1, place, hidden_in, pieces, w_outs, norm2_gain, w_in, w_ffout)
    own = middle(0, place, hidden_in, pieces, w_outs, norm2_gain, w_in, w_ffout)
    after_far, norm2_far, act_far, slope_far, part_far = far
    after_own, norm2_own, act_own, slope_own, part_own = own
    total_own, total_far = summed_over_narrow(part_own, part_far)
    out_own, pooled_own = pool(0, place, lengths, after_own, total_own, final_gain, None)
    out_far, block = pool(
        1, place, lengths, after_far, total_far, final_gain, (positive, pooled_own)
    )
    loss, pooled_all, embed_low, bias_grad, slot_grad = contrast(place, block, w_proj, proj_bias)

    share = hidden_in.shape[1] // (2 * pairs)
    pooled_cols = lax.dynamic_slice_in_dim(pooled_all, wide * share, share, 1)
    grad_proj = dot_over(pooled_cols, embed_low, 0, 0)
    far = turn(1, place, lengths, out_far, slot_grad, slope_far, final_gain, w_ffout, w_in)
    own = turn(0, place, lengths, out_own, slot_grad, slope_own, final_gain, w_ffout, w_in)
    out_grad_far, out_low_far, pre_far, part_far, last_far = far
    out_grad_own, out_low_own, pre_own, part_own, last_own = own
    part = add_low(part_own, exchange(part_far, "narrow", 1))
    came = exchange(part, "narrow", 2)
    keep_a, send_a = pair_grads(place, (out_low_far, out_low_own), (act_far, act_own), part, pairs)
    came_a = exchange(send_a, "wide", 1)
    keep_b, send_b = pair_grads(
        place, (norm2_far, norm2_own), (pre_far, pre_own), send_a, pairs
    )
    came_b = exchange(send_b, "wide", 1)
    layer_out, token = assemble(place, out_own, out_far, send_b)
    total_own = add_after(part, came, came_a, grad_proj, token)
    total_far = exchange(total_own, "narrow", 1)
    mid_own, mid_low_own, mixed_grad_own, two_own = join(
        0, place, out_grad_own, after_own, total_own, norm2_gain, w_out
    )
    mid_far, mid_low_far, mixed_grad_far, two_far = join(
        1, place, out_grad_far, after_far, total_far, norm2_gain, w_out
    )
    a_half = halved(place, (keep_a, came_a), total_own)
    a_arrived = over_parity(a_half)
    back = attend_back(
        place,
        lengths,
        table,
        query,
        key,
        value,
        (mixed_grad_own, mixed_grad_far),
        spread,
        hidden_in,
        weights,
        norm1,
        mixed,
        (),
    )
    dq, dk, dv, table_lines, hidden_near, weights_near, norm1_near, mixed_near = back
    grads = (dq, dk, dv)
    part_far, one_far = norm1_parts(
        1, place, grads, hidden_near, weights_near, (came_b, *a_arrived[1:])
    )
    far_came = exchange(part_far, "narrow", 1)
    part_own, one_own = norm1_parts(0, place, grads, hidden_near, weights_near, (part_far,))
    one = one_far + one_own
    one = one + exchange(one, "narrow", 1)
    one = one + exchange(one, "narrow", 2)
    part = add_after(part_own, far_came, one)
    came = exchange(part, "narrow", 2)
    head_keep, head_send = head_grads(
        place,
        norm1_near,
        grads,
        mid_low_own,
        mid_low_far,
        mixed_near,
        (one, two_own, two_far, last_own, last_far),
        table_lines,
        part,
        pairs,
    )
    head_came = exchange(head_send, "wide", 1)
    b_half = halved(place, (keep_b, came_b), head_send)
    b_arrived = over_parity(b_half)
    total_own = add_after(part, came, head_came, *b_arrived[1:])
    total_far = exchange(total_own, "narrow", 1)
    head_half = halved(place, (head_keep, head_came), total_own)
    head_arrived = over_parity(head_half)
    given, _ = last(0, place, mid_own, hidden_near, total_own, norm1_gain, total_own)
    grad_input, token = last(1, place, mid_far, hidden_near, total_far, norm1_gain, given)
    grad_ffout = summed(a_arrived, head_half[0]).T
    grad_in = summed(b_arrived, head_half[0])
    inner = query.shape[1]
    grad_query, grad_key, grad_value, grad_out, one, two, three, lines = finish(
        head_arrived, inner, token
    )
    return (
        layer_out,
        loss,
        grad_input,
        one,
        grad_query,
        grad_key,
        grad_value,
        lines[:head_count, :bucket_count].T,
        grad_out,
        two,
        grad_in,
        grad_ffout,
        three,
        grad_proj,
        bias_grad,
    )


def solution(mesh):
    in_specs = (
        P("wide", None),
        P("wide"),
        P("wide"),
        P(),
        P(None, "narrow"),
        P(None, "narrow"),
        P(None, "narrow"),
        P(None, "narrow"),
        P("narrow", None),
        P(),
        P(None, "narrow"),
        P("narrow", None),
        P(),
        P(),
        P(),
    )
    out_specs = (
        P("wide", None),
        P("wide"),
        P("wide", None),
        P(),
        P("wide", "narrow"),
        P("wide", "narrow"),
        P("wide", "narrow"),
        P(None, "narrow"),
        P("narrow", "wide"),
        P(),
        P("wide", "narrow"),
        P("narrow", "wide"),
        P(),
        P("wide", None),
        P(),
    )
    return jax.shard_map(body, mesh=mesh, in_specs=in_specs, out_specs=out_specs, check_vma=False)
```

```python
import functools

import jax
import jax.numpy as jnp
from jax import lax
from jax.experimental import pallas as pl
from jax.experimental.pallas import tpu as pltpu
from jax.sharding import PartitionSpec as P

EPSILON = 1e-06
CONTRAST = 30.0
THRESHOLDS = (12, 16, 23, 32, 46, 64, 91)
GELU = 0.7978845608028654
CUBE = 0.044715
BLOCK = 128
MIB = 1024 * 1024
QUICK = pl.CostEstimate(flops=2**20, bytes_accessed=2**16, transcendentals=0)
SCALARS = pl.BlockSpec(memory_space=pltpu.SMEM)
VECTORS = pl.BlockSpec(memory_space=pltpu.VMEM)
ANYWHERE = pl.BlockSpec(memory_space=pl.ANY)


def in_main(value):
    return pltpu.with_memory_space_constraint(value, pltpu.HBM)


def exchange(value, axis, step):
    count = lax.axis_size(axis)
    return lax.ppermute(value, axis, [(k, k ^ step) for k in range(count)])


def add_low(left, right):
    return (left.astype(jnp.float32) + right.astype(jnp.float32)).astype(jnp.bfloat16)


def summed_over_narrow(keep, send):
    part = add_low(keep, exchange(send, "narrow", 1))
    own = add_low(part, exchange(part, "narrow", 2))
    return own, exchange(own, "narrow", 1)


def over_parity(blocks):
    count = lax.axis_size("wide")
    return (blocks[0], *(exchange(blocks[k], "wide", 2 * k) for k in range(1, count // 2)))


def two_terms(value):
    high = value.astype(jnp.bfloat16)
    return high, (value - high.astype(jnp.float32)).astype(jnp.bfloat16)


def offset_buckets(offset):
    distance = jnp.abs(offset)
    far_bucket = 8 + sum(((distance >= limit).astype(jnp.int32) for limit in THRESHOLDS))
    return jnp.where(distance < 8, distance, far_bucket) + 16 * (offset > 0).astype(jnp.int32)


def dot_over(left, right, left_dim, right_dim):
    return lax.dot_general(
        left, right, (((left_dim,), (right_dim,)), ((), ())), preferred_element_type=jnp.float32
    )


def row_dot(left, right):
    return lax.dot_general(
        left, right, (((1,), (1,)), ((), ())), preferred_element_type=jnp.float32
    )


def plain_dot(left, right):
    return lax.dot_general(
        left, right, (((1,), (0,)), ((), ())), preferred_element_type=jnp.float32
    )


def col_dot(left, right):
    return lax.dot_general(
        left, right, (((0,), (0,)), ((), ())), preferred_element_type=jnp.float32
    )


def slot_edges(lengths_ref, position):
    low = jnp.zeros_like(position)
    high = jnp.zeros_like(position)
    start = jnp.int32(0)
    for slot in range(lengths_ref.shape[0]):
        reached = position >= start
        low = jnp.where(reached, start, low)
        start_next = start + lengths_ref[slot]
        high = jnp.where(reached, start_next, high)
        start = start_next
    padded = position >= start
    return jnp.where(padded, position, low), jnp.where(padded, position + 1, high)


def bias_tiles(table_ref, tiles, turned):
    head_count, bucket_count = table_ref.shape
    lane = lax.broadcasted_iota(jnp.int32, (8, 4 * BLOCK), 1)
    offset = 2 * BLOCK - lane if turned else lane - 2 * BLOCK
    bucket = offset_buckets(offset)
    for head in range(head_count):
        line = jnp.zeros((8, 4 * BLOCK), jnp.float32)
        for index in range(bucket_count):
            line = jnp.where(bucket == index, table_ref[head, index], line)
        spread = jnp.broadcast_to(line[:1], (BLOCK, 4 * BLOCK))
        tiles[head] = pltpu.roll(spread, 0, 1, stride=1, stride_axis=0)


def unrolled_sum(tile):
    width = tile.shape[1]
    group = tile[:8]
    for first in range(8, tile.shape[0], 8):
        group = group + pltpu.roll(tile[first : first + 8], width - first, 1)
    line = group[:1]
    for row in range(1, 8):
        line = line + pltpu.roll(group, width - row, 1)[row : row + 1]
    return line


def attend_kernel(
    lengths_ref,
    table_ref,
    hidden_hbm,
    gain_ref,
    wq_hbm,
    wk_hbm,
    wv_hbm,
    norm_hbm,
    q_hbm,
    k_hbm,
    v_hbm,
    mixed_hbm,
    packed_hbm,
    spread_hbm,
    tiles,
    heads_q,
    heads_k,
    heads_v,
    heads_o,
    edges,
    spreads,
    hidden_ref,
    wq_ref,
    wk_ref,
    wv_ref,
    norm_ref,
    q_ref,
    k_ref,
    v_ref,
    mixed_ref,
    packed_ref,
    spread_ref,
    came,
    left,
):
    token_count = hidden_ref.shape[0]
    head_count, bucket_count = table_ref.shape
    width = q_ref.shape[1] // head_count
    chunk = 2 * BLOCK
    blocks = token_count // BLOCK
    starts = range(0, token_count, chunk)
    loads = []
    for index, (source, target) in enumerate(
        ((wq_hbm, wq_ref), (wk_hbm, wk_ref), (wv_hbm, wv_ref))
    ):
        loads.append(pltpu.make_async_copy(source, target, came.at[index]))
    for index, start in enumerate(starts):
        rows = pl.ds(start, chunk)
        loads.append(
            pltpu.make_async_copy(
                hidden_hbm.at[rows, :], hidden_ref.at[rows, :], came.at[3 + index]
            )
        )
    for load in (loads[3], *loads[:3], *loads[4:]):
        load.start()
    bias_tiles(table_ref, tiles, False)
    stores = []

    def store(source, target):
        copy = pltpu.make_async_copy(source, target, left.at[len(stores)])
        copy.start()
        stores.append(copy)

    for index, start in enumerate(starts):
        rows = pl.ds(start, chunk)
        loads[3 + index].wait()
        values = hidden_ref[rows, :].astype(jnp.float32)
        norm = (values * norm_scale(values) * gain_ref[...].reshape(1, -1)).astype(jnp.bfloat16)
        norm_ref[rows, :] = norm
        if index == 0:
            for load in loads[:3]:
                load.wait()
        for weight, out, parts in (
            (wq_ref, q_ref, heads_q),
            (wk_ref, k_ref, heads_k),
            (wv_ref, v_ref, heads_v),
        ):
            value = row_dot(norm, weight[...]).astype(jnp.bfloat16)
            out[rows, :] = value
            for head in range(head_count):
                parts[head, rows, :] = value[:, head * width : (head + 1) * width]
    for source, target in (
        (norm_ref, norm_hbm),
        (q_ref, q_hbm),
        (k_ref, k_hbm),
        (v_ref, v_hbm),
    ):
        store(source, target)
    lane = lax.broadcasted_iota(jnp.int32, (1, BLOCK), 1)

    def finish(head, rows, scores):
        top = jnp.max(scores, axis=1, keepdims=True)
        weights = jnp.exp(scores - top)
        total = jnp.sum(weights, axis=1, keepdims=True)
        keep = jnp.where(lane == head, top + jnp.log(total), spreads[rows, :])
        spreads[rows, :] = keep
        return weights.astype(jnp.bfloat16), 1.0 / total

    @pl.when(lengths_ref[0] > lengths_ref.shape[0])
    def document():
        def one_head(head, carry):
            keys, values = heads_k[head], heads_v[head]
            past = table_ref[head, bucket_count // 2 - 1]
            future = table_ref[head, bucket_count - 1]
            for start in range(0, token_count, chunk):
                rows = pl.ds(start, chunk)
                raw = row_dot(heads_q[head, rows, :], keys)
                lines = []
                for part in range(chunk // BLOCK):
                    line = []
                    for block in range(blocks):
                        away = block - start // BLOCK - part
                        piece = raw[
                            part * BLOCK : (part + 1) * BLOCK, block * BLOCK : (block + 1) * BLOCK
                        ]
                        if abs(away) <= 1:
                            first = (2 + away) * BLOCK
                            piece = piece + tiles[head, :, first : first + BLOCK]
                        else:
                            piece = piece + (past if away < 0 else future)
                        line.append(piece)
                    lines.append(jnp.concatenate(line, axis=1))
                weights, scale = finish(head, rows, jnp.concatenate(lines, axis=0))
                heads_o[head, rows, :] = (plain_dot(weights, values) * scale).astype(jnp.bfloat16)
            return carry

        lax.fori_loop(0, head_count, one_head, 0)

    @pl.when(lengths_ref[0] <= lengths_ref.shape[0])
    def queries():
        position = lax.broadcasted_iota(jnp.int32, (8, token_count), 1)
        low, high = slot_edges(lengths_ref, position)
        edges[0] = low
        edges[1] = high

        def one_head(head, carry):
            for block in range(blocks):
                first = max(block - 1, 0)
                last = min(block + 1, blocks - 1) + 1
                rows = pl.ds(block * BLOCK, BLOCK)
                window = pl.ds(first * BLOCK, (last - first) * BLOCK)
                scores = row_dot(heads_q[head, rows, :], heads_k[head, window, :])
                shift = (2 + first - block) * BLOCK
                scores = scores + tiles[head, :, shift : shift + (last - first) * BLOCK]
                token = block * BLOCK + lax.broadcasted_iota(jnp.int32, scores.shape, 0)
                inside = (token >= edges[0, :1, window]) & (token < edges[1, :1, window])
                weights, scale = finish(head, rows, jnp.where(inside, scores, -1e30))
                heads_o[head, rows, :] = (
                    plain_dot(weights, heads_v[head, window, :]) * scale
                ).astype(jnp.bfloat16)
            return carry

        lax.fori_loop(0, head_count, one_head, 0)

    half = token_count // 2
    pair = jnp.concatenate([heads_o[0], heads_o[1]], axis=1)
    mixed_ref[:, : 2 * width] = pair
    mixed_ref[:, 2 * width :] = heads_o[2]
    packed_ref[:token_count, :] = pair
    packed_ref[token_count:, :] = jnp.concatenate([heads_o[2, :half], heads_o[2, half:]], axis=1)
    store(packed_ref, packed_hbm)
    store(mixed_ref, mixed_hbm)
    for start in range(0, token_count, BLOCK):
        turned = jnp.transpose(spreads[pl.ds(start, BLOCK), :])
        spread_ref[:, start : start + BLOCK] = turned[:8]
    store(spread_ref, spread_hbm)
    for copy in stores:
        copy.wait()


def attend(lengths, table, hidden_in, gain, w_query, w_key, w_value):
    token_count, model = hidden_in.shape
    head_count = table.shape[0]
    inner = w_query.shape[0]
    width = inner // head_count
    low = jnp.bfloat16
    heads = pltpu.VMEM((head_count, token_count, width), low)
    weight = pltpu.VMEM((inner, model), low)
    results = (
        ((token_count, model), low),
        ((token_count, inner), low),
        ((token_count, inner), low),
        ((token_count, inner), low),
        ((token_count, inner), low),
        ((token_count * 3 // 2, 2 * width), low),
        ((8, token_count), jnp.float32),
    )
    return pl.pallas_call(
        attend_kernel,
        out_shape=tuple(
            (jax.ShapeDtypeStruct if index == 5 else pltpu.HBM)(*result)
            for index, result in enumerate(results)
        ),
        in_specs=[SCALARS, SCALARS, ANYWHERE, VECTORS] + [ANYWHERE] * 3,
        out_specs=(ANYWHERE,) * 7,
        scratch_shapes=[
            pltpu.VMEM((head_count, BLOCK, 4 * BLOCK), jnp.float32),
            heads,
            heads,
            heads,
            heads,
            pltpu.VMEM((2, 8, token_count), jnp.int32),
            pltpu.VMEM((token_count, BLOCK), jnp.float32),
            pltpu.VMEM((token_count, model), low),
            weight,
            weight,
            weight,
            *(pltpu.VMEM(*result) for result in results),
            pltpu.SemaphoreType.DMA((3 + token_count // (2 * BLOCK),)),
            pltpu.SemaphoreType.DMA((7,)),
        ],
        compiler_params=pltpu.CompilerParams(vmem_limit_bytes=28 * MIB),
        cost_estimate=QUICK,
        name="attend",
    )(
        *(in_main(value) for value in (lengths, table, hidden_in, gain)),
        *(in_main(value) for value in (w_query, w_key, w_value)),
    )


def attend_back_kernel(
    later_count,
    place_ref,
    lengths_ref,
    table_ref,
    q_hbm,
    k_hbm,
    v_hbm,
    grad_own_hbm,
    grad_far_hbm,
    spread_hbm,
    hidden_hbm,
    wq_hbm,
    wk_hbm,
    wv_hbm,
    norm_hbm,
    mixed_hbm,
    *refs,
):
    refs = refs[later_count:]
    dq_hbm, dk_hbm, dv_hbm, table_grad_hbm, hidden_near, weights_near = refs[:6]
    norm_near, mixed_near = refs[6:8]
    refs = refs[8:]
    tiles, heads_q, heads_k, heads_v, heads_g, probs, grads, sums_q, sums_k, sums_v = refs[:10]
    near, far, edges, lines_s, q_ref, k_ref, v_ref, grad_own_ref, grad_far_ref = refs[10:19]
    spread_ref, dq_ref, dk_ref, dv_ref, table_grad_ref, came, left = refs[19:]
    token_count = q_ref.shape[0]
    head_count, bucket_count = table_ref.shape
    width = q_ref.shape[1] // head_count
    chunk = 2 * BLOCK
    blocks = token_count // BLOCK
    loads = [
        pltpu.make_async_copy(source, target, came.at[index])
        for index, (source, target) in enumerate(
            (
                (q_hbm, q_ref),
                (k_hbm, k_ref),
                (v_hbm, v_ref),
                (grad_own_hbm, grad_own_ref),
                (grad_far_hbm, grad_far_ref),
                (spread_hbm, spread_ref),
                (hidden_hbm, hidden_near),
                (wq_hbm, weights_near.at[0]),
                (wk_hbm, weights_near.at[1]),
                (wv_hbm, weights_near.at[2]),
                (norm_hbm, norm_near),
                (mixed_hbm, mixed_near),
            )
        )
    ]
    for load in loads:
        load.start()
    stores = []

    def store(source, target):
        copy = pltpu.make_async_copy(source, target, left.at[len(stores)])
        copy.start()
        stores.append(copy)

    half = token_count // 2
    side = place_ref[0] % 2
    own_rows = pl.ds(pl.multiple_of(side * half, half), half)
    far_rows = pl.ds(pl.multiple_of((1 - side) * half, half), half)
    bias_tiles(table_ref, tiles, True)
    token = lax.broadcasted_iota(jnp.int32, (token_count, BLOCK - width), 0)
    lane = lax.broadcasted_iota(jnp.int32, (token_count, BLOCK - width), 1)
    marks = (token // BLOCK == lane).astype(jnp.float32).astype(jnp.bfloat16)
    for load in loads[:6]:
        load.wait()
    for head in range(head_count):
        cut = slice(head * width, (head + 1) * width)
        heads_q[head] = jnp.concatenate([q_ref[:, cut], marks], axis=1)
        heads_k[head] = k_ref[:, cut]
        heads_v[head] = v_ref[:, cut]
        heads_g[head, own_rows, :] = grad_own_ref[:, cut]
        heads_g[head, far_rows, :] = grad_far_ref[:, cut]
        lines_s[head] = jnp.broadcast_to(spread_ref[head : head + 1, :], (8, token_count))
    near[...] = jnp.zeros_like(near)
    far[...] = jnp.zeros_like(far)

    def score_back(scores, spread, grad_probs):
        weights = jnp.exp(scores - spread)
        delta = jnp.sum(weights * grad_probs, axis=0, keepdims=True)
        return weights, weights * (grad_probs - delta)

    @pl.when(lengths_ref[0] > lengths_ref.shape[0])
    def document():
        def one_head(head, carry):
            keys, values = heads_k[head], heads_v[head]
            past = table_ref[head, bucket_count // 2 - 1]
            future = table_ref[head, bucket_count - 1]
            for start in range(0, token_count, chunk):
                rows = pl.ds(start, chunk)
                raw = row_dot(keys, heads_q[head, rows, :width])
                lines = []
                for block in range(blocks):
                    line = []
                    for part in range(chunk // BLOCK):
                        away = block - start // BLOCK - part
                        piece = raw[
                            block * BLOCK : (block + 1) * BLOCK, part * BLOCK : (part + 1) * BLOCK
                        ]
                        if abs(away) <= 1:
                            first = (2 - away) * BLOCK
                            piece = piece + tiles[head, :, first : first + BLOCK]
                        else:
                            piece = piece + (past if away < 0 else future)
                        line.append(piece)
                    lines.append(jnp.concatenate(line, axis=1))
                scores = jnp.concatenate(lines, axis=0)
                grad_probs = row_dot(values, heads_g[head, rows, :])
                weights, score_grad = score_back(
                    scores, lines_s[head, :1, rows], grad_probs
                )
                probs[:, rows] = weights.astype(jnp.bfloat16)
                grads[:, rows] = score_grad.astype(jnp.bfloat16)
                for block in range(blocks):
                    for part in range(chunk // BLOCK):
                        away = block - start // BLOCK - part
                        if abs(away) <= 1:
                            first = (2 - away) * BLOCK
                            near[head, :, first : first + BLOCK] += score_grad[
                                block * BLOCK : (block + 1) * BLOCK,
                                part * BLOCK : (part + 1) * BLOCK,
                            ]
            sums_v[head] = plain_dot(probs[...], heads_g[head])
            key_sums = plain_dot(grads[...], heads_q[head])
            sums_k[head] = key_sums[:, :width]
            sums_q[head] = col_dot(grads[...], keys)
            for block in range(blocks):
                line = jnp.sum(key_sums[block * BLOCK : (block + 1) * BLOCK], axis=0, keepdims=True)
                far[head, block : block + 1, :] = line
            return carry

        lax.fori_loop(0, head_count, one_head, 0)

    @pl.when(lengths_ref[0] <= lengths_ref.shape[0])
    def queries():
        position = lax.broadcasted_iota(jnp.int32, (8, token_count), 1)
        low, high = slot_edges(lengths_ref, position)
        edges[0] = low
        edges[1] = high
        sums_k[...] = jnp.zeros_like(sums_k)
        sums_v[...] = jnp.zeros_like(sums_v)

        def one_head(head, carry):
            for block in range(blocks):
                first = max(block - 1, 0)
                last = min(block + 1, blocks - 1) + 1
                rows = pl.ds(block * BLOCK, BLOCK)
                window = pl.ds(first * BLOCK, (last - first) * BLOCK)
                scores = row_dot(heads_k[head, window, :], heads_q[head, rows, :width])
                lines = []
                for other in range(first, last):
                    begin = (2 - (other - block)) * BLOCK
                    lines.append(tiles[head, :, begin : begin + BLOCK])
                scores = scores + jnp.concatenate(lines, axis=0)
                token = first * BLOCK + lax.broadcasted_iota(jnp.int32, scores.shape, 0)
                inside = (token >= edges[0, :1, rows]) & (token < edges[1, :1, rows])
                grad_probs = row_dot(heads_v[head, window, :], heads_g[head, rows, :])
                weights, score_grad = score_back(
                    jnp.where(inside, scores, -1e30), lines_s[head, :1, rows], grad_probs
                )
                for other in range(first, last):
                    begin = (2 - (other - block)) * BLOCK
                    near[head, :, begin : begin + BLOCK] += score_grad[
                        (other - first) * BLOCK : (other - first + 1) * BLOCK
                    ]
                grad_low = score_grad.astype(jnp.bfloat16)
                sums_v[head, window, :] += plain_dot(
                    weights.astype(jnp.bfloat16), heads_g[head, rows, :]
                )
                sums_k[head, window, :] += plain_dot(grad_low, heads_q[head, rows, :width])
                sums_q[head, rows, :] = col_dot(grad_low, heads_k[head, window, :])
            return carry

        lax.fori_loop(0, head_count, one_head, 0)

    for sums, out in ((sums_q, dq_ref), (sums_k, dk_ref), (sums_v, dv_ref)):
        out[...] = jnp.concatenate(
            [sums[head].astype(jnp.bfloat16) for head in range(head_count)], axis=1
        )
    for source, target in ((dq_ref, dq_hbm), (dk_ref, dk_hbm), (dv_ref, dv_hbm)):
        store(source, target)
    lines = []
    for head in range(head_count):
        lines.append(unrolled_sum(near[head]))
    lines.append(jnp.zeros((8 - head_count, 4 * BLOCK), jnp.float32))
    by_offset = jnp.concatenate(lines, axis=0)
    offset = 2 * BLOCK - lax.broadcasted_iota(jnp.int32, (4 * BLOCK, BLOCK), 0)
    place = lax.broadcasted_iota(jnp.int32, (4 * BLOCK, BLOCK), 1)
    onehot = (offset_buckets(offset) == place).astype(jnp.float32).astype(jnp.bfloat16)
    high, rest = two_terms(by_offset)
    table_grad = plain_dot(high, onehot) + plain_dot(rest, onehot)
    row = lax.broadcasted_iota(jnp.int32, (blocks, BLOCK), 0)
    column = lax.broadcasted_iota(jnp.int32, (blocks, BLOCK), 1) - width
    real = (column >= 0) & (column < blocks)
    is_past = real & (row - column <= -2)
    is_future = real & (row - column >= 2)
    lane = lax.broadcasted_iota(jnp.int32, (1, BLOCK), 1)
    lines = []
    for head in range(head_count):
        past = jnp.sum(jnp.where(is_past, far[head], 0.0), keepdims=True)
        future = jnp.sum(jnp.where(is_future, far[head], 0.0), keepdims=True)
        lines.append(
            table_grad[head : head + 1]
            + jnp.where(lane == bucket_count // 2 - 1, past, 0.0)
            + jnp.where(lane == bucket_count - 1, future, 0.0)
        )
    lines.append(jnp.zeros((8 - head_count, BLOCK), jnp.float32))
    table_grad_ref[...] = jnp.concatenate(lines, axis=0)
    store(table_grad_ref, table_grad_hbm)
    for copy in (*stores, *loads[6:]):
        copy.wait()


def attend_back(
    place, lengths, table, query, key, value, grads, spread, hidden_in, weights, norm, mixed, later
):
    token_count, inner = query.shape
    model = hidden_in.shape[1]
    head_count = table.shape[0]
    width = inner // head_count
    low, full = jnp.bfloat16, jnp.float32
    heads = pltpu.VMEM((head_count, token_count, width), low)
    sums = pltpu.VMEM((head_count, token_count, width), full)
    square = pltpu.VMEM((token_count, token_count), low)
    tile = pltpu.VMEM((head_count, BLOCK, 4 * BLOCK), full)
    flat = pltpu.VMEM((token_count, inner), low)
    half = pltpu.VMEM((token_count // 2, inner), low)
    return pl.pallas_call(
        functools.partial(attend_back_kernel, len(later)),
        out_shape=(
            shape_of(token_count, inner, low),
            shape_of(token_count, inner, low),
            shape_of(token_count, inner, low),
            shape_of(8, BLOCK, full),
            near_shape(token_count, model, low),
            pltpu.VMEM((3, inner, model), low),
            near_shape(token_count, model, low),
            near_shape(token_count, inner, low),
        ),
        in_specs=[SCALARS] * 3 + [ANYWHERE] * (12 + len(later)),
        out_specs=(ANYWHERE,) * 8,
        scratch_shapes=[
            tile,
            pltpu.VMEM((head_count, token_count, BLOCK), low),
            heads,
            heads,
            heads,
            square,
            square,
            sums,
            sums,
            sums,
            tile,
            pltpu.VMEM((head_count, token_count // BLOCK, BLOCK), full),
            pltpu.VMEM((2, 8, token_count), jnp.int32),
            pltpu.VMEM((head_count, 8, token_count), full),
            flat,
            flat,
            flat,
            half,
            half,
            pltpu.VMEM((8, token_count), full),
            flat,
            flat,
            flat,
            pltpu.VMEM((8, BLOCK), full),
            pltpu.SemaphoreType.DMA((12,)),
            pltpu.SemaphoreType.DMA((4,)),
        ],
        compiler_params=pltpu.CompilerParams(vmem_limit_bytes=34 * MIB),
        cost_estimate=pl.CostEstimate(
            flops=12 * 2**30, bytes_accessed=2**16, transcendentals=0
        ),
        name="attend_back",
    )(
        *(in_main(value) for value in (place, lengths, table, query, key, value)),
        *grads,
        *(in_main(value) for value in (spread, hidden_in, *weights, norm, mixed)),
        *later,
    )


def parts_kernel(flip, later_count, place_ref, dq_ref, dk_ref, dv_ref, hidden_ref, w_ref, *refs):
    part_ref, one_ref = refs[later_count:]
    half = (place_ref[0] % 2) ^ flip
    one = jnp.zeros(one_ref.shape, jnp.float32)
    for _, own, whole in chunk_rows(part_ref.shape[0], half):
        part = plain_dot(dq_ref[whole, :], w_ref[0])
        part = part + plain_dot(dk_ref[whole, :], w_ref[1])
        part = part + plain_dot(dv_ref[whole, :], w_ref[2])
        part_ref[own, :] = part.astype(jnp.bfloat16)
        values = hidden_ref[whole, :].astype(jnp.float32)
        one = one + jnp.sum(part * values * norm_scale(values), axis=0, keepdims=True)
    one_ref[...] = one


def norm1_parts(flip, place, grads, hidden, weights, later):
    token_count, model = hidden.shape
    return pl.pallas_call(
        functools.partial(parts_kernel, flip, len(later)),
        out_shape=(
            shape_of(token_count // 2, model, jnp.bfloat16),
            shape_of(1, model, jnp.float32),
        ),
        in_specs=[SCALARS] + [VECTORS] * 5 + [ANYWHERE] * len(later),
        out_specs=(VECTORS, VECTORS),
        compiler_params=pltpu.CompilerParams(vmem_limit_bytes=20 * MIB),
        cost_estimate=pl.CostEstimate(
            flops=3 * weights.size * token_count // 3,
            bytes_accessed=4 * hidden.size,
            transcendentals=0,
        ),
        name="norm1_parts",
    )(in_main(place), *grads, hidden, weights, *later)


def split_gelu(value):
    square = value * value
    inner = GELU * value * (1.0 + CUBE * square)
    turn = jnp.tanh(inner)
    half = 0.5 * (1.0 + turn)
    slope = half + 0.5 * value * (1.0 - turn * turn) * GELU * (1.0 + 3.0 * CUBE * square)
    return half * value, slope


def norm_scale(values):
    return lax.rsqrt(jnp.mean(values * values, axis=1, keepdims=True) + EPSILON)


def norm_back(values, gain, grad):
    scale = norm_scale(values)
    scaled = grad * gain
    share = jnp.mean(scaled * values, axis=1, keepdims=True)
    back = scale * scaled - (scale * scale * scale) * values * share
    return back, jnp.sum(grad * values * scale, axis=0, keepdims=True)


def slot_lines(lengths_ref, shape, axis):
    slot = lax.broadcasted_iota(jnp.int32, shape, axis)
    starts = jnp.zeros(shape, jnp.int32)
    ends = jnp.zeros(shape, jnp.int32)
    start = jnp.int32(0)
    for index in range(lengths_ref.shape[0]):
        end = start + lengths_ref[index]
        starts = jnp.where(slot == index, start, starts)
        ends = jnp.where(slot == index, end, ends)
        start = end
    return starts, ends


def as_low(mask):
    return mask.astype(jnp.float32).astype(jnp.bfloat16)


def row_call(kernel, flip, inputs, outputs, scratch, place, aliases, flops):
    specs = {"scalar": SCALARS, "line": VECTORS, "near": VECTORS, "any": ANYWHERE}
    return pl.pallas_call(
        functools.partial(kernel, flip),
        out_shape=tuple(shape for _, shape in outputs),
        in_specs=[SCALARS] + [specs[kind] for kind, _ in inputs],
        out_specs=tuple(specs[kind] for kind, _ in outputs),
        scratch_shapes=scratch,
        input_output_aliases=aliases,
        compiler_params=pltpu.CompilerParams(vmem_limit_bytes=24 * MIB),
        cost_estimate=pl.CostEstimate(flops=flops, bytes_accessed=6 * 2**20, transcendentals=0),
        name=kernel.__name__,
    )(
        in_main(place),
        *(in_main(value) if kind in ("line", "scalar") else value for kind, value in inputs),
    )


def near_shape(rows, columns, kind):
    return pltpu.VMEM((rows, columns), kind)


def main_shape(rows, columns, kind):
    return pltpu.HBM((rows, columns), kind)


def shape_of(rows, columns, kind):
    return jax.ShapeDtypeStruct((rows, columns), kind)


def chunk_rows(rows, half):
    chunk = rows // 2
    for step in range(2):
        whole = pl.ds(pl.multiple_of(half * rows + step * chunk, chunk), chunk)
        yield step, pl.ds(step * chunk, chunk), whole


def middle_kernel(
    flip,
    place_ref,
    hidden_ref,
    wide0_ref,
    wide1_ref,
    wide2_ref,
    wide3_ref,
    rest0_ref,
    rest1_ref,
    rest2_ref,
    rest3_ref,
    weight0_ref,
    weight1_ref,
    weight2_ref,
    weight3_ref,
    gain_ref,
    w_in_ref,
    w_ffout_ref,
    after_ref,
    norm_ref,
    act_ref,
    slope_ref,
    part_ref,
    pieces,
    weights,
):
    narrow = place_ref[0]

    @pl.when(pl.program_id(0) == 0)
    def first():
        for index, ref in enumerate((weight0_ref, weight1_ref, weight2_ref, weight3_ref)):
            weights[narrow ^ index] = ref[...]

    half = (narrow % 2) ^ flip
    inner = pieces.shape[2]
    mains = (wide0_ref, wide1_ref, wide2_ref, wide3_ref)
    rests = (rest0_ref, rest1_ref, rest2_ref, rest3_ref)
    for index in range(4):
        rest = rests[index][...]
        width = rest.shape[1] // 2
        tail = jnp.where(half == 0, rest[:, :width], rest[:, width:])
        pieces[narrow ^ index] = jnp.concatenate([mains[index][...], tail], axis=1)
    total = plain_dot(pieces[0], weights[0])
    for index in range(1, 4):
        total = total + plain_dot(pieces[index], weights[index])
    after = hidden_ref[...].astype(jnp.float32) + total
    after_ref[...] = after
    norm = (after * norm_scale(after) * gain_ref[...].reshape(1, -1)).astype(jnp.bfloat16)
    norm_ref[...] = norm
    act, slope = split_gelu(plain_dot(norm, w_in_ref[...]))
    act_low = act.astype(jnp.bfloat16)
    act_ref[...] = act_low
    slope_ref[...] = slope.astype(jnp.bfloat16)
    part_ref[...] = plain_dot(act_low, w_ffout_ref[...]).astype(jnp.bfloat16)


def half_block(flip):
    def place(step, place_ref):
        return (((place_ref[0] % 2) ^ flip) * 2 + step, 0)

    return place


def own_block(step, place_ref):
    return (step, 0)


def whole_block(step, place_ref):
    return (0, 0)


def grid_call(kernel, flip, inputs, outputs, scratch, place, aliases, flops):
    kinds = {"half": half_block(flip), "own": own_block, "all": whole_block}

    def spec(item):
        kind, shape = item
        if kind == "scalar":
            return SCALARS
        if kind == "any":
            return pl.BlockSpec(memory_space=pl.ANY)
        if kind == "rest":
            return pl.BlockSpec(shape, lambda step, place_ref: (4 + step, 0))
        if kind == "line":
            return pl.BlockSpec(shape, lambda step, place_ref: (0,))
        return pl.BlockSpec(shape, kinds[kind])

    return pl.pallas_call(
        functools.partial(kernel, flip),
        out_shape=tuple(shape for _, _, shape in outputs),
        grid_spec=pltpu.PrefetchScalarGridSpec(
            num_scalar_prefetch=1,
            grid=(2,),
            in_specs=[spec((kind, shape)) for kind, shape, _ in inputs],
            out_specs=tuple(spec((kind, shape)) for kind, shape, _ in outputs),
            scratch_shapes=scratch,
        ),
        input_output_aliases=aliases,
        compiler_params=pltpu.CompilerParams(
            vmem_limit_bytes=16 * MIB, dimension_semantics=("arbitrary",)
        ),
        cost_estimate=pl.CostEstimate(flops=flops, bytes_accessed=6 * 2**20, transcendentals=0),
        name=kernel.__name__,
    )(
        in_main(place),
        *(in_main(value) if kind in ("line", "scalar") else value for kind, _, value in inputs),
    )


def middle(flip, place, hidden_in, packed, w_outs, gain, w_in, w_ffout):
    token_count, model = hidden_in.shape
    hidden_count = w_in.shape[1]
    rows, chunk = token_count // 2, token_count // 4
    inner = w_outs[0].shape[0]
    low = jnp.bfloat16
    inputs = [("half", (chunk, model), hidden_in)]
    inputs += [("half", (chunk, 128), piece) for piece in packed]
    inputs += [("rest", (chunk, 128), piece) for piece in packed]
    inputs += [
        *(("all", weight.shape, weight) for weight in w_outs),
        ("line", (model,), gain),
        ("all", w_in.shape, w_in),
        ("all", w_ffout.shape, w_ffout),
    ]
    outputs = [
        ("own", (chunk, model), shape_of(rows, model, jnp.float32)),
        ("own", (chunk, model), shape_of(rows, model, low)),
        ("own", (chunk, hidden_count), shape_of(rows, hidden_count, low)),
        ("own", (chunk, hidden_count), shape_of(rows, hidden_count, low)),
        ("own", (chunk, model), shape_of(rows, model, low)),
    ]
    scratch = [pltpu.VMEM((4, chunk, inner), low), pltpu.VMEM((4, inner, model), low)]
    flops = 2 * rows * model * (model + 2 * hidden_count)
    return grid_call(middle_kernel, flip, inputs, outputs, scratch, place, {}, flops)


def pool_kernel(flip, place_ref, lengths_ref, after_ref, total_ref, gain_ref, *refs):
    half = (place_ref[0] % 2) ^ flip
    rows, model = after_ref.shape
    chunk = rows // 2
    slots = lengths_ref.shape[0]
    if flip == 0:
        out_ref, pooled_ref = refs
        pooled = jnp.zeros(pooled_ref.shape, jnp.float32)
    else:
        positive_ref, partial_ref, out_ref, block_ref, rows_s = refs
        pooled = partial_ref[...]
    starts, ends = slot_lines(lengths_ref, (slots, 1), 0)
    for step, own, _ in chunk_rows(rows, half):
        value = after_ref[own, :] + total_ref[own, :].astype(jnp.float32)
        out_ref[own, :] = value
        high, rest = two_terms(value * norm_scale(value) * gain_ref[...].reshape(1, -1))
        token = half * rows + step * chunk
        token = token + lax.broadcasted_iota(jnp.int32, (slots, chunk), 1)
        member = as_low((token >= starts) & (token < ends))
        pooled = pooled + (plain_dot(member, high) + plain_dot(member, rest))
    if flip == 0:
        pooled_ref[...] = pooled
        return
    count = jnp.maximum(ends - starts, 1).astype(jnp.float32)
    slot = lax.broadcasted_iota(jnp.int32, (slots, 128), 0)
    lane = lax.broadcasted_iota(jnp.int32, (slots, 128), 1)
    partner = jnp.zeros((slots, 128), jnp.int32)
    for index in range(slots):
        partner = jnp.where(slot == index, positive_ref[index], partner)
    used = jnp.where(ends > starts, 1, 0)
    facts = jnp.where(lane == 0, used, jnp.where(lane == 1, partner >> 7, partner & 127))
    rows_s[:, :model] = pooled / count
    rows_s[:, model:] = facts.astype(jnp.float32)
    part = slots // 2
    own = rows_s[pl.ds(pl.multiple_of((place_ref[0] % 2) * part, part), part), :]
    block_ref[...] = own.astype(jnp.bfloat16)


def pool(flip, place, lengths, after, total, gain, more):
    rows, model = after.shape
    slots = lengths.shape[0]
    inputs = [("scalar", lengths), ("near", after), ("near", total), ("line", gain)]
    outputs = [("near", shape_of(rows, model, jnp.float32))]
    scratch = []
    if flip == 0:
        outputs.append(("near", shape_of(slots, model, jnp.float32)))
    else:
        positive, partial = more
        inputs += [("scalar", positive), ("near", partial)]
        outputs.append(("near", shape_of(slots // 2, model + 128, jnp.bfloat16)))
        scratch = [pltpu.VMEM((slots, model + 128), jnp.float32)]
    return row_call(pool_kernel, flip, inputs, outputs, scratch, place, {}, 2**24)


def assemble_kernel(place_ref, own_ref, far_ref, later_ref, out_hbm, token_ref, sems):
    rows = own_ref.shape[0]
    token_ref[...] = jnp.zeros(token_ref.shape, jnp.float32)
    copies = []
    for flip, ref in enumerate((own_ref, far_ref)):
        half = (place_ref[0] % 2) ^ flip
        target = out_hbm.at[pl.ds(pl.multiple_of(half * rows, rows), rows), :]
        copies.append(pltpu.make_async_copy(ref, target, sems.at[flip]))
    for copy in copies:
        copy.start()
    for copy in copies:
        copy.wait()


def assemble(place, own, far, later):
    rows, model = own.shape
    return pl.pallas_call(
        assemble_kernel,
        out_shape=(main_shape(2 * rows, model, own.dtype), shape_of(8, 128, jnp.float32)),
        in_specs=[SCALARS] + [ANYWHERE] * 3,
        out_specs=(ANYWHERE, VECTORS),
        scratch_shapes=[pltpu.SemaphoreType.DMA((2,))],
        compiler_params=pltpu.CompilerParams(vmem_limit_bytes=4 * MIB),
        cost_estimate=QUICK,
        name="assemble",
    )(in_main(place), own, far, later)


def contrast_kernel(groups, place_ref, *refs):
    mine, other = refs[:groups], refs[groups : 2 * groups]
    w_proj_ref, bias_ref, loss_ref, pooled_hbm, low_hbm, bias_grad_ref = refs[
        2 * groups : 2 * groups + 6
    ]
    slot_grad_ref, pooled_ref, low_ref, sems, embeds, units, facts, spreads, losses = refs[
        2 * groups + 6 :
    ]
    narrow, wide = place_ref[0], place_ref[1]
    part = mine[0].shape[0] // 2
    model = w_proj_ref.shape[0]
    slots = 2 * part
    count = 2 * groups * slots
    block = min(count, 256)
    side = narrow % 2
    for refs_at, at in ((mine, side), (other, 1 - side)):
        for index, ref in enumerate(refs_at):
            for odd in range(2):
                pack = wide ^ (2 * index + odd)
                rows = pl.ds(pl.multiple_of(pack * slots + at * part, part), part)
                pooled_ref[rows, :] = ref[odd * part : (odd + 1) * part, :model]
                facts[rows, :] = ref[odd * part : (odd + 1) * part, model:]
    for start in range(0, count, block):
        rows = pl.ds(start, block)
        embed = plain_dot(pooled_ref[rows, :], w_proj_ref[...]) + bias_ref[...].reshape(1, -1)
        embeds[rows, :] = embed
        scale = lax.rsqrt(jnp.sum(embed * embed, axis=1, keepdims=True) + EPSILON)
        units[rows, :] = (embed * scale).astype(jnp.bfloat16)
    pick_row = lax.broadcasted_iota(jnp.int32, (8, 128), 0)
    pick_lane = lax.broadcasted_iota(jnp.int32, (8, 128), 1)
    pick = as_low(pick_row == pick_lane)
    lines = row_dot(pick, facts[...])
    used_line = lines[:1] > 0.5
    partner_line = (lines[1:2] * 128.0 + lines[2:3]).astype(jnp.int32)
    column = lax.broadcasted_iota(jnp.int32, (block, count), 1)
    row = lax.broadcasted_iota(jnp.int32, (block, count), 0)

    def columns_of(rows):
        values = facts[rows, :].astype(jnp.float32)
        used = values[:, :1] > 0.5
        partner = (values[:, 1:2] * 128.0 + values[:, 2:3]).astype(jnp.int32)
        return used, partner

    for start in range(0, count, block):
        rows = pl.ds(start, block)
        sims = CONTRAST * row_dot(units[rows, :], units[...])
        used, partner = columns_of(rows)
        usable = used_line & (column != row + start)
        masked = jnp.where(usable, sims, -1e30)
        top = jnp.max(masked, axis=1, keepdims=True)
        total = jnp.sum(jnp.exp(masked - top), axis=1, keepdims=True)
        spread = top + jnp.log(total)
        score = jnp.sum(jnp.where(column == partner, sims, 0.0), axis=1, keepdims=True)
        losses[rows, :] = jnp.where(used, spread - score, 0.0)
        turned = jnp.transpose(jnp.broadcast_to(spread, (block, 128)))
        spreads[:, start : start + block] = turned[:8]
    loss = losses[pl.ds(pl.multiple_of(wide * slots, slots), slots), :]
    loss = jnp.transpose(jnp.broadcast_to(loss, (slots, 128)))
    loss_ref[...] = loss[:1, :].reshape(slots)
    bias_grad = jnp.zeros((1, model), jnp.float32)
    for start in range(0, count, block):
        rows = pl.ds(start, block)
        sims = CONTRAST * row_dot(units[rows, :], units[...])
        used, partner = columns_of(rows)
        differ = column != row + start
        spread = jnp.transpose(jnp.broadcast_to(spreads[:1, start : start + block], (128, block)))
        masked = jnp.where(used_line & differ, sims, -1e30)
        ahead = jnp.exp(masked - spread[:, :1]) - jnp.where(column == partner, 1.0, 0.0)
        masked = jnp.where(used & differ, sims, -1e30)
        behind = jnp.exp(masked - spreads[:1, :]) - jnp.where(
            row + start == partner_line, 1.0, 0.0
        )
        both = jnp.where(used, ahead, 0.0) + jnp.where(used_line, behind, 0.0)
        high, rest = two_terms(both)
        grad = CONTRAST * (plain_dot(high, units[...]) + plain_dot(rest, units[...]))
        embed = embeds[rows, :]
        scale = lax.rsqrt(jnp.sum(embed * embed, axis=1, keepdims=True) + EPSILON)
        share = jnp.sum(embed * grad, axis=1, keepdims=True)
        back = scale * grad - (scale * scale * scale) * embed * share
        back_low = back.astype(jnp.bfloat16)
        low_ref[rows, :] = back_low
        bias_grad = bias_grad + jnp.sum(back_low.astype(jnp.float32), axis=0, keepdims=True)
    bias_grad_ref[...] = bias_grad.reshape(model)
    own = low_ref[pl.ds(pl.multiple_of(wide * slots, slots), slots), :]
    stores = [
        pltpu.make_async_copy(pooled_ref, pooled_hbm, sems.at[0]),
        pltpu.make_async_copy(low_ref, low_hbm, sems.at[1]),
    ]
    for store in stores:
        store.start()
    slot_grad_ref[...] = row_dot(own, w_proj_ref[...])
    for store in stores:
        store.wait()


def gathered_blocks(block):
    pair = jnp.concatenate([block, exchange(block, "wide", 1)], axis=0)
    mine = [pair]
    for mask in range(2, lax.axis_size("wide"), 2):
        mine.append(exchange(pair, "wide", mask))
    return (*mine, *(exchange(blocks, "narrow", 1) for blocks in mine))


def contrast(place, block, w_proj, proj_bias):
    parts = gathered_blocks(block)
    part = block.shape[0]
    model = w_proj.shape[0]
    count = len(parts) * 2 * part
    low = jnp.bfloat16
    return pl.pallas_call(
        functools.partial(contrast_kernel, len(parts) // 2),
        out_shape=(
            jax.ShapeDtypeStruct((2 * part,), jnp.float32),
            main_shape(count, model, low),
            main_shape(count, model, low),
            jax.ShapeDtypeStruct((model,), jnp.float32),
            shape_of(2 * part, model, jnp.float32),
        ),
        in_specs=[SCALARS] + [VECTORS] * (len(parts) + 2),
        out_specs=(VECTORS, ANYWHERE, ANYWHERE, VECTORS, VECTORS),
        scratch_shapes=[
            pltpu.VMEM((count, model), low),
            pltpu.VMEM((count, model), low),
            pltpu.SemaphoreType.DMA((2,)),
            pltpu.VMEM((count, model), jnp.float32),
            pltpu.VMEM((count, model), low),
            pltpu.VMEM((count, 128), low),
            pltpu.VMEM((8, count), jnp.float32),
            pltpu.VMEM((count, 1), jnp.float32),
        ],
        compiler_params=pltpu.CompilerParams(vmem_limit_bytes=(12 if count <= 256 else 56) * MIB),
        cost_estimate=pl.CostEstimate(
            flops=2 * count * model * (model + 4 * count),
            bytes_accessed=4 * model * model,
            transcendentals=3 * count * count,
        ),
        name="contrast",
    )(in_main(place), *parts, w_proj, in_main(proj_bias))


def turn_kernel(
    flip,
    place_ref,
    lengths_ref,
    out_ref,
    slot_grad_ref,
    slope_ref,
    gain_ref,
    w_ffout_ref,
    w_in_ref,
    grad_ref,
    low_ref,
    pre_ref,
    part_ref,
    gain_grad_ref,
):
    half = (place_ref[0] % 2) ^ flip
    rows = out_ref.shape[0]
    chunk = rows // 2
    slots = lengths_ref.shape[0]
    starts, ends = slot_lines(lengths_ref, (slots, 1), 0)
    count = jnp.maximum(ends - starts, 1).astype(jnp.float32)
    high, rest = two_terms(slot_grad_ref[...] / count)
    starts, ends = slot_lines(lengths_ref, (1, slots), 1)
    total = jnp.zeros(gain_grad_ref.shape, jnp.float32)
    for step, own, _ in chunk_rows(rows, half):
        token = half * rows + step * chunk
        token = token + lax.broadcasted_iota(jnp.int32, (chunk, slots), 0)
        member = as_low((token >= starts) & (token < ends))
        final_grad = plain_dot(member, high) + plain_dot(member, rest)
        gain = gain_ref[...].reshape(1, -1)
        grad, gain_grad = norm_back(out_ref[own, :], gain, final_grad)
        total = total + gain_grad
        grad_ref[own, :] = grad
        low = grad.astype(jnp.bfloat16)
        low_ref[own, :] = low
        pre = row_dot(low, w_ffout_ref[...]) * slope_ref[own, :].astype(jnp.float32)
        pre = pre.astype(jnp.bfloat16)
        pre_ref[own, :] = pre
        part_ref[own, :] = row_dot(pre, w_in_ref[...]).astype(jnp.bfloat16)
    gain_grad_ref[...] = total


def turn(flip, place, lengths, layer_out, slot_grad, slope, gain, w_ffout, w_in):
    rows, hidden_count = slope.shape
    model = layer_out.shape[1]
    low = jnp.bfloat16
    inputs = [("scalar", lengths), ("near", layer_out), ("near", slot_grad), ("near", slope)]
    inputs += [("line", gain), ("near", w_ffout), ("near", w_in)]
    outputs = [
        ("near", shape_of(rows, model, jnp.float32)),
        ("near", shape_of(rows, model, low)),
        ("near", shape_of(rows, hidden_count, low)),
        ("near", shape_of(rows, model, low)),
        ("near", shape_of(1, model, jnp.float32)),
    ]
    flops = 4 * rows * model * hidden_count
    return row_call(turn_kernel, flip, inputs, outputs, [], place, {}, flops)


def join_kernel(
    flip,
    place_ref,
    out_grad_ref,
    after_ref,
    total_ref,
    gain_ref,
    w_out_ref,
    mid_ref,
    low_ref,
    mixed_grad_ref,
    gain_grad_ref,
):
    total = jnp.zeros(gain_grad_ref.shape, jnp.float32)
    gain = gain_ref[...].reshape(1, -1)
    for _, own, _ in chunk_rows(after_ref.shape[0], 0):
        back, gain_grad = norm_back(
            after_ref[own, :], gain, total_ref[own, :].astype(jnp.float32)
        )
        total = total + gain_grad
        mid = out_grad_ref[own, :] + back
        mid_ref[own, :] = mid
        low = mid.astype(jnp.bfloat16)
        low_ref[own, :] = low
        mixed_grad_ref[own, :] = row_dot(low, w_out_ref[...]).astype(jnp.bfloat16)
    gain_grad_ref[...] = total


def join(flip, place, out_grad, after, total, gain, w_out):
    rows, model = out_grad.shape
    inner = w_out.shape[0]
    low = jnp.bfloat16
    inputs = [("near", out_grad), ("near", after), ("near", total)]
    inputs += [("line", gain), ("near", w_out)]
    outputs = [
        ("near", shape_of(rows, model, jnp.float32)),
        ("near", shape_of(rows, model, low)),
        ("near", shape_of(rows, inner, low)),
        ("near", shape_of(1, model, jnp.float32)),
    ]
    flops = 2 * rows * model * inner
    return row_call(join_kernel, flip, inputs, outputs, [], place, {}, flops)


def last_kernel(flip, place_ref, mid_ref, hidden_ref, total_ref, gain_ref, *refs):
    out_hbm, token_ref, rows_s, sems = refs[-4:]
    half = (place_ref[0] % 2) ^ flip
    gain = gain_ref[...].reshape(1, -1)
    copies = []
    for step, own, whole in chunk_rows(mid_ref.shape[0], half):
        back, _ = norm_back(
            hidden_ref[whole, :].astype(jnp.float32), gain, total_ref[own, :].astype(jnp.float32)
        )
        rows_s[own, :] = mid_ref[own, :] + back
        copy = pltpu.make_async_copy(rows_s.at[own, :], out_hbm.at[whole, :], sems.at[step])
        copy.start()
        copies.append(copy)
    token_ref[...] = jnp.zeros(token_ref.shape, jnp.float32)
    for copy in copies:
        copy.wait()


def last(flip, place, mid, hidden_in, total, gain, given):
    rows, model = mid.shape
    inputs = [("near", mid), ("near", hidden_in), ("near", total), ("line", gain)]
    inputs.append(("any", given))
    aliases = {5: 0} if flip == 1 else {}
    outputs = [
        ("any", main_shape(2 * rows, model, jnp.float32)),
        ("near", shape_of(8, 128, jnp.float32)),
    ]
    scratch = [pltpu.VMEM((rows, model), jnp.float32), pltpu.SemaphoreType.DMA((2,))]
    return row_call(last_kernel, flip, inputs, outputs, scratch, place, aliases, 2**22)


def sum_kernel(count, *refs):
    refs[-1][...] = arrived_sum(refs[:count])


def summed(blocks, later):
    return pl.pallas_call(
        functools.partial(sum_kernel, len(blocks)),
        out_shape=jax.ShapeDtypeStruct(blocks[0].shape, jnp.float32),
        in_specs=[VECTORS] * len(blocks) + [ANYWHERE],
        out_specs=VECTORS,
        compiler_params=pltpu.CompilerParams(vmem_limit_bytes=12 * MIB),
        cost_estimate=QUICK,
        name="summed",
    )(*blocks, later)


def pair_grads_kernel(place_ref, *refs):
    lefts, rights = refs[0:2], refs[2:4]
    value = col_dot(lefts[0][...], rights[0][...]) + col_dot(lefts[1][...], rights[1][...])
    split_pairs(value, place_ref[1] % 2, refs[5], refs[6])


def split_pairs(value, parity, keep_ref, send_ref):
    pairs = keep_ref.shape[0]
    rows = value.shape[0] // (2 * pairs)
    for pair in range(pairs):
        first = value[2 * pair * rows : (2 * pair + 1) * rows].astype(jnp.bfloat16)
        second = value[(2 * pair + 1) * rows : (2 * pair + 2) * rows].astype(jnp.bfloat16)
        keep_ref[pair, :rows, :] = jnp.where(parity == 0, first, second)
        send_ref[pair, :rows, :] = jnp.where(parity == 0, second, first)


def pair_grads(place, lefts, rights, later, pairs):
    rows, model = lefts[0].shape
    width = rights[0].shape[1]
    piece = jax.ShapeDtypeStruct((pairs, model // (2 * pairs), width), jnp.bfloat16)
    return pl.pallas_call(
        pair_grads_kernel,
        out_shape=(piece, piece),
        in_specs=[SCALARS] + [VECTORS] * 4 + [ANYWHERE],
        out_specs=(VECTORS, VECTORS),
        compiler_params=pltpu.CompilerParams(vmem_limit_bytes=16 * MIB),
        cost_estimate=pl.CostEstimate(
            flops=4 * rows * model * width, bytes_accessed=5 * rows * model, transcendentals=0
        ),
        name="pair_grads",
    )(in_main(place), *lefts, *rights, later)


def add_kernel(left_ref, right_ref, *refs):
    refs[-1][...] = add_low(left_ref[...], right_ref[...])


def add_after(left, right, *later):
    return pl.pallas_call(
        add_kernel,
        out_shape=jax.ShapeDtypeStruct(left.shape, jnp.bfloat16),
        in_specs=[VECTORS, VECTORS] + [ANYWHERE] * len(later),
        out_specs=VECTORS,
        compiler_params=pltpu.CompilerParams(vmem_limit_bytes=12 * MIB),
        cost_estimate=pl.CostEstimate(
            flops=left.size, bytes_accessed=6 * left.size, transcendentals=0
        ),
        name="add_after",
    )(left, right, *later)


def copy_kernel(source_ref, later_ref, out_ref):
    out_ref[...] = source_ref[...]


def copied(value, later):
    return pl.pallas_call(
        copy_kernel,
        out_shape=jax.ShapeDtypeStruct(value.shape, value.dtype),
        in_specs=[VECTORS, ANYWHERE],
        out_specs=VECTORS,
        compiler_params=pltpu.CompilerParams(vmem_limit_bytes=12 * MIB),
        cost_estimate=QUICK,
        name="copied",
    )(value, later)


def halve_kernel(count, later_count, place_ref, *refs):
    own = place_ref[1] // 2
    outs = refs[2 * count + later_count :]
    width = refs[0].shape[2]
    for index, out in enumerate(outs):
        for part in range(count):
            out[:, part * width : (part + 1) * width] = add_low(
                refs[2 * part][own ^ index], refs[2 * part + 1][own ^ index]
            )


def halved(place, sides, *later):
    pairs, rows, width = sides[0].shape
    count = len(sides) // 2
    return pl.pallas_call(
        functools.partial(halve_kernel, count, len(later)),
        out_shape=(shape_of(rows, count * width, jnp.bfloat16),) * pairs,
        in_specs=[SCALARS] + [VECTORS] * len(sides) + [ANYWHERE] * len(later),
        out_specs=(VECTORS,) * pairs,
        compiler_params=pltpu.CompilerParams(vmem_limit_bytes=16 * MIB),
        cost_estimate=QUICK,
        name="halved",
    )(in_main(place), *sides, *later)


def arrived_sum(refs):
    total = refs[0][...].astype(jnp.float32)
    for ref in refs[1:]:
        total = total + ref[...].astype(jnp.float32)
    return total


def head_grads_kernel(
    place_ref,
    norm_ref,
    dq_ref,
    dk_ref,
    dv_ref,
    mid_own_ref,
    mid_far_ref,
    mixed_ref,
    one_ref,
    two_own_ref,
    two_far_ref,
    last_own_ref,
    last_far_ref,
    table_ref,
    later_ref,
    keep_ref,
    send_ref,
):
    half, model = mid_own_ref.shape
    side = place_ref[0] % 2
    own_rows = pl.ds(pl.multiple_of(side * half, half), half)
    far_rows = pl.ds(pl.multiple_of((1 - side) * half, half), half)
    norm = norm_ref[...]
    values = [col_dot(norm, ref[...]) for ref in (dq_ref, dk_ref, dv_ref)]
    last = col_dot(mid_own_ref[...], mixed_ref[own_rows, :])
    values.append(last + col_dot(mid_far_ref[...], mixed_ref[far_rows, :]))
    split_pairs(jnp.concatenate(values, axis=1), place_ref[1] % 2, keep_ref, send_ref)
    table = [table_ref[head : head + 1, :] for head in range(model // 128)]
    small = jnp.concatenate(
        [
            one_ref[...],
            two_own_ref[...] + two_far_ref[...],
            last_own_ref[...] + last_far_ref[...],
            jnp.concatenate(table, axis=1),
        ],
        axis=0,
    )
    high, rest = two_terms(small)
    small = jnp.concatenate([high, rest, jnp.zeros((8, model), jnp.bfloat16)], axis=0)
    rows = keep_ref.shape[1] - 16
    for pair in range(keep_ref.shape[0]):
        keep_ref[pair, rows:, :] = small
        send_ref[pair, rows:, :] = small


def head_grads(place, norm, grads, mid_own, mid_far, mixed, lines, table, later, pairs):
    model = norm.shape[1]
    piece = jax.ShapeDtypeStruct((pairs, model // (2 * pairs) + 16, model), jnp.bfloat16)
    return pl.pallas_call(
        head_grads_kernel,
        out_shape=(piece, piece),
        in_specs=[SCALARS] + [VECTORS] * 13 + [ANYWHERE],
        out_specs=(VECTORS, VECTORS),
        compiler_params=pltpu.CompilerParams(vmem_limit_bytes=24 * MIB),
        cost_estimate=QUICK,
        name="head_grads",
    )(in_main(place), norm, *grads, mid_own, mid_far, mixed, *lines, table, later)


def finish_kernel(count, *refs):
    dq_ref, dk_ref, dv_ref, out_ref, one_ref, two_ref, last_ref, rest_ref = refs[count + 1 :]
    total = arrived_sum(refs[:count])
    rows, inner = dq_ref.shape
    model = total.shape[1]
    dq_ref[...] = total[:rows, :inner]
    dk_ref[...] = total[:rows, inner : 2 * inner]
    dv_ref[...] = total[:rows, 2 * inner : 3 * inner]
    last = total[:rows, 3 * inner :]
    out_ref[...] = jnp.transpose(last) if out_ref.shape[0] == inner else last
    small = total[rows : rows + 4] + total[rows + 4 : rows + 8]
    one_ref[...] = small[0:1].reshape(model)
    two_ref[...] = small[1:2].reshape(model)
    last_ref[...] = small[2:3].reshape(model)
    lines = [small[3:4, index * 128 : (index + 1) * 128] for index in range(model // 128)]
    lines.append(jnp.zeros((8 - len(lines), 128), jnp.float32))
    rest_ref[...] = jnp.concatenate(lines, axis=0)


def finish(arrived, inner, later):
    rows, model = arrived[0].shape
    rows = rows - 16
    full = jnp.float32
    line = jax.ShapeDtypeStruct((model,), full)
    piece = shape_of(rows, inner, full)
    turned = rows % 8 == 0
    results = pl.pallas_call(
        functools.partial(finish_kernel, len(arrived)),
        out_shape=(
            piece,
            piece,
            piece,
            shape_of(inner, rows, full) if turned else piece,
            line,
            line,
            line,
            shape_of(8, 128, full),
        ),
        in_specs=[VECTORS] * len(arrived) + [ANYWHERE],
        out_specs=(VECTORS,) * 8,
        compiler_params=pltpu.CompilerParams(vmem_limit_bytes=12 * MIB),
        cost_estimate=pl.CostEstimate(
            flops=8 * rows * model, bytes_accessed=16 * rows * model, transcendentals=0
        ),
        name="finish",
    )(*arrived, later)
    grad_out = results[3] if turned else results[3].T
    return (*results[:3], grad_out, *results[4:])


def body(
    hidden_in,
    lengths,
    positive,
    norm1_gain,
    w_query,
    w_key,
    w_value,
    rel_bias,
    w_out,
    norm2_gain,
    w_in,
    w_ffout,
    final_gain,
    w_proj,
    proj_bias,
):
    bucket_count, head_count = rel_bias.shape
    pairs = lax.axis_size("wide") // 2
    wide = lax.axis_index("wide")
    place = jnp.stack([lax.axis_index("narrow"), wide]).astype(jnp.int32)
    table = rel_bias.T
    weights = (w_query.T, w_key.T, w_value.T)
    norm1, query, key, value, mixed, packed, spread = attend(
        lengths, table, hidden_in, norm1_gain, *weights
    )
    w_across = exchange(w_out, "narrow", 2)
    w_outs = (w_out, exchange(w_out, "narrow", 1), w_across, exchange(w_across, "narrow", 1))
    across = exchange(copied(packed, w_across), "narrow", 2)
    pieces = (packed, exchange(packed, "narrow", 1), across, exchange(across, "narrow", 1))
    far = middle(1, place, hidden_in, pieces, w_outs, norm2_gain, w_in, w_ffout)
    own = middle(0, place, hidden_in, pieces, w_outs, norm2_gain, w_in, w_ffout)
    after_far, norm2_far, act_far, slope_far, part_far = far
    after_own, norm2_own, act_own, slope_own, part_own = own
    total_own, total_far = summed_over_narrow(part_own, part_far)
    out_own, pooled_own = pool(0, place, lengths, after_own, total_own, final_gain, None)
    out_far, block = pool(
        1, place, lengths, after_far, total_far, final_gain, (positive, pooled_own)
    )
    loss, pooled_all, embed_low, bias_grad, slot_grad = contrast(place, block, w_proj, proj_bias)

    share = hidden_in.shape[1] // (2 * pairs)
    pooled_cols = lax.dynamic_slice_in_dim(pooled_all, wide * share, share, 1)
    grad_proj = dot_over(pooled_cols, embed_low, 0, 0)
    far = turn(1, place, lengths, out_far, slot_grad, slope_far, final_gain, w_ffout, w_in)
    own = turn(0, place, lengths, out_own, slot_grad, slope_own, final_gain, w_ffout, w_in)
    out_grad_far, out_low_far, pre_far, part_far, last_far = far
    out_grad_own, out_low_own, pre_own, part_own, last_own = own
    part = add_low(part_own, exchange(part_far, "narrow", 1))
    came = exchange(part, "narrow", 2)
    keep_a, send_a = pair_grads(place, (out_low_far, out_low_own), (act_far, act_own), part, pairs)
    came_a = exchange(send_a, "wide", 1)
    keep_b, send_b = pair_grads(
        place, (norm2_far, norm2_own), (pre_far, pre_own), send_a, pairs
    )
    came_b = exchange(send_b, "wide", 1)
    layer_out, token = assemble(place, out_own, out_far, send_b)
    total_own = add_after(part, came, came_a, grad_proj, token)
    total_far = exchange(total_own, "narrow", 1)
    mid_own, mid_low_own, mixed_grad_own, two_own = join(
        0, place, out_grad_own, after_own, total_own, norm2_gain, w_out
    )
    mid_far, mid_low_far, mixed_grad_far, two_far = join(
        1, place, out_grad_far, after_far, total_far, norm2_gain, w_out
    )
    a_half = halved(place, (keep_a, came_a), total_own)
    a_arrived = over_parity(a_half)
    back = attend_back(
        place,
        lengths,
        table,
        query,
        key,
        value,
        (mixed_grad_own, mixed_grad_far),
        spread,
        hidden_in,
        weights,
        norm1,
        mixed,
        (),
    )
    dq, dk, dv, table_lines, hidden_near, weights_near, norm1_near, mixed_near = back
    grads = (dq, dk, dv)
    part_far, one_far = norm1_parts(
        1, place, grads, hidden_near, weights_near, (came_b, *a_arrived[1:])
    )
    far_came = exchange(part_far, "narrow", 1)
    part_own, one_own = norm1_parts(0, place, grads, hidden_near, weights_near, (part_far,))
    one = one_far + one_own
    one = one + exchange(one, "narrow", 1)
    one = one + exchange(one, "narrow", 2)
    part = add_after(part_own, far_came, one)
    came = exchange(part, "narrow", 2)
    head_keep, head_send = head_grads(
        place,
        norm1_near,
        grads,
        mid_low_own,
        mid_low_far,
        mixed_near,
        (one, two_own, two_far, last_own, last_far),
        table_lines,
        part,
        pairs,
    )
    head_came = exchange(head_send, "wide", 1)
    b_half = halved(place, (keep_b, came_b), head_send)
    b_arrived = over_parity(b_half)
    total_own = add_after(part, came, head_came, *b_arrived[1:])
    total_far = exchange(total_own, "narrow", 1)
    head_half = halved(place, (head_keep, head_came), total_own)
    head_arrived = over_parity(head_half)
    given, _ = last(0, place, mid_own, hidden_near, total_own, norm1_gain, total_own)
    grad_input, token = last(1, place, mid_far, hidden_near, total_far, norm1_gain, given)
    grad_ffout = summed(a_arrived, head_half[0]).T
    grad_in = summed(b_arrived, head_half[0])
    inner = query.shape[1]
    grad_query, grad_key, grad_value, grad_out, one, two, three, lines = finish(
        head_arrived, inner, token
    )
    return (
        layer_out,
        loss,
        grad_input,
        one,
        grad_query,
        grad_key,
        grad_value,
        lines[:head_count, :bucket_count].T,
        grad_out,
        two,
        grad_in,
        grad_ffout,
        three,
        grad_proj,
        bias_grad,
    )


def solution(mesh):
    in_specs = (
        P("wide", None),
        P("wide"),
        P("wide"),
        P(),
        P(None, "narrow"),
        P(None, "narrow"),
        P(None, "narrow"),
        P(None, "narrow"),
        P("narrow", None),
        P(),
        P(None, "narrow"),
        P("narrow", None),
        P(),
        P(),
        P(),
    )
    out_specs = (
        P("wide", None),
        P("wide"),
        P("wide", None),
        P(),
        P("wide", "narrow"),
        P("wide", "narrow"),
        P("wide", "narrow"),
        P(None, "narrow"),
        P("narrow", "wide"),
        P(),
        P("wide", "narrow"),
        P("narrow", "wide"),
        P(),
        P("wide", None),
        P(),
    )
    return jax.shard_map(body, mesh=mesh, in_specs=in_specs, out_specs=out_specs, check_vma=False)
```

```python
import functools

import jax
import jax.numpy as jnp
from jax import lax
from jax.experimental import pallas as pl
from jax.experimental.pallas import tpu as pltpu
from jax.sharding import PartitionSpec as P

EPSILON = 1e-06
CONTRAST = 30.0
THRESHOLDS = (12, 16, 23, 32, 46, 64, 91)
GELU = 0.7978845608028654
CUBE = 0.044715
BLOCK = 128
MIB = 1024 * 1024
QUICK = pl.CostEstimate(flops=2**20, bytes_accessed=2**16, transcendentals=0)
SCALARS = pl.BlockSpec(memory_space=pltpu.SMEM)
VECTORS = pl.BlockSpec(memory_space=pltpu.VMEM)
ANYWHERE = pl.BlockSpec(memory_space=pl.ANY)


def in_main(value):
    return pltpu.with_memory_space_constraint(value, pltpu.HBM)


def exchange(value, axis, step):
    count = lax.axis_size(axis)
    return lax.ppermute(value, axis, [(k, k ^ step) for k in range(count)])


def add_low(left, right):
    return (left.astype(jnp.float32) + right.astype(jnp.float32)).astype(jnp.bfloat16)


def summed_over_narrow(keep, send):
    part = add_low(keep, exchange(send, "narrow", 1))
    own = add_low(part, exchange(part, "narrow", 2))
    return own, exchange(own, "narrow", 1)


def over_parity(blocks):
    count = lax.axis_size("wide")
    return (blocks[0], *(exchange(blocks[k], "wide", 2 * k) for k in range(1, count // 2)))


def two_terms(value):
    high = value.astype(jnp.bfloat16)
    return high, (value - high.astype(jnp.float32)).astype(jnp.bfloat16)


def offset_buckets(offset):
    distance = jnp.abs(offset)
    far_bucket = 8 + sum(((distance >= limit).astype(jnp.int32) for limit in THRESHOLDS))
    return jnp.where(distance < 8, distance, far_bucket) + 16 * (offset > 0).astype(jnp.int32)


def dot_over(left, right, left_dim, right_dim):
    return lax.dot_general(
        left, right, (((left_dim,), (right_dim,)), ((), ())), preferred_element_type=jnp.float32
    )


def row_dot(left, right):
    return lax.dot_general(
        left, right, (((1,), (1,)), ((), ())), preferred_element_type=jnp.float32
    )


def plain_dot(left, right):
    return lax.dot_general(
        left, right, (((1,), (0,)), ((), ())), preferred_element_type=jnp.float32
    )


def col_dot(left, right):
    return lax.dot_general(
        left, right, (((0,), (0,)), ((), ())), preferred_element_type=jnp.float32
    )


def slot_edges(lengths_ref, position):
    low = jnp.zeros_like(position)
    high = jnp.zeros_like(position)
    start = jnp.int32(0)
    for slot in range(lengths_ref.shape[0]):
        reached = position >= start
        low = jnp.where(reached, start, low)
        start_next = start + lengths_ref[slot]
        high = jnp.where(reached, start_next, high)
        start = start_next
    padded = position >= start
    return jnp.where(padded, position, low), jnp.where(padded, position + 1, high)


def bias_tiles(table_ref, tiles, turned):
    head_count, bucket_count = table_ref.shape
    lane = lax.broadcasted_iota(jnp.int32, (8, 4 * BLOCK), 1)
    offset = 2 * BLOCK - lane if turned else lane - 2 * BLOCK
    bucket = offset_buckets(offset)
    for head in range(head_count):
        line = jnp.zeros((8, 4 * BLOCK), jnp.float32)
        for index in range(bucket_count):
            line = jnp.where(bucket == index, table_ref[head, index], line)
        spread = jnp.broadcast_to(line[:1], (BLOCK, 4 * BLOCK))
        tiles[head] = pltpu.roll(spread, 0, 1, stride=1, stride_axis=0)


def unrolled_sum(tile):
    width = tile.shape[1]
    group = tile[:8]
    for first in range(8, tile.shape[0], 8):
        group = group + pltpu.roll(tile[first : first + 8], width - first, 1)
    line = group[:1]
    for row in range(1, 8):
        line = line + pltpu.roll(group, width - row, 1)[row : row + 1]
    return line


def attend_kernel(
    lengths_ref,
    table_ref,
    hidden_hbm,
    gain_ref,
    wq_hbm,
    wk_hbm,
    wv_hbm,
    norm_hbm,
    q_hbm,
    k_hbm,
    v_hbm,
    mixed_hbm,
    packed_hbm,
    spread_hbm,
    tiles,
    heads_q,
    heads_k,
    heads_v,
    heads_o,
    edges,
    spreads,
    hidden_ref,
    wq_ref,
    wk_ref,
    wv_ref,
    norm_ref,
    q_ref,
    k_ref,
    v_ref,
    mixed_ref,
    packed_ref,
    spread_ref,
    came,
    left,
):
    token_count = hidden_ref.shape[0]
    head_count, bucket_count = table_ref.shape
    width = q_ref.shape[1] // head_count
    chunk = 2 * BLOCK
    blocks = token_count // BLOCK
    starts = range(0, token_count, chunk)
    loads = []
    for index, (source, target) in enumerate(
        ((wq_hbm, wq_ref), (wk_hbm, wk_ref), (wv_hbm, wv_ref))
    ):
        loads.append(pltpu.make_async_copy(source, target, came.at[index]))
    for index, start in enumerate(starts):
        rows = pl.ds(start, chunk)
        loads.append(
            pltpu.make_async_copy(
                hidden_hbm.at[rows, :], hidden_ref.at[rows, :], came.at[3 + index]
            )
        )
    for load in (loads[3], *loads[:3], *loads[4:]):
        load.start()
    bias_tiles(table_ref, tiles, False)
    stores = []

    def store(source, target):
        copy = pltpu.make_async_copy(source, target, left.at[len(stores)])
        copy.start()
        stores.append(copy)

    for index, start in enumerate(starts):
        rows = pl.ds(start, chunk)
        loads[3 + index].wait()
        values = hidden_ref[rows, :].astype(jnp.float32)
        norm = (values * norm_scale(values) * gain_ref[...].reshape(1, -1)).astype(jnp.bfloat16)
        norm_ref[rows, :] = norm
        if index == 0:
            for load in loads[:3]:
                load.wait()
        for weight, out, parts in (
            (wq_ref, q_ref, heads_q),
            (wk_ref, k_ref, heads_k),
            (wv_ref, v_ref, heads_v),
        ):
            value = row_dot(norm, weight[...]).astype(jnp.bfloat16)
            out[rows, :] = value
            for head in range(head_count):
                parts[head, rows, :] = value[:, head * width : (head + 1) * width]
    for source, target in (
        (norm_ref, norm_hbm),
        (q_ref, q_hbm),
        (k_ref, k_hbm),
        (v_ref, v_hbm),
    ):
        store(source, target)
    lane = lax.broadcasted_iota(jnp.int32, (1, BLOCK), 1)

    def finish(head, rows, scores):
        top = jnp.max(scores, axis=1, keepdims=True)
        weights = jnp.exp(scores - top)
        total = jnp.sum(weights, axis=1, keepdims=True)
        keep = jnp.where(lane == head, top + jnp.log(total), spreads[rows, :])
        spreads[rows, :] = keep
        return weights.astype(jnp.bfloat16), 1.0 / total

    @pl.when(lengths_ref[0] > lengths_ref.shape[0])
    def document():
        def one_head(head, carry):
            keys, values = heads_k[head], heads_v[head]
            past = table_ref[head, bucket_count // 2 - 1]
            future = table_ref[head, bucket_count - 1]
            for start in range(0, token_count, chunk):
                rows = pl.ds(start, chunk)
                raw = row_dot(heads_q[head, rows, :], keys)
                lines = []
                for part in range(chunk // BLOCK):
                    line = []
                    for block in range(blocks):
                        away = block - start // BLOCK - part
                        piece = raw[
                            part * BLOCK : (part + 1) * BLOCK, block * BLOCK : (block + 1) * BLOCK
                        ]
                        if abs(away) <= 1:
                            first = (2 + away) * BLOCK
                            piece = piece + tiles[head, :, first : first + BLOCK]
                        else:
                            piece = piece + (past if away < 0 else future)
                        line.append(piece)
                    lines.append(jnp.concatenate(line, axis=1))
                weights, scale = finish(head, rows, jnp.concatenate(lines, axis=0))
                heads_o[head, rows, :] = (plain_dot(weights, values) * scale).astype(jnp.bfloat16)
            return carry

        lax.fori_loop(0, head_count, one_head, 0)

    @pl.when(lengths_ref[0] <= lengths_ref.shape[0])
    def queries():
        position = lax.broadcasted_iota(jnp.int32, (8, token_count), 1)
        low, high = slot_edges(lengths_ref, position)
        edges[0] = low
        edges[1] = high

        def one_head(head, carry):
            for block in range(blocks):
                first = max(block - 1, 0)
                last = min(block + 1, blocks - 1) + 1
                rows = pl.ds(block * BLOCK, BLOCK)
                window = pl.ds(first * BLOCK, (last - first) * BLOCK)
                scores = row_dot(heads_q[head, rows, :], heads_k[head, window, :])
                shift = (2 + first - block) * BLOCK
                scores = scores + tiles[head, :, shift : shift + (last - first) * BLOCK]
                token = block * BLOCK + lax.broadcasted_iota(jnp.int32, scores.shape, 0)
                inside = (token >= edges[0, :1, window]) & (token < edges[1, :1, window])
                weights, scale = finish(head, rows, jnp.where(inside, scores, -1e30))
                heads_o[head, rows, :] = (
                    plain_dot(weights, heads_v[head, window, :]) * scale
                ).astype(jnp.bfloat16)
            return carry

        lax.fori_loop(0, head_count, one_head, 0)

    half = token_count // 2
    pair = jnp.concatenate([heads_o[0], heads_o[1]], axis=1)
    mixed_ref[:, : 2 * width] = pair
    mixed_ref[:, 2 * width :] = heads_o[2]
    packed_ref[:token_count, :] = pair
    packed_ref[token_count:, :] = jnp.concatenate([heads_o[2, :half], heads_o[2, half:]], axis=1)
    store(packed_ref, packed_hbm)
    store(mixed_ref, mixed_hbm)
    for start in range(0, token_count, BLOCK):
        turned = jnp.transpose(spreads[pl.ds(start, BLOCK), :])
        spread_ref[:, start : start + BLOCK] = turned[:8]
    store(spread_ref, spread_hbm)
    for copy in stores:
        copy.wait()


def attend(lengths, table, hidden_in, gain, w_query, w_key, w_value):
    token_count, model = hidden_in.shape
    head_count = table.shape[0]
    inner = w_query.shape[0]
    width = inner // head_count
    low = jnp.bfloat16
    heads = pltpu.VMEM((head_count, token_count, width), low)
    weight = pltpu.VMEM((inner, model), low)
    results = (
        ((token_count, model), low),
        ((token_count, inner), low),
        ((token_count, inner), low),
        ((token_count, inner), low),
        ((token_count, inner), low),
        ((token_count * 3 // 2, 2 * width), low),
        ((8, token_count), jnp.float32),
    )
    return pl.pallas_call(
        attend_kernel,
        out_shape=tuple(
            (jax.ShapeDtypeStruct if index == 5 else pltpu.HBM)(*result)
            for index, result in enumerate(results)
        ),
        in_specs=[SCALARS, SCALARS, ANYWHERE, VECTORS] + [ANYWHERE] * 3,
        out_specs=(ANYWHERE,) * 7,
        scratch_shapes=[
            pltpu.VMEM((head_count, BLOCK, 4 * BLOCK), jnp.float32),
            heads,
            heads,
            heads,
            heads,
            pltpu.VMEM((2, 8, token_count), jnp.int32),
            pltpu.VMEM((token_count, BLOCK), jnp.float32),
            pltpu.VMEM((token_count, model), low),
            weight,
            weight,
            weight,
            *(pltpu.VMEM(*result) for result in results),
            pltpu.SemaphoreType.DMA((3 + token_count // (2 * BLOCK),)),
            pltpu.SemaphoreType.DMA((7,)),
        ],
        compiler_params=pltpu.CompilerParams(vmem_limit_bytes=28 * MIB),
        cost_estimate=QUICK,
        name="attend",
    )(
        *(in_main(value) for value in (lengths, table, hidden_in, gain)),
        *(in_main(value) for value in (w_query, w_key, w_value)),
    )


def attend_back_kernel(
    later_count,
    place_ref,
    lengths_ref,
    table_ref,
    q_hbm,
    k_hbm,
    v_hbm,
    grad_own_hbm,
    grad_far_hbm,
    spread_hbm,
    hidden_hbm,
    wq_hbm,
    wk_hbm,
    wv_hbm,
    norm_hbm,
    mixed_hbm,
    *refs,
):
    refs = refs[later_count:]
    dq_hbm, dk_hbm, dv_hbm, table_grad_hbm, hidden_near, weights_near = refs[:6]
    norm_near, mixed_near = refs[6:8]
    refs = refs[8:]
    tiles, heads_q, heads_k, heads_v, heads_g, probs, grads, sums_q, sums_k, sums_v = refs[:10]
    near, far, edges, lines_s, q_ref, k_ref, v_ref, grad_own_ref, grad_far_ref = refs[10:19]
    spread_ref, dq_ref, dk_ref, dv_ref, table_grad_ref, came, left = refs[19:]
    token_count = q_ref.shape[0]
    head_count, bucket_count = table_ref.shape
    width = q_ref.shape[1] // head_count
    chunk = 2 * BLOCK
    blocks = token_count // BLOCK
    loads = [
        pltpu.make_async_copy(source, target, came.at[index])
        for index, (source, target) in enumerate(
            (
                (q_hbm, q_ref),
                (k_hbm, k_ref),
                (v_hbm, v_ref),
                (grad_own_hbm, grad_own_ref),
                (grad_far_hbm, grad_far_ref),
                (spread_hbm, spread_ref),
                (hidden_hbm, hidden_near),
                (wq_hbm, weights_near.at[0]),
                (wk_hbm, weights_near.at[1]),
                (wv_hbm, weights_near.at[2]),
                (norm_hbm, norm_near),
                (mixed_hbm, mixed_near),
            )
        )
    ]
    for load in loads:
        load.start()
    stores = []

    def store(source, target):
        copy = pltpu.make_async_copy(source, target, left.at[len(stores)])
        copy.start()
        stores.append(copy)

    half = token_count // 2
    side = place_ref[0] % 2
    own_rows = pl.ds(pl.multiple_of(side * half, half), half)
    far_rows = pl.ds(pl.multiple_of((1 - side) * half, half), half)
    bias_tiles(table_ref, tiles, True)
    token = lax.broadcasted_iota(jnp.int32, (token_count, BLOCK - width), 0)
    lane = lax.broadcasted_iota(jnp.int32, (token_count, BLOCK - width), 1)
    marks = (token // BLOCK == lane).astype(jnp.float32).astype(jnp.bfloat16)
    for load in loads[:6]:
        load.wait()
    for head in range(head_count):
        cut = slice(head * width, (head + 1) * width)
        heads_q[head] = jnp.concatenate([q_ref[:, cut], marks], axis=1)
        heads_k[head] = k_ref[:, cut]
        heads_v[head] = v_ref[:, cut]
        heads_g[head, own_rows, :] = grad_own_ref[:, cut]
        heads_g[head, far_rows, :] = grad_far_ref[:, cut]
        lines_s[head] = jnp.broadcast_to(spread_ref[head : head + 1, :], (8, token_count))
    near[...] = jnp.zeros_like(near)
    far[...] = jnp.zeros_like(far)

    def score_back(scores, spread, grad_probs):
        weights = jnp.exp(scores - spread)
        delta = jnp.sum(weights * grad_probs, axis=0, keepdims=True)
        return weights, weights * (grad_probs - delta)

    @pl.when(lengths_ref[0] > lengths_ref.shape[0])
    def document():
        def one_head(head, carry):
            keys, values = heads_k[head], heads_v[head]
            past = table_ref[head, bucket_count // 2 - 1]
            future = table_ref[head, bucket_count - 1]
            for start in range(0, token_count, chunk):
                rows = pl.ds(start, chunk)
                raw = row_dot(keys, heads_q[head, rows, :width])
                lines = []
                for block in range(blocks):
                    line = []
                    for part in range(chunk // BLOCK):
                        away = block - start // BLOCK - part
                        piece = raw[
                            block * BLOCK : (block + 1) * BLOCK, part * BLOCK : (part + 1) * BLOCK
                        ]
                        if abs(away) <= 1:
                            first = (2 - away) * BLOCK
                            piece = piece + tiles[head, :, first : first + BLOCK]
                        else:
                            piece = piece + (past if away < 0 else future)
                        line.append(piece)
                    lines.append(jnp.concatenate(line, axis=1))
                scores = jnp.concatenate(lines, axis=0)
                grad_probs = row_dot(values, heads_g[head, rows, :])
                weights, score_grad = score_back(
                    scores, lines_s[head, :1, rows], grad_probs
                )
                probs[:, rows] = weights.astype(jnp.bfloat16)
                grads[:, rows] = score_grad.astype(jnp.bfloat16)
                for block in range(blocks):
                    for part in range(chunk // BLOCK):
                        away = block - start // BLOCK - part
                        if abs(away) <= 1:
                            first = (2 - away) * BLOCK
                            near[head, :, first : first + BLOCK] += score_grad[
                                block * BLOCK : (block + 1) * BLOCK,
                                part * BLOCK : (part + 1) * BLOCK,
                            ]
            sums_v[head] = plain_dot(probs[...], heads_g[head])
            key_sums = plain_dot(grads[...], heads_q[head])
            sums_k[head] = key_sums[:, :width]
            sums_q[head] = col_dot(grads[...], keys)
            for block in range(blocks):
                line = jnp.sum(key_sums[block * BLOCK : (block + 1) * BLOCK], axis=0, keepdims=True)
                far[head, block : block + 1, :] = line
            return carry

        lax.fori_loop(0, head_count, one_head, 0)

    @pl.when(lengths_ref[0] <= lengths_ref.shape[0])
    def queries():
        position = lax.broadcasted_iota(jnp.int32, (8, token_count), 1)
        low, high = slot_edges(lengths_ref, position)
        edges[0] = low
        edges[1] = high
        sums_k[...] = jnp.zeros_like(sums_k)
        sums_v[...] = jnp.zeros_like(sums_v)

        def one_head(head, carry):
            for block in range(blocks):
                first = max(block - 1, 0)
                last = min(block + 1, blocks - 1) + 1
                rows = pl.ds(block * BLOCK, BLOCK)
                window = pl.ds(first * BLOCK, (last - first) * BLOCK)
                scores = row_dot(heads_k[head, window, :], heads_q[head, rows, :width])
                lines = []
                for other in range(first, last):
                    begin = (2 - (other - block)) * BLOCK
                    lines.append(tiles[head, :, begin : begin + BLOCK])
                scores = scores + jnp.concatenate(lines, axis=0)
                token = first * BLOCK + lax.broadcasted_iota(jnp.int32, scores.shape, 0)
                inside = (token >= edges[0, :1, rows]) & (token < edges[1, :1, rows])
                grad_probs = row_dot(heads_v[head, window, :], heads_g[head, rows, :])
                weights, score_grad = score_back(
                    jnp.where(inside, scores, -1e30), lines_s[head, :1, rows], grad_probs
                )
                for other in range(first, last):
                    begin = (2 - (other - block)) * BLOCK
                    near[head, :, begin : begin + BLOCK] += score_grad[
                        (other - first) * BLOCK : (other - first + 1) * BLOCK
                    ]
                grad_low = score_grad.astype(jnp.bfloat16)
                sums_v[head, window, :] += plain_dot(
                    weights.astype(jnp.bfloat16), heads_g[head, rows, :]
                )
                sums_k[head, window, :] += plain_dot(grad_low, heads_q[head, rows, :width])
                sums_q[head, rows, :] = col_dot(grad_low, heads_k[head, window, :])
            return carry

        lax.fori_loop(0, head_count, one_head, 0)

    for sums, out in ((sums_q, dq_ref), (sums_k, dk_ref), (sums_v, dv_ref)):
        out[...] = jnp.concatenate(
            [sums[head].astype(jnp.bfloat16) for head in range(head_count)], axis=1
        )
    for source, target in ((dq_ref, dq_hbm), (dk_ref, dk_hbm), (dv_ref, dv_hbm)):
        store(source, target)
    lines = []
    for head in range(head_count):
        lines.append(unrolled_sum(near[head]))
    lines.append(jnp.zeros((8 - head_count, 4 * BLOCK), jnp.float32))
    by_offset = jnp.concatenate(lines, axis=0)
    offset = 2 * BLOCK - lax.broadcasted_iota(jnp.int32, (4 * BLOCK, BLOCK), 0)
    place = lax.broadcasted_iota(jnp.int32, (4 * BLOCK, BLOCK), 1)
    onehot = (offset_buckets(offset) == place).astype(jnp.float32).astype(jnp.bfloat16)
    high, rest = two_terms(by_offset)
    table_grad = plain_dot(high, onehot) + plain_dot(rest, onehot)
    row = lax.broadcasted_iota(jnp.int32, (blocks, BLOCK), 0)
    column = lax.broadcasted_iota(jnp.int32, (blocks, BLOCK), 1) - width
    real = (column >= 0) & (column < blocks)
    is_past = real & (row - column <= -2)
    is_future = real & (row - column >= 2)
    lane = lax.broadcasted_iota(jnp.int32, (1, BLOCK), 1)
    lines = []
    for head in range(head_count):
        past = jnp.sum(jnp.where(is_past, far[head], 0.0), keepdims=True)
        future = jnp.sum(jnp.where(is_future, far[head], 0.0), keepdims=True)
        lines.append(
            table_grad[head : head + 1]
            + jnp.where(lane == bucket_count // 2 - 1, past, 0.0)
            + jnp.where(lane == bucket_count - 1, future, 0.0)
        )
    lines.append(jnp.zeros((8 - head_count, BLOCK), jnp.float32))
    table_grad_ref[...] = jnp.concatenate(lines, axis=0)
    store(table_grad_ref, table_grad_hbm)
    for copy in (*stores, *loads[6:]):
        copy.wait()


def attend_back(
    place, lengths, table, query, key, value, grads, spread, hidden_in, weights, norm, mixed, later
):
    token_count, inner = query.shape
    model = hidden_in.shape[1]
    head_count = table.shape[0]
    width = inner // head_count
    low, full = jnp.bfloat16, jnp.float32
    heads = pltpu.VMEM((head_count, token_count, width), low)
    sums = pltpu.VMEM((head_count, token_count, width), full)
    square = pltpu.VMEM((token_count, token_count), low)
    tile = pltpu.VMEM((head_count, BLOCK, 4 * BLOCK), full)
    flat = pltpu.VMEM((token_count, inner), low)
    half = pltpu.VMEM((token_count // 2, inner), low)
    return pl.pallas_call(
        functools.partial(attend_back_kernel, len(later)),
        out_shape=(
            shape_of(token_count, inner, low),
            shape_of(token_count, inner, low),
            shape_of(token_count, inner, low),
            shape_of(8, BLOCK, full),
            near_shape(token_count, model, low),
            pltpu.VMEM((3, inner, model), low),
            near_shape(token_count, model, low),
            near_shape(token_count, inner, low),
        ),
        in_specs=[SCALARS] * 3 + [ANYWHERE] * (12 + len(later)),
        out_specs=(ANYWHERE,) * 8,
        scratch_shapes=[
            tile,
            pltpu.VMEM((head_count, token_count, BLOCK), low),
            heads,
            heads,
            heads,
            square,
            square,
            sums,
            sums,
            sums,
            tile,
            pltpu.VMEM((head_count, token_count // BLOCK, BLOCK), full),
            pltpu.VMEM((2, 8, token_count), jnp.int32),
            pltpu.VMEM((head_count, 8, token_count), full),
            flat,
            flat,
            flat,
            half,
            half,
            pltpu.VMEM((8, token_count), full),
            flat,
            flat,
            flat,
            pltpu.VMEM((8, BLOCK), full),
            pltpu.SemaphoreType.DMA((12,)),
            pltpu.SemaphoreType.DMA((4,)),
        ],
        compiler_params=pltpu.CompilerParams(vmem_limit_bytes=34 * MIB),
        cost_estimate=pl.CostEstimate(
            flops=12 * 2**30, bytes_accessed=2**16, transcendentals=0
        ),
        name="attend_back",
    )(
        *(in_main(value) for value in (place, lengths, table, query, key, value)),
        *grads,
        *(in_main(value) for value in (spread, hidden_in, *weights, norm, mixed)),
        *later,
    )


def parts_kernel(flip, later_count, place_ref, dq_ref, dk_ref, dv_ref, hidden_ref, w_ref, *refs):
    part_ref, one_ref = refs[later_count:]
    half = (place_ref[0] % 2) ^ flip
    one = jnp.zeros(one_ref.shape, jnp.float32)
    for _, own, whole in chunk_rows(part_ref.shape[0], half):
        part = plain_dot(dq_ref[whole, :], w_ref[0])
        part = part + plain_dot(dk_ref[whole, :], w_ref[1])
        part = part + plain_dot(dv_ref[whole, :], w_ref[2])
        part_ref[own, :] = part.astype(jnp.bfloat16)
        values = hidden_ref[whole, :].astype(jnp.float32)
        one = one + jnp.sum(part * values * norm_scale(values), axis=0, keepdims=True)
    one_ref[...] = one


def norm1_parts(flip, place, grads, hidden, weights, later):
    token_count, model = hidden.shape
    return pl.pallas_call(
        functools.partial(parts_kernel, flip, len(later)),
        out_shape=(
            shape_of(token_count // 2, model, jnp.bfloat16),
            shape_of(1, model, jnp.float32),
        ),
        in_specs=[SCALARS] + [VECTORS] * 5 + [ANYWHERE] * len(later),
        out_specs=(VECTORS, VECTORS),
        compiler_params=pltpu.CompilerParams(vmem_limit_bytes=20 * MIB),
        cost_estimate=pl.CostEstimate(
            flops=3 * weights.size * token_count // 3,
            bytes_accessed=4 * hidden.size,
            transcendentals=0,
        ),
        name="norm1_parts",
    )(in_main(place), *grads, hidden, weights, *later)


def split_gelu(value):
    square = value * value
    inner = GELU * value * (1.0 + CUBE * square)
    turn = jnp.tanh(inner)
    half = 0.5 * (1.0 + turn)
    slope = half + 0.5 * value * (1.0 - turn * turn) * GELU * (1.0 + 3.0 * CUBE * square)
    return half * value, slope


def norm_scale(values):
    return lax.rsqrt(jnp.mean(values * values, axis=1, keepdims=True) + EPSILON)


def norm_back(values, gain, grad):
    scale = norm_scale(values)
    scaled = grad * gain
    share = jnp.mean(scaled * values, axis=1, keepdims=True)
    back = scale * scaled - (scale * scale * scale) * values * share
    return back, jnp.sum(grad * values * scale, axis=0, keepdims=True)


def slot_lines(lengths_ref, shape, axis):
    slot = lax.broadcasted_iota(jnp.int32, shape, axis)
    starts = jnp.zeros(shape, jnp.int32)
    ends = jnp.zeros(shape, jnp.int32)
    start = jnp.int32(0)
    for index in range(lengths_ref.shape[0]):
        end = start + lengths_ref[index]
        starts = jnp.where(slot == index, start, starts)
        ends = jnp.where(slot == index, end, ends)
        start = end
    return starts, ends


def as_low(mask):
    return mask.astype(jnp.float32).astype(jnp.bfloat16)


def row_call(kernel, flip, inputs, outputs, scratch, place, aliases, flops):
    specs = {"scalar": SCALARS, "line": VECTORS, "near": VECTORS, "any": ANYWHERE}
    return pl.pallas_call(
        functools.partial(kernel, flip),
        out_shape=tuple(shape for _, shape in outputs),
        in_specs=[SCALARS] + [specs[kind] for kind, _ in inputs],
        out_specs=tuple(specs[kind] for kind, _ in outputs),
        scratch_shapes=scratch,
        input_output_aliases=aliases,
        compiler_params=pltpu.CompilerParams(vmem_limit_bytes=24 * MIB),
        cost_estimate=pl.CostEstimate(flops=flops, bytes_accessed=6 * 2**20, transcendentals=0),
        name=kernel.__name__,
    )(
        in_main(place),
        *(in_main(value) if kind in ("line", "scalar") else value for kind, value in inputs),
    )


def near_shape(rows, columns, kind):
    return pltpu.VMEM((rows, columns), kind)


def main_shape(rows, columns, kind):
    return pltpu.HBM((rows, columns), kind)


def shape_of(rows, columns, kind):
    return jax.ShapeDtypeStruct((rows, columns), kind)


def chunk_rows(rows, half):
    chunk = rows // 2
    for step in range(2):
        whole = pl.ds(pl.multiple_of(half * rows + step * chunk, chunk), chunk)
        yield step, pl.ds(step * chunk, chunk), whole


def middle_kernel(
    flip,
    place_ref,
    hidden_ref,
    wide0_ref,
    wide1_ref,
    wide2_ref,
    wide3_ref,
    rest0_ref,
    rest1_ref,
    rest2_ref,
    rest3_ref,
    weight0_ref,
    weight1_ref,
    weight2_ref,
    weight3_ref,
    gain_ref,
    w_in_ref,
    w_ffout_ref,
    after_ref,
    norm_ref,
    act_ref,
    slope_ref,
    part_ref,
    pieces,
    weights,
):
    narrow = place_ref[0]

    @pl.when(pl.program_id(0) == 0)
    def first():
        for index, ref in enumerate((weight0_ref, weight1_ref, weight2_ref, weight3_ref)):
            weights[narrow ^ index] = ref[...]

    half = (narrow % 2) ^ flip
    inner = pieces.shape[2]
    mains = (wide0_ref, wide1_ref, wide2_ref, wide3_ref)
    rests = (rest0_ref, rest1_ref, rest2_ref, rest3_ref)
    for index in range(4):
        rest = rests[index][...]
        width = rest.shape[1] // 2
        tail = jnp.where(half == 0, rest[:, :width], rest[:, width:])
        pieces[narrow ^ index] = jnp.concatenate([mains[index][...], tail], axis=1)
    total = plain_dot(pieces[0], weights[0])
    for index in range(1, 4):
        total = total + plain_dot(pieces[index], weights[index])
    after = hidden_ref[...].astype(jnp.float32) + total
    after_ref[...] = after
    norm = (after * norm_scale(after) * gain_ref[...].reshape(1, -1)).astype(jnp.bfloat16)
    norm_ref[...] = norm
    act, slope = split_gelu(plain_dot(norm, w_in_ref[...]))
    act_low = act.astype(jnp.bfloat16)
    act_ref[...] = act_low
    slope_ref[...] = slope.astype(jnp.bfloat16)
    part_ref[...] = plain_dot(act_low, w_ffout_ref[...]).astype(jnp.bfloat16)


def half_block(flip):
    def place(step, place_ref):
        return (((place_ref[0] % 2) ^ flip) * 2 + step, 0)

    return place


def own_block(step, place_ref):
    return (step, 0)


def whole_block(step, place_ref):
    return (0, 0)


def grid_call(kernel, flip, inputs, outputs, scratch, place, aliases, flops):
    kinds = {"half": half_block(flip), "own": own_block, "all": whole_block}

    def spec(item):
        kind, shape = item
        if kind == "scalar":
            return SCALARS
        if kind == "any":
            return pl.BlockSpec(memory_space=pl.ANY)
        if kind == "rest":
            return pl.BlockSpec(shape, lambda step, place_ref: (4 + step, 0))
        if kind == "line":
            return pl.BlockSpec(shape, lambda step, place_ref: (0,))
        return pl.BlockSpec(shape, kinds[kind])

    return pl.pallas_call(
        functools.partial(kernel, flip),
        out_shape=tuple(shape for _, _, shape in outputs),
        grid_spec=pltpu.PrefetchScalarGridSpec(
            num_scalar_prefetch=1,
            grid=(2,),
            in_specs=[spec((kind, shape)) for kind, shape, _ in inputs],
            out_specs=tuple(spec((kind, shape)) for kind, shape, _ in outputs),
            scratch_shapes=scratch,
        ),
        input_output_aliases=aliases,
        compiler_params=pltpu.CompilerParams(
            vmem_limit_bytes=16 * MIB, dimension_semantics=("arbitrary",)
        ),
        cost_estimate=pl.CostEstimate(flops=flops, bytes_accessed=6 * 2**20, transcendentals=0),
        name=kernel.__name__,
    )(
        in_main(place),
        *(in_main(value) if kind in ("line", "scalar") else value for kind, _, value in inputs),
    )


def middle(flip, place, hidden_in, packed, w_outs, gain, w_in, w_ffout):
    token_count, model = hidden_in.shape
    hidden_count = w_in.shape[1]
    rows, chunk = token_count // 2, token_count // 4
    inner = w_outs[0].shape[0]
    low = jnp.bfloat16
    inputs = [("half", (chunk, model), in_main(hidden_in))]
    inputs += [("half", (chunk, 128), piece) for piece in packed]
    inputs += [("rest", (chunk, 128), piece) for piece in packed]
    inputs += [
        *(("all", weight.shape, weight) for weight in w_outs),
        ("line", (model,), gain),
        ("all", w_in.shape, w_in),
        ("all", w_ffout.shape, w_ffout),
    ]
    outputs = [
        ("own", (chunk, model), shape_of(rows, model, jnp.float32)),
        ("own", (chunk, model), shape_of(rows, model, low)),
        ("own", (chunk, hidden_count), shape_of(rows, hidden_count, low)),
        ("own", (chunk, hidden_count), shape_of(rows, hidden_count, low)),
        ("own", (chunk, model), shape_of(rows, model, low)),
    ]
    scratch = [pltpu.VMEM((4, chunk, inner), low), pltpu.VMEM((4, inner, model), low)]
    flops = 2 * rows * model * (model + 2 * hidden_count)
    return grid_call(middle_kernel, flip, inputs, outputs, scratch, place, {}, flops)


def pool_kernel(flip, place_ref, lengths_ref, after_ref, total_ref, gain_ref, *refs):
    half = (place_ref[0] % 2) ^ flip
    rows, model = after_ref.shape
    chunk = rows // 2
    slots = lengths_ref.shape[0]
    if flip == 0:
        out_ref, pooled_ref = refs
        pooled = jnp.zeros(pooled_ref.shape, jnp.float32)
    else:
        positive_ref, partial_ref, out_ref, block_ref, rows_s = refs
        pooled = partial_ref[...]
    starts, ends = slot_lines(lengths_ref, (slots, 1), 0)
    for step, own, _ in chunk_rows(rows, half):
        value = after_ref[own, :] + total_ref[own, :].astype(jnp.float32)
        out_ref[own, :] = value
        high, rest = two_terms(value * norm_scale(value) * gain_ref[...].reshape(1, -1))
        token = half * rows + step * chunk
        token = token + lax.broadcasted_iota(jnp.int32, (slots, chunk), 1)
        member = as_low((token >= starts) & (token < ends))
        pooled = pooled + (plain_dot(member, high) + plain_dot(member, rest))
    if flip == 0:
        pooled_ref[...] = pooled
        return
    count = jnp.maximum(ends - starts, 1).astype(jnp.float32)
    slot = lax.broadcasted_iota(jnp.int32, (slots, 128), 0)
    lane = lax.broadcasted_iota(jnp.int32, (slots, 128), 1)
    partner = jnp.zeros((slots, 128), jnp.int32)
    for index in range(slots):
        partner = jnp.where(slot == index, positive_ref[index], partner)
    used = jnp.where(ends > starts, 1, 0)
    facts = jnp.where(lane == 0, used, jnp.where(lane == 1, partner >> 7, partner & 127))
    rows_s[:, :model] = pooled / count
    rows_s[:, model:] = facts.astype(jnp.float32)
    part = slots // 2
    own = rows_s[pl.ds(pl.multiple_of((place_ref[0] % 2) * part, part), part), :]
    block_ref[...] = own.astype(jnp.bfloat16)


def pool(flip, place, lengths, after, total, gain, more):
    rows, model = after.shape
    slots = lengths.shape[0]
    inputs = [("scalar", lengths), ("near", after), ("near", total), ("line", gain)]
    outputs = [("near", shape_of(rows, model, jnp.float32))]
    scratch = []
    if flip == 0:
        outputs.append(("near", shape_of(slots, model, jnp.float32)))
    else:
        positive, partial = more
        inputs += [("scalar", positive), ("near", partial)]
        outputs.append(("near", shape_of(slots // 2, model + 128, jnp.bfloat16)))
        scratch = [pltpu.VMEM((slots, model + 128), jnp.float32)]
    return row_call(pool_kernel, flip, inputs, outputs, scratch, place, {}, 2**24)


def assemble_kernel(place_ref, own_ref, far_ref, later_ref, out_hbm, token_ref, sems):
    rows = own_ref.shape[0]
    token_ref[...] = jnp.zeros(token_ref.shape, jnp.float32)
    copies = []
    for flip, ref in enumerate((own_ref, far_ref)):
        half = (place_ref[0] % 2) ^ flip
        target = out_hbm.at[pl.ds(pl.multiple_of(half * rows, rows), rows), :]
        copies.append(pltpu.make_async_copy(ref, target, sems.at[flip]))
    for copy in copies:
        copy.start()
    for copy in copies:
        copy.wait()


def assemble(place, own, far, later):
    rows, model = own.shape
    return pl.pallas_call(
        assemble_kernel,
        out_shape=(main_shape(2 * rows, model, own.dtype), shape_of(8, 128, jnp.float32)),
        in_specs=[SCALARS] + [ANYWHERE] * 3,
        out_specs=(ANYWHERE, VECTORS),
        scratch_shapes=[pltpu.SemaphoreType.DMA((2,))],
        compiler_params=pltpu.CompilerParams(vmem_limit_bytes=4 * MIB),
        cost_estimate=QUICK,
        name="assemble",
    )(in_main(place), own, far, later)


def contrast_kernel(groups, place_ref, *refs):
    mine, other = refs[:groups], refs[groups : 2 * groups]
    w_proj_ref, bias_ref, loss_ref, pooled_hbm, low_hbm, bias_grad_ref = refs[
        2 * groups : 2 * groups + 6
    ]
    slot_grad_ref, pooled_ref, low_ref, sems, embeds, units, facts, spreads, losses = refs[
        2 * groups + 6 :
    ]
    narrow, wide = place_ref[0], place_ref[1]
    part = mine[0].shape[0] // 2
    model = w_proj_ref.shape[0]
    slots = 2 * part
    count = 2 * groups * slots
    block = min(count, 256)
    side = narrow % 2
    for refs_at, at in ((mine, side), (other, 1 - side)):
        for index, ref in enumerate(refs_at):
            for odd in range(2):
                pack = wide ^ (2 * index + odd)
                rows = pl.ds(pl.multiple_of(pack * slots + at * part, part), part)
                pooled_ref[rows, :] = ref[odd * part : (odd + 1) * part, :model]
                facts[rows, :] = ref[odd * part : (odd + 1) * part, model:]
    stores = [
        pltpu.make_async_copy(pooled_ref, pooled_hbm, sems.at[0]),
        pltpu.make_async_copy(low_ref, low_hbm, sems.at[1]),
    ]
    stores[0].start()
    for start in range(0, count, block):
        rows = pl.ds(start, block)
        embed = plain_dot(pooled_ref[rows, :], w_proj_ref[...]) + bias_ref[...].reshape(1, -1)
        embeds[rows, :] = embed
        scale = lax.rsqrt(jnp.sum(embed * embed, axis=1, keepdims=True) + EPSILON)
        units[rows, :] = (embed * scale).astype(jnp.bfloat16)
    pick_row = lax.broadcasted_iota(jnp.int32, (8, 128), 0)
    pick_lane = lax.broadcasted_iota(jnp.int32, (8, 128), 1)
    pick = as_low(pick_row == pick_lane)
    lines = row_dot(pick, facts[...])
    used_line = lines[:1] > 0.5
    partner_line = (lines[1:2] * 128.0 + lines[2:3]).astype(jnp.int32)
    column = lax.broadcasted_iota(jnp.int32, (block, count), 1)
    row = lax.broadcasted_iota(jnp.int32, (block, count), 0)

    def columns_of(rows):
        values = facts[rows, :].astype(jnp.float32)
        used = values[:, :1] > 0.5
        partner = (values[:, 1:2] * 128.0 + values[:, 2:3]).astype(jnp.int32)
        return used, partner

    for start in range(0, count, block):
        rows = pl.ds(start, block)
        sims = CONTRAST * row_dot(units[rows, :], units[...])
        used, partner = columns_of(rows)
        usable = used_line & (column != row + start)
        masked = jnp.where(usable, sims, -1e30)
        top = jnp.max(masked, axis=1, keepdims=True)
        total = jnp.sum(jnp.exp(masked - top), axis=1, keepdims=True)
        spread = top + jnp.log(total)
        score = jnp.sum(jnp.where(column == partner, sims, 0.0), axis=1, keepdims=True)
        losses[rows, :] = jnp.where(used, spread - score, 0.0)
        turned = jnp.transpose(jnp.broadcast_to(spread, (block, 128)))
        spreads[:, start : start + block] = turned[:8]
    loss = losses[pl.ds(pl.multiple_of(wide * slots, slots), slots), :]
    loss = jnp.transpose(jnp.broadcast_to(loss, (slots, 128)))
    loss_ref[...] = loss[:1, :].reshape(slots)
    bias_grad = jnp.zeros((1, model), jnp.float32)
    for start in range(0, count, block):
        rows = pl.ds(start, block)
        if block < count:
            sims = CONTRAST * row_dot(units[rows, :], units[...])
        used, partner = columns_of(rows)
        differ = column != row + start
        spread = jnp.transpose(jnp.broadcast_to(spreads[:1, start : start + block], (128, block)))
        masked = jnp.where(used_line & differ, sims, -1e30)
        ahead = jnp.exp(masked - spread[:, :1]) - jnp.where(column == partner, 1.0, 0.0)
        masked = jnp.where(used & differ, sims, -1e30)
        behind = jnp.exp(masked - spreads[:1, :]) - jnp.where(
            row + start == partner_line, 1.0, 0.0
        )
        both = jnp.where(used, ahead, 0.0) + jnp.where(used_line, behind, 0.0)
        high, rest = two_terms(both)
        grad = CONTRAST * (plain_dot(high, units[...]) + plain_dot(rest, units[...]))
        embed = embeds[rows, :]
        scale = lax.rsqrt(jnp.sum(embed * embed, axis=1, keepdims=True) + EPSILON)
        share = jnp.sum(embed * grad, axis=1, keepdims=True)
        back = scale * grad - (scale * scale * scale) * embed * share
        back_low = back.astype(jnp.bfloat16)
        low_ref[rows, :] = back_low
        bias_grad = bias_grad + jnp.sum(back_low.astype(jnp.float32), axis=0, keepdims=True)
    bias_grad_ref[...] = bias_grad.reshape(model)
    own = low_ref[pl.ds(pl.multiple_of(wide * slots, slots), slots), :]
    stores[1].start()
    slot_grad_ref[...] = row_dot(own, w_proj_ref[...])
    for store in stores:
        store.wait()


def gathered_blocks(block):
    pair = jnp.concatenate([block, exchange(block, "wide", 1)], axis=0)
    mine = [pair]
    for mask in range(2, lax.axis_size("wide"), 2):
        mine.append(exchange(pair, "wide", mask))
    return (*mine, *(exchange(blocks, "narrow", 1) for blocks in mine))


def contrast(place, block, w_proj, proj_bias):
    parts = gathered_blocks(block)
    part = block.shape[0]
    model = w_proj.shape[0]
    count = len(parts) * 2 * part
    low = jnp.bfloat16
    return pl.pallas_call(
        functools.partial(contrast_kernel, len(parts) // 2),
        out_shape=(
            jax.ShapeDtypeStruct((2 * part,), jnp.float32),
            main_shape(count, model, low),
            main_shape(count, model, low),
            jax.ShapeDtypeStruct((model,), jnp.float32),
            shape_of(2 * part, model, jnp.float32),
        ),
        in_specs=[SCALARS] + [VECTORS] * (len(parts) + 2),
        out_specs=(VECTORS, ANYWHERE, ANYWHERE, VECTORS, VECTORS),
        scratch_shapes=[
            pltpu.VMEM((count, model), low),
            pltpu.VMEM((count, model), low),
            pltpu.SemaphoreType.DMA((2,)),
            pltpu.VMEM((count, model), jnp.float32),
            pltpu.VMEM((count, model), low),
            pltpu.VMEM((count, 128), low),
            pltpu.VMEM((8, count), jnp.float32),
            pltpu.VMEM((count, 1), jnp.float32),
        ],
        compiler_params=pltpu.CompilerParams(vmem_limit_bytes=(12 if count <= 256 else 56) * MIB),
        cost_estimate=pl.CostEstimate(
            flops=2 * count * model * (model + 4 * count),
            bytes_accessed=4 * model * model,
            transcendentals=3 * count * count,
        ),
        name="contrast",
    )(in_main(place), *parts, w_proj, in_main(proj_bias))


def turn_kernel(
    flip,
    place_ref,
    lengths_ref,
    out_ref,
    slot_grad_ref,
    slope_ref,
    gain_ref,
    w_ffout_ref,
    w_in_ref,
    grad_ref,
    low_ref,
    pre_ref,
    part_ref,
    gain_grad_ref,
):
    half = (place_ref[0] % 2) ^ flip
    rows = out_ref.shape[0]
    chunk = rows // 2
    slots = lengths_ref.shape[0]
    starts, ends = slot_lines(lengths_ref, (slots, 1), 0)
    count = jnp.maximum(ends - starts, 1).astype(jnp.float32)
    high, rest = two_terms(slot_grad_ref[...] / count)
    starts, ends = slot_lines(lengths_ref, (1, slots), 1)
    total = jnp.zeros(gain_grad_ref.shape, jnp.float32)
    for step, own, _ in chunk_rows(rows, half):
        token = half * rows + step * chunk
        token = token + lax.broadcasted_iota(jnp.int32, (chunk, slots), 0)
        member = as_low((token >= starts) & (token < ends))
        final_grad = plain_dot(member, high) + plain_dot(member, rest)
        gain = gain_ref[...].reshape(1, -1)
        grad, gain_grad = norm_back(out_ref[own, :], gain, final_grad)
        total = total + gain_grad
        grad_ref[own, :] = grad
        low = grad.astype(jnp.bfloat16)
        low_ref[own, :] = low
        pre = row_dot(low, w_ffout_ref[...]) * slope_ref[own, :].astype(jnp.float32)
        pre = pre.astype(jnp.bfloat16)
        pre_ref[own, :] = pre
        part_ref[own, :] = row_dot(pre, w_in_ref[...]).astype(jnp.bfloat16)
    gain_grad_ref[...] = total


def turn(flip, place, lengths, layer_out, slot_grad, slope, gain, w_ffout, w_in):
    rows, hidden_count = slope.shape
    model = layer_out.shape[1]
    low = jnp.bfloat16
    inputs = [("scalar", lengths), ("near", layer_out), ("near", slot_grad), ("near", slope)]
    inputs += [("line", gain), ("near", w_ffout), ("near", w_in)]
    outputs = [
        ("near", shape_of(rows, model, jnp.float32)),
        ("near", shape_of(rows, model, low)),
        ("near", shape_of(rows, hidden_count, low)),
        ("near", shape_of(rows, model, low)),
        ("near", shape_of(1, model, jnp.float32)),
    ]
    flops = 4 * rows * model * hidden_count
    return row_call(turn_kernel, flip, inputs, outputs, [], place, {}, flops)


def join_kernel(
    flip,
    place_ref,
    out_grad_ref,
    after_ref,
    total_ref,
    gain_ref,
    w_out_ref,
    mid_ref,
    low_ref,
    mixed_grad_ref,
    gain_grad_ref,
):
    total = jnp.zeros(gain_grad_ref.shape, jnp.float32)
    gain = gain_ref[...].reshape(1, -1)
    for _, own, _ in chunk_rows(after_ref.shape[0], 0):
        back, gain_grad = norm_back(
            after_ref[own, :], gain, total_ref[own, :].astype(jnp.float32)
        )
        total = total + gain_grad
        mid = out_grad_ref[own, :] + back
        mid_ref[own, :] = mid
        low = mid.astype(jnp.bfloat16)
        low_ref[own, :] = low
        mixed_grad_ref[own, :] = row_dot(low, w_out_ref[...]).astype(jnp.bfloat16)
    gain_grad_ref[...] = total


def join(flip, place, out_grad, after, total, gain, w_out):
    rows, model = out_grad.shape
    inner = w_out.shape[0]
    low = jnp.bfloat16
    inputs = [("near", out_grad), ("near", after), ("near", total)]
    inputs += [("line", gain), ("near", w_out)]
    outputs = [
        ("near", shape_of(rows, model, jnp.float32)),
        ("near", shape_of(rows, model, low)),
        ("near", shape_of(rows, inner, low)),
        ("near", shape_of(1, model, jnp.float32)),
    ]
    flops = 2 * rows * model * inner
    return row_call(join_kernel, flip, inputs, outputs, [], place, {}, flops)


def last_kernel(flip, place_ref, mid_ref, hidden_ref, total_ref, gain_ref, *refs):
    out_hbm, token_ref, rows_s, sems = refs[-4:]
    half = (place_ref[0] % 2) ^ flip
    gain = gain_ref[...].reshape(1, -1)
    copies = []
    for step, own, whole in chunk_rows(mid_ref.shape[0], half):
        back, _ = norm_back(
            hidden_ref[whole, :].astype(jnp.float32), gain, total_ref[own, :].astype(jnp.float32)
        )
        rows_s[own, :] = mid_ref[own, :] + back
        copy = pltpu.make_async_copy(rows_s.at[own, :], out_hbm.at[whole, :], sems.at[step])
        copy.start()
        copies.append(copy)
    token_ref[...] = jnp.zeros(token_ref.shape, jnp.float32)
    for copy in copies:
        copy.wait()


def last(flip, place, mid, hidden_in, total, gain, given):
    rows, model = mid.shape
    inputs = [("near", mid), ("near", hidden_in), ("near", total), ("line", gain)]
    inputs.append(("any", given))
    aliases = {5: 0} if flip == 1 else {}
    outputs = [
        ("any", main_shape(2 * rows, model, jnp.float32)),
        ("near", shape_of(8, 128, jnp.float32)),
    ]
    scratch = [pltpu.VMEM((rows, model), jnp.float32), pltpu.SemaphoreType.DMA((2,))]
    return row_call(last_kernel, flip, inputs, outputs, scratch, place, aliases, 2**22)


def sum_kernel(count, *refs):
    refs[-1][...] = arrived_sum(refs[:count])


def summed(blocks, later):
    return pl.pallas_call(
        functools.partial(sum_kernel, len(blocks)),
        out_shape=jax.ShapeDtypeStruct(blocks[0].shape, jnp.float32),
        in_specs=[VECTORS] * len(blocks) + [ANYWHERE],
        out_specs=VECTORS,
        compiler_params=pltpu.CompilerParams(vmem_limit_bytes=12 * MIB),
        cost_estimate=QUICK,
        name="summed",
    )(*blocks, later)


def pair_grads_kernel(place_ref, *refs):
    lefts, rights = refs[0:2], refs[2:4]
    value = col_dot(lefts[0][...], rights[0][...]) + col_dot(lefts[1][...], rights[1][...])
    split_pairs(value, place_ref[1] % 2, refs[5], refs[6])


def split_pairs(value, parity, keep_ref, send_ref):
    pairs = keep_ref.shape[0]
    rows = value.shape[0] // (2 * pairs)
    for pair in range(pairs):
        first = value[2 * pair * rows : (2 * pair + 1) * rows].astype(jnp.bfloat16)
        second = value[(2 * pair + 1) * rows : (2 * pair + 2) * rows].astype(jnp.bfloat16)
        keep_ref[pair, :rows, :] = jnp.where(parity == 0, first, second)
        send_ref[pair, :rows, :] = jnp.where(parity == 0, second, first)


def pair_grads(place, lefts, rights, later, pairs):
    rows, model = lefts[0].shape
    width = rights[0].shape[1]
    piece = jax.ShapeDtypeStruct((pairs, model // (2 * pairs), width), jnp.bfloat16)
    return pl.pallas_call(
        pair_grads_kernel,
        out_shape=(piece, piece),
        in_specs=[SCALARS] + [VECTORS] * 4 + [ANYWHERE],
        out_specs=(VECTORS, VECTORS),
        compiler_params=pltpu.CompilerParams(vmem_limit_bytes=16 * MIB),
        cost_estimate=pl.CostEstimate(
            flops=4 * rows * model * width, bytes_accessed=5 * rows * model, transcendentals=0
        ),
        name="pair_grads",
    )(in_main(place), *lefts, *rights, later)


def add_kernel(left_ref, right_ref, *refs):
    refs[-1][...] = add_low(left_ref[...], right_ref[...])


def add_after(left, right, *later):
    return pl.pallas_call(
        add_kernel,
        out_shape=jax.ShapeDtypeStruct(left.shape, jnp.bfloat16),
        in_specs=[VECTORS, VECTORS] + [ANYWHERE] * len(later),
        out_specs=VECTORS,
        compiler_params=pltpu.CompilerParams(vmem_limit_bytes=12 * MIB),
        cost_estimate=pl.CostEstimate(
            flops=left.size, bytes_accessed=6 * left.size, transcendentals=0
        ),
        name="add_after",
    )(left, right, *later)


def copy_kernel(source_ref, later_ref, out_ref):
    out_ref[...] = source_ref[...]


def copied(value, later):
    return pl.pallas_call(
        copy_kernel,
        out_shape=jax.ShapeDtypeStruct(value.shape, value.dtype),
        in_specs=[VECTORS, ANYWHERE],
        out_specs=VECTORS,
        compiler_params=pltpu.CompilerParams(vmem_limit_bytes=12 * MIB),
        cost_estimate=QUICK,
        name="copied",
    )(value, later)


def halve_kernel(count, later_count, place_ref, *refs):
    own = place_ref[1] // 2
    outs = refs[2 * count + later_count :]
    width = refs[0].shape[2]
    for index, out in enumerate(outs):
        for part in range(count):
            out[:, part * width : (part + 1) * width] = add_low(
                refs[2 * part][own ^ index], refs[2 * part + 1][own ^ index]
            )


def halved(place, sides, *later):
    pairs, rows, width = sides[0].shape
    count = len(sides) // 2
    return pl.pallas_call(
        functools.partial(halve_kernel, count, len(later)),
        out_shape=(shape_of(rows, count * width, jnp.bfloat16),) * pairs,
        in_specs=[SCALARS] + [VECTORS] * len(sides) + [ANYWHERE] * len(later),
        out_specs=(VECTORS,) * pairs,
        compiler_params=pltpu.CompilerParams(vmem_limit_bytes=16 * MIB),
        cost_estimate=QUICK,
        name="halved",
    )(in_main(place), *sides, *later)


def fold_kernel(later_count, place_ref, keep_ref, came_ref, *refs):
    mine_ref, send_ref = refs[later_count:]
    own = place_ref[1] // 2
    half = mine_ref.shape[0]
    for index in range(half):
        near, far = own ^ index, own ^ (index + half)
        mine_ref[index] = add_low(keep_ref[near], came_ref[near])
        send_ref[index] = add_low(keep_ref[far], came_ref[far])


def folded(place, keep, came, *later):
    pairs, rows, width = keep.shape
    piece = jax.ShapeDtypeStruct((pairs // 2, rows, width), jnp.bfloat16)
    return pl.pallas_call(
        functools.partial(fold_kernel, len(later)),
        out_shape=(piece, piece),
        in_specs=[SCALARS, VECTORS, VECTORS] + [ANYWHERE] * len(later),
        out_specs=(VECTORS, VECTORS),
        compiler_params=pltpu.CompilerParams(vmem_limit_bytes=12 * MIB),
        cost_estimate=QUICK,
        name="folded",
    )(in_main(place), keep, came, *later)


def refold_kernel(later_count, mine_ref, came_ref, *refs):
    keep_ref, send_ref = refs[later_count:]
    half = keep_ref.shape[0]
    for index in range(half):
        keep_ref[index] = add_low(mine_ref[index], came_ref[index])
        send_ref[index] = add_low(mine_ref[index + half], came_ref[index + half])


def refolded(mine, came, *later):
    pairs, rows, width = mine.shape
    piece = jax.ShapeDtypeStruct((pairs // 2, rows, width), jnp.bfloat16)
    return pl.pallas_call(
        functools.partial(refold_kernel, len(later)),
        out_shape=(piece, piece),
        in_specs=[VECTORS, VECTORS] + [ANYWHERE] * len(later),
        out_specs=(VECTORS, VECTORS),
        compiler_params=pltpu.CompilerParams(vmem_limit_bytes=12 * MIB),
        cost_estimate=QUICK,
        name="refolded",
    )(mine, came, *later)


def arrived_sum(refs):
    total = refs[0][...].astype(jnp.float32)
    for ref in refs[1:]:
        total = total + ref[...].astype(jnp.float32)
    return total


def head_grads_kernel(
    place_ref,
    norm_ref,
    dq_ref,
    dk_ref,
    dv_ref,
    mid_own_ref,
    mid_far_ref,
    mixed_ref,
    one_ref,
    two_own_ref,
    two_far_ref,
    last_own_ref,
    last_far_ref,
    table_ref,
    later_ref,
    keep_ref,
    send_ref,
):
    half, model = mid_own_ref.shape
    side = place_ref[0] % 2
    own_rows = pl.ds(pl.multiple_of(side * half, half), half)
    far_rows = pl.ds(pl.multiple_of((1 - side) * half, half), half)
    norm = norm_ref[...]
    values = [col_dot(norm, ref[...]) for ref in (dq_ref, dk_ref, dv_ref)]
    last = col_dot(mid_own_ref[...], mixed_ref[own_rows, :])
    values.append(last + col_dot(mid_far_ref[...], mixed_ref[far_rows, :]))
    split_pairs(jnp.concatenate(values, axis=1), place_ref[1] % 2, keep_ref, send_ref)
    table = [table_ref[head : head + 1, :] for head in range(model // 128)]
    small = jnp.concatenate(
        [
            one_ref[...],
            two_own_ref[...] + two_far_ref[...],
            last_own_ref[...] + last_far_ref[...],
            jnp.concatenate(table, axis=1),
        ],
        axis=0,
    )
    high, rest = two_terms(small)
    small = jnp.concatenate([high, rest, jnp.zeros((8, model), jnp.bfloat16)], axis=0)
    rows = keep_ref.shape[1] - 16
    for pair in range(keep_ref.shape[0]):
        keep_ref[pair, rows:, :] = small
        send_ref[pair, rows:, :] = small


def head_grads(place, norm, grads, mid_own, mid_far, mixed, lines, table, later, pairs):
    model = norm.shape[1]
    piece = jax.ShapeDtypeStruct((pairs, model // (2 * pairs) + 16, model), jnp.bfloat16)
    return pl.pallas_call(
        head_grads_kernel,
        out_shape=(piece, piece),
        in_specs=[SCALARS] + [VECTORS] * 13 + [ANYWHERE],
        out_specs=(VECTORS, VECTORS),
        compiler_params=pltpu.CompilerParams(vmem_limit_bytes=24 * MIB),
        cost_estimate=QUICK,
        name="head_grads",
    )(in_main(place), norm, *grads, mid_own, mid_far, mixed, *lines, table, later)


def finish_kernel(count, *refs):
    dq_ref, dk_ref, dv_ref, out_ref, one_ref, two_ref, last_ref, rest_ref = refs[count + 1 :]
    total = arrived_sum(refs[:count])
    rows, inner = dq_ref.shape
    model = total.shape[1]
    dq_ref[...] = total[:rows, :inner]
    dk_ref[...] = total[:rows, inner : 2 * inner]
    dv_ref[...] = total[:rows, 2 * inner : 3 * inner]
    last = total[:rows, 3 * inner :]
    out_ref[...] = jnp.transpose(last) if out_ref.shape[0] == inner else last
    small = total[rows : rows + 4] + total[rows + 4 : rows + 8]
    one_ref[...] = small[0:1].reshape(model)
    two_ref[...] = small[1:2].reshape(model)
    last_ref[...] = small[2:3].reshape(model)
    lines = [small[3:4, index * 128 : (index + 1) * 128] for index in range(model // 128)]
    lines.append(jnp.zeros((8 - len(lines), 128), jnp.float32))
    rest_ref[...] = jnp.concatenate(lines, axis=0)


def finish(arrived, inner, later):
    rows, model = arrived[0].shape
    rows = rows - 16
    full = jnp.float32
    line = jax.ShapeDtypeStruct((model,), full)
    piece = shape_of(rows, inner, full)
    turned = rows % 8 == 0
    results = pl.pallas_call(
        functools.partial(finish_kernel, len(arrived)),
        out_shape=(
            piece,
            piece,
            piece,
            shape_of(inner, rows, full) if turned else piece,
            line,
            line,
            line,
            shape_of(8, 128, full),
        ),
        in_specs=[VECTORS] * len(arrived) + [ANYWHERE],
        out_specs=(VECTORS,) * 8,
        compiler_params=pltpu.CompilerParams(vmem_limit_bytes=12 * MIB),
        cost_estimate=pl.CostEstimate(
            flops=8 * rows * model, bytes_accessed=16 * rows * model, transcendentals=0
        ),
        name="finish",
    )(*arrived, later)
    grad_out = results[3] if turned else results[3].T
    return (*results[:3], grad_out, *results[4:])


def body(
    hidden_in,
    lengths,
    positive,
    norm1_gain,
    w_query,
    w_key,
    w_value,
    rel_bias,
    w_out,
    norm2_gain,
    w_in,
    w_ffout,
    final_gain,
    w_proj,
    proj_bias,
):
    bucket_count, head_count = rel_bias.shape
    pairs = lax.axis_size("wide") // 2
    wide = lax.axis_index("wide")
    place = jnp.stack([lax.axis_index("narrow"), wide]).astype(jnp.int32)
    table = rel_bias.T
    weights = (w_query.T, w_key.T, w_value.T)
    norm1, query, key, value, mixed, packed, spread = attend(
        lengths, table, hidden_in, norm1_gain, *weights
    )
    w_across = exchange(w_out, "narrow", 2)
    w_outs = (w_out, exchange(w_out, "narrow", 1), w_across, exchange(w_across, "narrow", 1))
    across = exchange(copied(packed, w_across), "narrow", 2)
    pieces = (packed, exchange(packed, "narrow", 1), across, exchange(across, "narrow", 1))
    far = middle(1, place, hidden_in, pieces, w_outs, norm2_gain, w_in, w_ffout)
    own = middle(0, place, hidden_in, pieces, w_outs, norm2_gain, w_in, w_ffout)
    after_far, norm2_far, act_far, slope_far, part_far = far
    after_own, norm2_own, act_own, slope_own, part_own = own
    total_own, total_far = summed_over_narrow(part_own, part_far)
    out_own, pooled_own = pool(0, place, lengths, after_own, total_own, final_gain, None)
    out_far, block = pool(
        1, place, lengths, after_far, total_far, final_gain, (positive, pooled_own)
    )
    loss, pooled_all, embed_low, bias_grad, slot_grad = contrast(place, block, w_proj, proj_bias)

    share = hidden_in.shape[1] // (2 * pairs)
    pooled_cols = lax.dynamic_slice_in_dim(pooled_all, wide * share, share, 1)
    grad_proj = dot_over(pooled_cols, embed_low, 0, 0)
    far = turn(1, place, lengths, out_far, slot_grad, slope_far, final_gain, w_ffout, w_in)
    own = turn(0, place, lengths, out_own, slot_grad, slope_own, final_gain, w_ffout, w_in)
    out_grad_far, out_low_far, pre_far, part_far, last_far = far
    out_grad_own, out_low_own, pre_own, part_own, last_own = own
    part = add_low(part_own, exchange(part_far, "narrow", 1))
    came = exchange(part, "narrow", 2)
    keep_a, send_a = pair_grads(place, (out_low_far, out_low_own), (act_far, act_own), part, pairs)
    came_a = exchange(send_a, "wide", 1)
    keep_b, send_b = pair_grads(
        place, (norm2_far, norm2_own), (pre_far, pre_own), send_a, pairs
    )
    came_b = exchange(send_b, "wide", 1)
    layer_out, token = assemble(place, out_own, out_far, send_b)
    total_own = add_after(part, came, came_a, grad_proj, token)
    total_far = exchange(total_own, "narrow", 1)
    mid_own, mid_low_own, mixed_grad_own, two_own = join(
        0, place, out_grad_own, after_own, total_own, norm2_gain, w_out
    )
    mid_far, mid_low_far, mixed_grad_far, two_far = join(
        1, place, out_grad_far, after_far, total_far, norm2_gain, w_out
    )
    a_mine, a_send = folded(place, keep_a, came_a, total_own)
    a_came = exchange(a_send, "wide", pairs)
    back = attend_back(
        place,
        lengths,
        table,
        query,
        key,
        value,
        (mixed_grad_own, mixed_grad_far),
        spread,
        hidden_in,
        weights,
        norm1,
        mixed,
        (),
    )
    dq, dk, dv, table_lines, hidden_near, weights_near, norm1_near, mixed_near = back
    grads = (dq, dk, dv)
    part_far, one_far = norm1_parts(
        1, place, grads, hidden_near, weights_near, (came_b, a_came)
    )
    far_came = exchange(part_far, "narrow", 1)
    part_own, one_own = norm1_parts(0, place, grads, hidden_near, weights_near, (part_far,))
    one = one_far + one_own
    one = one + exchange(one, "narrow", 1)
    one = one + exchange(one, "narrow", 2)
    part = add_after(part_own, far_came, one)
    came = exchange(part, "narrow", 2)
    head_keep, head_send = head_grads(
        place,
        norm1_near,
        grads,
        mid_low_own,
        mid_low_far,
        mixed_near,
        (one, two_own, two_far, last_own, last_far),
        table_lines,
        part,
        pairs,
    )
    head_came = exchange(head_send, "wide", 1)
    b_half = halved(place, (keep_b, came_b), head_send)
    b_arrived = over_parity(b_half)
    step = pairs
    while step > 2:
        a_mine, a_send = refolded(a_mine, a_came, b_half[0])
        step //= 2
        a_came = exchange(a_send, "wide", step)
    total_own = add_after(part, came, head_came, a_came, *b_arrived[1:])
    total_far = exchange(total_own, "narrow", 1)
    head_half = halved(place, (head_keep, head_came), total_own)
    head_arrived = over_parity(head_half)
    given, _ = last(0, place, mid_own, hidden_near, total_own, norm1_gain, total_own)
    grad_input, token = last(1, place, mid_far, hidden_near, total_far, norm1_gain, given)
    grad_ffout = summed((a_mine[0], a_came[0]), head_half[0]).T
    grad_in = summed(b_arrived, head_half[0])
    inner = query.shape[1]
    grad_query, grad_key, grad_value, grad_out, one, two, three, lines = finish(
        head_arrived, inner, token
    )
    return (
        layer_out,
        loss,
        grad_input,
        one,
        grad_query,
        grad_key,
        grad_value,
        lines[:head_count, :bucket_count].T,
        grad_out,
        two,
        grad_in,
        grad_ffout,
        three,
        grad_proj,
        bias_grad,
    )


def solution(mesh):
    in_specs = (
        P("wide", None),
        P("wide"),
        P("wide"),
        P(),
        P(None, "narrow"),
        P(None, "narrow"),
        P(None, "narrow"),
        P(None, "narrow"),
        P("narrow", None),
        P(),
        P(None, "narrow"),
        P("narrow", None),
        P(),
        P(),
        P(),
    )
    out_specs = (
        P("wide", None),
        P("wide"),
        P("wide", None),
        P(),
        P("wide", "narrow"),
        P("wide", "narrow"),
        P("wide", "narrow"),
        P(None, "narrow"),
        P("narrow", "wide"),
        P(),
        P("wide", "narrow"),
        P("narrow", "wide"),
        P(),
        P("wide", None),
        P(),
    )
    return jax.shard_map(body, mesh=mesh, in_specs=in_specs, out_specs=out_specs, check_vma=False)
```
